32 devices in a mesh: dp: 8 (over y, x, core), mp: 4 (over z).
Axes of the slice: x: 2, y: 2, z: 4, core: 2. Of those that a mesh axis runs over, the one named last changes fastest.
Arguments:
- clips: bfloat16 [1024, 768], P('dp', 'mp')
- captions: bfloat16 [1024, 768], P('dp', 'mp')
- video_id: int32 [1024], replicated, may hold values from 0 to 63, never falling along the last dimension, each value on 1 to 128 neighbouring positions
- logit_scale: float32 [], replicated, may hold values from 110 to 160
Outputs:
- d_clips: float32 [1024, 768], P(('dp', 'mp'))
- d_captions: float32 [1024, 768], P(('dp', 'mp'))
The draws below stay inside these ranges and needn't reach their ends.
Inputs may be any that keep to these rules, and one draw needn't show every extreme that they name: `video_id`: video ids never fall along the rows; each video covers 1 to 128 consecutive rows.
All inputs are finite; a program needn't handle non-finite values.
Results may differ from the reference program's by a relative error of at most 0.0095.
Values may be sent and summed in bfloat16 or wider, within the bound.
No kernel may reach another device: no remote copies, remote signals or barrier semaphores. Data moves between devices by JAX's collectives and lax.ppermute only.
A program may use at most 64 MiB of HBM per device.

```python
import math
import jax
import jax.numpy as jnp
import numpy as np
from jax import lax

D = 768
ROWS = 128
CLIPS = 1024
VIDEOS = 64


def paired_parts(key):
    shared = jax.random.normal(jax.random.fold_in(key, 101), (CLIPS, D), jnp.float32)
    clip_noise = jax.random.normal(jax.random.fold_in(key, 202), (CLIPS, D), jnp.float32)
    caption_noise = jax.random.normal(jax.random.fold_in(key, 303), (CLIPS, D), jnp.float32)
    aligned = jax.random.bernoulli(jax.random.fold_in(key, 505), 1.0 / 32.0, (CLIPS, 1))
    return (shared, clip_noise, caption_noise, aligned)


def mixed_rows(shared, noise, aligned):
    drawn = 0.42 * shared + noise
    close = shared + 0.05 * noise
    return jnp.where(aligned, close, drawn)


def draw_clips(key, part):
    shared, clip_noise, caption_noise, aligned = paired_parts(key)
    return mixed_rows(shared, clip_noise, aligned).astype(jnp.bfloat16)


def draw_captions(key, part):
    shared, clip_noise, caption_noise, aligned = paired_parts(key)
    return mixed_rows(shared, caption_noise, aligned).astype(jnp.bfloat16)


def split_up(count, total, reach, slope):
    loads = [(1 << 20) // math.isqrt(standing ** slope) + 1 for standing in range(2, count + 1)]
    spare, given = total - reach - (count - 1), [1] * (count - 1)
    while spare > 0:
        free = [i for i in range(count - 1) if given[i] < reach]
        whole, left = sum([loads[i] for i in free]), spare
        for i in free:
            extra = min(reach - given[i], max(1, left * loads[i] // whole), spare)
            given[i] = given[i] + extra
            spare = spare - extra
    return np.array([reach] + given)


def uneven(stream_key, count, total, most, lean):
    if count == 2:
        one = jax.random.randint(stream_key, (), max(1, total - most), min(most, total - 1) + 1)
        return jnp.stack([one, total - one])
    sizes = jnp.asarray(split_up(count, total, most, lean), jnp.int32)
    twos = (count - 1) // 2
    giver, sink = sizes[1:1 + 2 * twos:2], sizes[2:2 + 2 * twos:2]
    margin = jnp.minimum(giver - 1, most - sink)
    passed = jax.random.randint(jax.random.fold_in(stream_key, 1), (twos,), 0, 1 << 20) % (margin + 1)
    sizes = sizes.at[1:1 + 2 * twos:2].set(giver - passed).at[2:2 + 2 * twos:2].set(sink + passed)
    return sizes[jax.random.permutation(jax.random.fold_in(stream_key, 2), count)]


def setup_inputs(seed: int = 0) -> dict:
    splits = jax.random.split(jax.random.key(seed), 5)
    return {
        "clips": draw_clips(jax.random.fold_in(splits[4], 71), 0),
        "captions": draw_captions(jax.random.fold_in(splits[4], 71), 0),
        "video_id": jnp.searchsorted(jnp.cumsum(uneven(splits[2], VIDEOS, CLIPS, ROWS, 2)), jnp.arange(CLIPS), side="right").astype(jnp.int32),
        "logit_scale": jnp.clip(jnp.exp(jax.random.uniform(splits[3], (), jnp.float32, math.log(110.0), math.log(160.0))), 110.0, 160.0),
    }


epsilon = 1e-06
negative_fill = -1e+30

def unit_rows(values):
    widened = values.astype(jnp.float32)
    length = jnp.sqrt(lax.optimization_barrier(jnp.sum(widened * widened, axis=-1)) + epsilon)
    return (widened / length[:, None], length)

def reference(clips, captions, video_id, logit_scale):
    all_rows = clips.shape[0]
    clip_float, clip_length = unit_rows(clips)
    clip_unit = clip_float.astype(jnp.bfloat16)
    cap_float, cap_length = unit_rows(captions)
    cap_unit = cap_float.astype(jnp.bfloat16)
    pooled = jax.ops.segment_sum(clip_unit.astype(jnp.float32), video_id, num_segments=VIDEOS)[video_id]
    pool_length = jnp.sqrt(lax.optimization_barrier(jnp.sum(pooled * pooled, axis=-1)) + epsilon)
    pool_unit = pooled / pool_length[:, None]
    caption_pool = jax.ops.segment_sum(cap_unit.astype(jnp.float32), video_id, num_segments=VIDEOS)[video_id]
    positions = jnp.arange(all_rows, dtype=jnp.int32)
    block_count = all_rows // ROWS

    def block_scores(query_units, other_units, block_index):
        first_row = (block_index * ROWS).astype(jnp.int32)
        query_rows = lax.dynamic_slice_in_dim(query_units, first_row, ROWS, 0)
        row_videos = lax.dynamic_slice_in_dim(video_id, first_row, ROWS, 0)
        row_positions = first_row + jnp.arange(ROWS, dtype=jnp.int32)
        scores = logit_scale * jnp.dot(query_rows, other_units.T, preferred_element_type=jnp.float32)
        allowed = (row_videos[:, None] != video_id[None, :]) | (row_positions[:, None] == positions[None, :])
        return (scores, allowed, query_rows, first_row)

    def log_totals(query_units, other_units):

        def one_block(block_index):
            scores, allowed, query_rows, first_row = block_scores(query_units, other_units, block_index)
            top_score = lax.optimization_barrier(jnp.max(jnp.where(allowed, scores, negative_fill), axis=1))
            totals = lax.optimization_barrier(jnp.sum(jnp.where(allowed, jnp.exp(scores - top_score[:, None]), 0.0), axis=1))
            return top_score + jnp.log(totals)
        return lax.map(one_block, jnp.arange(block_count, dtype=jnp.int32)).reshape(all_rows)
    row_lse = log_totals(clip_unit, cap_unit)
    col_lse = log_totals(cap_unit, clip_unit)

    def backward_block(cap_acc, block_index):
        scores, allowed, query_rows, first_row = block_scores(clip_unit, cap_unit, block_index)
        row_part = lax.dynamic_slice_in_dim(row_lse, first_row, ROWS, 0)
        weights = 0.5 * (jnp.exp(scores - row_part[:, None]) + jnp.exp(scores - col_lse[None, :]))
        weights = jnp.where(allowed, weights, 0.0).astype(jnp.bfloat16)
        clip_part = jnp.dot(weights, cap_unit, preferred_element_type=jnp.float32)
        cap_acc = cap_acc + jnp.dot(weights.T, query_rows, preferred_element_type=jnp.float32)
        return (cap_acc, clip_part)
    cap_acc, clip_parts = lax.scan(backward_block, jnp.zeros((all_rows, clips.shape[1]), jnp.float32), jnp.arange(block_count, dtype=jnp.int32))
    clip_acc = clip_parts.reshape(all_rows, clips.shape[1])
    projected = caption_pool - pool_unit * lax.optimization_barrier(jnp.sum(pool_unit * caption_pool, axis=-1, keepdims=True))
    clip_grad_unit = logit_scale * clip_acc - 0.5 * logit_scale * cap_unit.astype(jnp.float32) - 0.5 * logit_scale * projected / pool_length[:, None]
    cap_grad_unit = logit_scale * cap_acc - 0.5 * logit_scale * clip_unit.astype(jnp.float32) - 0.5 * logit_scale * pool_unit
    d_clips = (clip_grad_unit - clip_float * lax.optimization_barrier(jnp.sum(clip_float * clip_grad_unit, axis=-1, keepdims=True))) / clip_length[:, None]
    d_captions = (cap_grad_unit - cap_float * lax.optimization_barrier(jnp.sum(cap_float * cap_grad_unit, axis=-1, keepdims=True))) / cap_length[:, None]
    return (d_clips, d_captions)
```

```python
import functools
import math

import jax
import jax.numpy as jnp
from jax import lax
from jax.experimental import pallas as pl
from jax.experimental.pallas import tpu as pltpu
from jax.sharding import PartitionSpec as P

epsilon = 1e-06
negative_fill = -1e30
log2_e = math.log2(math.e)


def unit_rows(values):
    widened = values.astype(jnp.float32)
    length = jnp.sqrt(jnp.sum(widened * widened, axis=-1, keepdims=True) + epsilon)
    return widened / length, length


def gather_columns(block):
    count = lax.axis_size("mp")
    chunks = [block]
    for k in range(1, count):
        chunks.append(lax.ppermute(block, "mp", [(i, i ^ k) for i in range(count)]))
    return jnp.concatenate(chunks, axis=-1)


def gather_orders(dp_count):
    bits = [1 << k for k in range(1, dp_count.bit_length() - 1)]
    return bits, bits[1:] + bits[:1]


def gather_blocks(block):
    dp_count = lax.axis_size("dp")
    even, odd = gather_orders(dp_count)
    held = block[None]
    for bit_even, bit_odd in zip(even, odd):
        route = [(i, i ^ (bit_odd if i & 1 else bit_even)) for i in range(dp_count)]
        held = jnp.concatenate([held, lax.ppermute(held, "dp", route)], axis=0)
    other = lax.ppermute(held, "dp", [(i, i ^ 1) for i in range(dp_count)])
    return jnp.concatenate([held, other], axis=0)


def block_offsets(dp_count):
    even, odd = gather_orders(dp_count)
    own = []
    for order in (even, odd):
        held = [0]
        for bit in order:
            held = held + [h ^ bit for h in held]
        own.append(held)
    return [own[0] + [h ^ 1 for h in own[1]], own[1] + [h ^ 1 for h in own[0]]]


def kernel(
    mp_ref,
    scale_ref,
    clips_ref,
    caps_ref,
    own_clips_ref,
    own_caps_ref,
    row_videos_ref,
    column_videos_ref,
    d_clips_ref,
    d_caps_ref,
    row_lse_ref,
    col_max_ref,
    col_sum_ref,
    *,
    mp_count,
):
    total = clips_ref.shape[0]
    own = own_clips_ref.shape[0]
    width = clips_ref.shape[1]
    row_tile = min(256, total)
    col_tile = min(1024, total)
    mp_index = mp_ref[0]
    scale = scale_ref[0]
    scale2 = scale * log2_e
    contract_last = (((1,), (1,)), ((), ()))

    col_max_ref[...] = jnp.full(col_max_ref.shape, negative_fill, jnp.float32)
    col_sum_ref[...] = jnp.zeros(col_sum_ref.shape, jnp.float32)

    def one_tile(row_first, col_first, carry):
        row_max, row_sum = carry
        rows = pl.ds(row_first, row_tile)
        cols = pl.ds(col_first, col_tile)
        scores = scale2 * lax.dot_general(
            clips_ref[rows, :], caps_ref[cols, :], contract_last, preferred_element_type=jnp.float32
        )
        same = column_videos_ref[rows, :] == row_videos_ref[:, cols]
        distance = lax.broadcasted_iota(jnp.int32, scores.shape, 0) - lax.broadcasted_iota(
            jnp.int32, scores.shape, 1
        )
        off_diagonal = distance != col_first - row_first
        scores = jnp.where(same & off_diagonal, negative_fill, scores)
        new_row = jnp.maximum(row_max, jnp.max(scores, axis=1, keepdims=True))
        row_sum = row_sum * jnp.exp2(row_max - new_row) + jnp.sum(
            jnp.exp2(scores - new_row), axis=1, keepdims=True
        )
        old_col = col_max_ref[:, cols]
        new_col = jnp.maximum(old_col, jnp.max(scores, axis=0, keepdims=True))
        col_sum_ref[:, cols] = col_sum_ref[:, cols] * jnp.exp2(old_col - new_col) + jnp.sum(
            jnp.exp2(scores - new_col), axis=0, keepdims=True
        )
        col_max_ref[:, cols] = new_col
        return new_row, row_sum

    def one_row_block(block):
        row_first = block * row_tile
        if not isinstance(block, int):
            row_first = pl.multiple_of(row_first, row_tile)
        carry = (
            jnp.full((row_tile, 1), negative_fill, jnp.float32),
            jnp.zeros((row_tile, 1), jnp.float32),
        )
        if total == col_tile:
            row_max, row_sum = one_tile(row_first, 0, carry)
        else:
            row_max, row_sum = lax.fori_loop(
                0,
                total // col_tile,
                lambda c, so_far: one_tile(row_first, pl.multiple_of(c * col_tile, col_tile), so_far),
                carry,
            )
        lse = row_max + jnp.log2(row_sum)
        row_lse_ref[:, pl.ds(row_first, row_tile)] = jnp.transpose(
            jnp.broadcast_to(lse, (row_tile, 128))
        )[:8, :]

    if total // row_tile <= 8:
        for block in range(total // row_tile):
            one_row_block(block)
    else:
        pl.loop(0, total // row_tile)(one_row_block)

    col_lse = col_max_ref[...] + jnp.log2(col_sum_ref[...])
    row_lse = row_lse_ref[0:1, :]

    own_first = pl.multiple_of(mp_index * own, own)
    own_rows = pl.ds(own_first, own)
    clip_unit = clips_ref[own_rows, :]
    cap_unit = caps_ref[own_rows, :]
    same = column_videos_ref[own_rows, :] == row_videos_ref[...]
    distance = lax.broadcasted_iota(jnp.int32, (own, total), 1) - lax.broadcasted_iota(
        jnp.int32, (own, total), 0
    )
    blocked = same & (distance != own_first)
    same = same.astype(jnp.bfloat16)

    def strip(unit, others_ref, own_lse_all, other_lse):
        scores = scale2 * lax.dot_general(
            unit, others_ref[...], contract_last, preferred_element_type=jnp.float32
        )
        scores = jnp.where(blocked, negative_fill, scores)
        top = jnp.max(scores, axis=1, keepdims=True)
        own_lse = top + jnp.log2(jnp.sum(jnp.exp2(scores - top), axis=1, keepdims=True))
        weights = 0.5 * (jnp.exp2(scores - own_lse) + jnp.exp2(scores - other_lse))
        weights = weights.astype(jnp.bfloat16)
        both = jnp.concatenate([weights, same], axis=0)
        sums = jnp.dot(both, others_ref[...], preferred_element_type=jnp.float32)
        return sums[:own], sums[own:]

    clip_acc, caption_pool = strip(clip_unit, caps_ref, None, col_lse)
    cap_acc, pooled = strip(cap_unit, clips_ref, None, row_lse)
    clip_unit = clip_unit.astype(jnp.float32)
    cap_unit = cap_unit.astype(jnp.float32)
    pool_length = jnp.sqrt(jnp.sum(pooled * pooled, axis=1, keepdims=True) + epsilon)
    pool_unit = pooled / pool_length
    projected = caption_pool - pool_unit * jnp.sum(pool_unit * caption_pool, axis=1, keepdims=True)
    clip_grad = scale * clip_acc - 0.5 * scale * cap_unit - 0.5 * scale * projected / pool_length
    cap_grad = scale * cap_acc - 0.5 * scale * clip_unit - 0.5 * scale * pool_unit

    def finish(values_ref, grad, out_ref):
        unit, length = unit_rows(values_ref[...])
        result = (grad - unit * jnp.sum(unit * grad, axis=1, keepdims=True)) / length
        chunk = width // mp_count
        for index in range(mp_count):

            @pl.when(mp_index == index)
            def _():
                out_ref[...] = jnp.concatenate(
                    [result[:, (q ^ index) * chunk : ((q ^ index) + 1) * chunk] for q in range(mp_count)],
                    axis=1,
                )

    finish(own_clips_ref, clip_grad, d_clips_ref)
    finish(own_caps_ref, cap_grad, d_caps_ref)


def body(clips, captions, video_id, logit_scale):
    dp_count = lax.axis_size("dp")
    mp_count = lax.axis_size("mp")
    row_count = clips.shape[0]
    own = row_count // mp_count
    width = clips.shape[1] * mp_count
    total = row_count * dp_count
    dp_index = lax.axis_index("dp")
    mp_index = lax.axis_index("mp")

    full = gather_columns(jnp.stack([clips, captions]))
    unit = unit_rows(full)[0].astype(jnp.bfloat16)
    own_raw = lax.dynamic_slice_in_dim(full, mp_index * own, own, 1)
    every = gather_blocks(unit)
    all_clips = every[:, 0].reshape(total, width)
    all_caps = every[:, 1].reshape(total, width)

    offsets = block_offsets(dp_count)
    videos = []
    for even, odd in zip(*offsets):
        block = dp_index ^ jnp.where(dp_index & 1, odd, even)
        videos.append(lax.dynamic_slice_in_dim(video_id, block * row_count, row_count, 0))
    videos = jnp.concatenate(videos)

    vmem = pl.BlockSpec(memory_space=pltpu.VMEM)
    smem = pl.BlockSpec(memory_space=pltpu.SMEM)
    out = jax.ShapeDtypeStruct((own, width), jnp.float32)
    return pl.pallas_call(
        functools.partial(kernel, mp_count=mp_count),
        out_shape=(out, out),
        in_specs=[smem, smem] + [vmem] * 6,
        out_specs=(vmem, vmem),
        scratch_shapes=[
            pltpu.VMEM((8, total), jnp.float32),
            pltpu.VMEM((1, total), jnp.float32),
            pltpu.VMEM((1, total), jnp.float32),
        ],
        compiler_params=pltpu.CompilerParams(vmem_limit_bytes=48 * 1024 * 1024),
    )(
        jnp.reshape(mp_index, (1,)).astype(jnp.int32),
        jnp.reshape(logit_scale, (1,)),
        all_clips,
        all_caps,
        own_raw[0],
        own_raw[1],
        videos[None, :],
        videos[:, None],
    )


def solution(mesh):
    in_specs = (P("dp", "mp"), P("dp", "mp"), P(), P())
    out_specs = (P(("dp", "mp"), None), P(("dp", "mp"), None))
    return jax.shard_map(body, mesh=mesh, in_specs=in_specs, out_specs=out_specs, check_vma=False)
```

```python
import functools
import math

import jax
import jax.numpy as jnp
from jax import lax
from jax.experimental import pallas as pl
from jax.experimental.pallas import tpu as pltpu
from jax.sharding import PartitionSpec as P

epsilon = 1e-06
negative_fill = -1e30
log2_e = math.log2(math.e)
resident_limit = 8 * 1024 * 1024


def unit_rows(values):
    widened = values.astype(jnp.float32)
    length = jnp.sqrt(jnp.sum(widened * widened, axis=-1, keepdims=True) + epsilon)
    return widened / length, length


def gather_columns(block):
    count = lax.axis_size("mp")
    chunks = [block]
    for k in range(1, count):
        chunks.append(lax.ppermute(block, "mp", [(i, i ^ k) for i in range(count)]))
    return jnp.concatenate(chunks, axis=-1)


def gather_orders(dp_count):
    bits = [1 << k for k in range(1, dp_count.bit_length() - 1)]
    return bits, bits[1:] + bits[:1]


def gather_blocks(block):
    dp_count = lax.axis_size("dp")
    even, odd = gather_orders(dp_count)
    held = block[None]
    for bit_even, bit_odd in zip(even, odd):
        route = [(i, i ^ (bit_odd if i & 1 else bit_even)) for i in range(dp_count)]
        held = jnp.concatenate([held, lax.ppermute(held, "dp", route)], axis=0)
    other = lax.ppermute(held, "dp", [(i, i ^ 1) for i in range(dp_count)])
    return jnp.concatenate([held, other], axis=0)


def block_offsets(dp_count):
    even, odd = gather_orders(dp_count)
    own = []
    for order in (even, odd):
        held = [0]
        for bit in order:
            held = held + [h ^ bit for h in held]
        own.append(held)
    return [own[0] + [h ^ 1 for h in own[1]], own[1] + [h ^ 1 for h in own[0]]]


def streamed_kernel(
    mp_ref,
    scale_ref,
    clips_ref,
    caps_ref,
    own_clips_ref,
    own_caps_ref,
    row_videos_ref,
    column_videos_ref,
    d_clips_ref,
    d_caps_ref,
    row_lse_ref,
    col_max_ref,
    col_sum_ref,
    *,
    mp_count,
):
    total = clips_ref.shape[0]
    own = own_clips_ref.shape[0]
    width = clips_ref.shape[1]
    row_tile = min(256, total)
    col_tile = min(1024, total)
    mp_index = mp_ref[0]
    scale = scale_ref[0]
    scale2 = scale * log2_e
    contract_last = (((1,), (1,)), ((), ()))

    col_max_ref[...] = jnp.full(col_max_ref.shape, negative_fill, jnp.float32)
    col_sum_ref[...] = jnp.zeros(col_sum_ref.shape, jnp.float32)

    def one_tile(row_first, col_first, carry):
        row_max, row_sum = carry
        rows = pl.ds(row_first, row_tile)
        cols = pl.ds(col_first, col_tile)
        scores = scale2 * lax.dot_general(
            clips_ref[rows, :], caps_ref[cols, :], contract_last, preferred_element_type=jnp.float32
        )
        same = column_videos_ref[rows, :] == row_videos_ref[:, cols]
        distance = lax.broadcasted_iota(jnp.int32, scores.shape, 0) - lax.broadcasted_iota(
            jnp.int32, scores.shape, 1
        )
        off_diagonal = distance != col_first - row_first
        scores = jnp.where(same & off_diagonal, negative_fill, scores)
        new_row = jnp.maximum(row_max, jnp.max(scores, axis=1, keepdims=True))
        row_sum = row_sum * jnp.exp2(row_max - new_row) + jnp.sum(
            jnp.exp2(scores - new_row), axis=1, keepdims=True
        )
        old_col = col_max_ref[:, cols]
        new_col = jnp.maximum(old_col, jnp.max(scores, axis=0, keepdims=True))
        col_sum_ref[:, cols] = col_sum_ref[:, cols] * jnp.exp2(old_col - new_col) + jnp.sum(
            jnp.exp2(scores - new_col), axis=0, keepdims=True
        )
        col_max_ref[:, cols] = new_col
        return new_row, row_sum

    def one_row_block(block):
        row_first = block * row_tile
        if not isinstance(block, int):
            row_first = pl.multiple_of(row_first, row_tile)
        carry = (
            jnp.full((row_tile, 1), negative_fill, jnp.float32),
            jnp.zeros((row_tile, 1), jnp.float32),
        )
        if total == col_tile:
            row_max, row_sum = one_tile(row_first, 0, carry)
        else:
            row_max, row_sum = lax.fori_loop(
                0,
                total // col_tile,
                lambda c, so_far: one_tile(row_first, pl.multiple_of(c * col_tile, col_tile), so_far),
                carry,
            )
        lse = row_max + jnp.log2(row_sum)
        row_lse_ref[:, pl.ds(row_first, row_tile)] = jnp.transpose(
            jnp.broadcast_to(lse, (row_tile, 128))
        )[:8, :]

    if total // row_tile <= 8:
        for block in range(total // row_tile):
            one_row_block(block)
    else:
        pl.loop(0, total // row_tile)(one_row_block)

    col_lse = col_max_ref[...] + jnp.log2(col_sum_ref[...])
    row_lse = row_lse_ref[0:1, :]

    own_first = pl.multiple_of(mp_index * own, own)
    own_rows = pl.ds(own_first, own)
    clip_unit = clips_ref[own_rows, :]
    cap_unit = caps_ref[own_rows, :]
    same = column_videos_ref[own_rows, :] == row_videos_ref[...]
    distance = lax.broadcasted_iota(jnp.int32, (own, total), 1) - lax.broadcasted_iota(
        jnp.int32, (own, total), 0
    )
    blocked = same & (distance != own_first)
    same = same.astype(jnp.bfloat16)

    def strip(unit, others_ref, own_lse_all, other_lse):
        scores = scale2 * lax.dot_general(
            unit, others_ref[...], contract_last, preferred_element_type=jnp.float32
        )
        scores = jnp.where(blocked, negative_fill, scores)
        top = jnp.max(scores, axis=1, keepdims=True)
        own_lse = top + jnp.log2(jnp.sum(jnp.exp2(scores - top), axis=1, keepdims=True))
        weights = 0.5 * (jnp.exp2(scores - own_lse) + jnp.exp2(scores - other_lse))
        weights = weights.astype(jnp.bfloat16)
        both = jnp.concatenate([weights, same], axis=0)
        sums = jnp.dot(both, others_ref[...], preferred_element_type=jnp.float32)
        return sums[:own], sums[own:]

    clip_acc, caption_pool = strip(clip_unit, caps_ref, None, col_lse)
    cap_acc, pooled = strip(cap_unit, clips_ref, None, row_lse)
    clip_unit = clip_unit.astype(jnp.float32)
    cap_unit = cap_unit.astype(jnp.float32)
    pool_length = jnp.sqrt(jnp.sum(pooled * pooled, axis=1, keepdims=True) + epsilon)
    pool_unit = pooled / pool_length
    projected = caption_pool - pool_unit * jnp.sum(pool_unit * caption_pool, axis=1, keepdims=True)
    clip_grad = scale * clip_acc - 0.5 * scale * cap_unit - 0.5 * scale * projected / pool_length
    cap_grad = scale * cap_acc - 0.5 * scale * clip_unit - 0.5 * scale * pool_unit

    def finish(values_ref, grad, out_ref):
        unit, length = unit_rows(values_ref[...])
        result = (grad - unit * jnp.sum(unit * grad, axis=1, keepdims=True)) / length
        chunk = width // mp_count
        for index in range(mp_count):

            @pl.when(mp_index == index)
            def _():
                out_ref[...] = jnp.concatenate(
                    [result[:, (q ^ index) * chunk : ((q ^ index) + 1) * chunk] for q in range(mp_count)],
                    axis=1,
                )

    finish(own_clips_ref, clip_grad, d_clips_ref)
    finish(own_caps_ref, cap_grad, d_caps_ref)


def streamed_body(clips, captions, video_id, logit_scale):
    dp_count = lax.axis_size("dp")
    mp_count = lax.axis_size("mp")
    row_count = clips.shape[0]
    own = row_count // mp_count
    width = clips.shape[1] * mp_count
    total = row_count * dp_count
    dp_index = lax.axis_index("dp")
    mp_index = lax.axis_index("mp")

    full = gather_columns(jnp.stack([clips, captions]))
    unit = unit_rows(full)[0].astype(jnp.bfloat16)
    own_raw = lax.dynamic_slice_in_dim(full, mp_index * own, own, 1)
    every = gather_blocks(unit)
    all_clips = every[:, 0].reshape(total, width)
    all_caps = every[:, 1].reshape(total, width)

    offsets = block_offsets(dp_count)
    videos = []
    for even, odd in zip(*offsets):
        block = dp_index ^ jnp.where(dp_index & 1, odd, even)
        videos.append(lax.dynamic_slice_in_dim(video_id, block * row_count, row_count, 0))
    videos = jnp.concatenate(videos)

    vmem = pl.BlockSpec(memory_space=pltpu.VMEM)
    smem = pl.BlockSpec(memory_space=pltpu.SMEM)
    out = jax.ShapeDtypeStruct((own, width), jnp.float32)
    return pl.pallas_call(
        functools.partial(streamed_kernel, mp_count=mp_count),
        out_shape=(out, out),
        in_specs=[smem, smem] + [vmem] * 6,
        out_specs=(vmem, vmem),
        scratch_shapes=[
            pltpu.VMEM((8, total), jnp.float32),
            pltpu.VMEM((1, total), jnp.float32),
            pltpu.VMEM((1, total), jnp.float32),
        ],
        compiler_params=pltpu.CompilerParams(vmem_limit_bytes=48 * 1024 * 1024),
    )(
        jnp.reshape(mp_index, (1,)).astype(jnp.int32),
        jnp.reshape(logit_scale, (1,)),
        all_clips,
        all_caps,
        own_raw[0],
        own_raw[1],
        videos[None, :],
        videos[:, None],
    )


def resident_kernel(
    mp_ref,
    scale_ref,
    *refs,
    piece_counts,
    places,
    mp_count,
):
    lead_refs = refs[: piece_counts[0]]
    rest_refs = refs[piece_counts[0] : sum(piece_counts)]
    refs = refs[sum(piece_counts) :]
    row_videos_ref, column_videos_ref, d_clips_ref, d_caps_ref = refs[:4]
    clips_ref, caps_ref, own_ref, row_lse_ref = refs[4:]
    total, width = clips_ref.shape
    rows = own_ref.shape[1]
    own = d_clips_ref.shape[0]
    mp_index = mp_ref[0]
    scale = scale_ref[0]
    scale2 = scale * log2_e

    for position, (lead_place, rest_place) in enumerate(places):
        span = pl.ds(position * rows, rows)
        for kind in range(2):
            lead_ref, lead_at = lead_refs[lead_place[0]], lead_place[1]
            rest_ref, rest_at = rest_refs[rest_place[0]], rest_place[1]
            chunk = width // mp_count
            raw = jnp.concatenate(
                [
                    lead_ref[kind, lead_at * chunk : (lead_at + 1) * chunk, :],
                    rest_ref[kind, rest_at * (width - chunk) : (rest_at + 1) * (width - chunk), :],
                ],
                axis=0,
            )
            if position == 0:
                own_ref[kind] = jnp.transpose(raw)
            wide = raw.astype(jnp.float32)
            inverse = 1.0 / jnp.sqrt(jnp.sum(wide * wide, axis=0, keepdims=True) + epsilon)
            unit = (wide * inverse).astype(jnp.bfloat16)
            if kind == 0:
                clips_ref[span, :] = jnp.transpose(unit)
            else:
                caps_ref[:, span] = unit

    row_tile = min(256, total)
    col_max = jnp.full((1, total), negative_fill, jnp.float32)
    col_sum = jnp.zeros((1, total), jnp.float32)
    for row_first in range(0, total, row_tile):
        span = pl.ds(row_first, row_tile)
        scores = scale2 * jnp.dot(clips_ref[span, :], caps_ref[...], preferred_element_type=jnp.float32)
        same = column_videos_ref[span, :] == row_videos_ref[...]
        distance = lax.broadcasted_iota(jnp.int32, scores.shape, 1) - lax.broadcasted_iota(
            jnp.int32, scores.shape, 0
        )
        scores = jnp.where(same & (distance != row_first), negative_fill, scores)
        row_max = jnp.max(scores, axis=1, keepdims=True)
        row_sum = jnp.sum(jnp.exp2(scores - row_max), axis=1, keepdims=True)
        new_col = jnp.maximum(col_max, jnp.max(scores, axis=0, keepdims=True))
        col_sum = col_sum * jnp.exp2(col_max - new_col) + jnp.sum(
            jnp.exp2(scores - new_col), axis=0, keepdims=True
        )
        col_max = new_col
        row_lse_ref[:, span] = jnp.transpose(
            jnp.broadcast_to(row_max + jnp.log2(row_sum), (row_tile, 128))
        )[:8, :]
    col_lse = col_max + jnp.log2(col_sum)
    row_lse = row_lse_ref[0:1, :]

    own_first = pl.multiple_of(mp_index * own, own)
    own_rows = pl.ds(own_first, own)
    clip_float, clip_length = unit_rows(own_ref[0, own_rows, :])
    cap_float, cap_length = unit_rows(own_ref[1, own_rows, :])
    clip_unit = clips_ref[own_rows, :]
    cap_unit = cap_float.astype(jnp.bfloat16)
    same = column_videos_ref[own_rows, :] == row_videos_ref[...]
    distance = lax.broadcasted_iota(jnp.int32, (own, total), 1) - lax.broadcasted_iota(
        jnp.int32, (own, total), 0
    )
    blocked = same & (distance != own_first)
    same = same.astype(jnp.bfloat16)
    last = (((1,), (1,)), ((), ()))

    def strip(products, other_lse):
        scores = jnp.where(blocked, negative_fill, scale2 * products)
        top = jnp.max(scores, axis=1, keepdims=True)
        own_lse = top + jnp.log2(jnp.sum(jnp.exp2(scores - top), axis=1, keepdims=True))
        weights = 0.5 * (jnp.exp2(scores - own_lse) + jnp.exp2(scores - other_lse))
        return jnp.concatenate([weights.astype(jnp.bfloat16), same], axis=0)

    clip_products = jnp.dot(clip_unit, caps_ref[...], preferred_element_type=jnp.float32)
    cap_products = lax.dot_general(cap_unit, clips_ref[...], last, preferred_element_type=jnp.float32)
    clip_sums = lax.dot_general(
        strip(clip_products, col_lse), caps_ref[...], last, preferred_element_type=jnp.float32
    )
    cap_sums = jnp.dot(strip(cap_products, row_lse), clips_ref[...], preferred_element_type=jnp.float32)
    clip_acc, caption_pool = clip_sums[:own], clip_sums[own:]
    cap_acc, pooled = cap_sums[:own], cap_sums[own:]
    pool_length = jnp.sqrt(jnp.sum(pooled * pooled, axis=1, keepdims=True) + epsilon)
    pool_unit = pooled / pool_length
    projected = caption_pool - pool_unit * jnp.sum(pool_unit * caption_pool, axis=1, keepdims=True)
    clip_grad = (
        scale * clip_acc
        - 0.5 * scale * cap_unit.astype(jnp.float32)
        - 0.5 * scale * projected / pool_length
    )
    cap_grad = scale * cap_acc - 0.5 * scale * clip_unit.astype(jnp.float32) - 0.5 * scale * pool_unit

    def finish(unit, length, grad, out_ref):
        result = (grad - unit * jnp.sum(unit * grad, axis=1, keepdims=True)) / length
        chunk = width // mp_count
        for index in range(mp_count):

            @pl.when(mp_index == index)
            def _():
                out_ref[...] = jnp.concatenate(
                    [result[:, (q ^ index) * chunk : ((q ^ index) + 1) * chunk] for q in range(mp_count)],
                    axis=1,
                )

    finish(clip_float, clip_length, clip_grad, d_clips_ref)
    finish(cap_float, cap_length, cap_grad, d_caps_ref)


def resident_body(clips, captions, video_id, logit_scale):
    dp_count = lax.axis_size("dp")
    mp_count = lax.axis_size("mp")
    row_count = clips.shape[0]
    own = row_count // mp_count
    width = clips.shape[1] * mp_count
    total = row_count * dp_count
    dp_index = lax.axis_index("dp")
    mp_index = lax.axis_index("mp")
    even, odd = gather_orders(dp_count)

    def along(step, block):
        route = [(i, i ^ (odd[step] if i & 1 else even[step])) for i in range(dp_count)]
        return lax.ppermute(block, "dp", route)

    def across(block):
        return lax.ppermute(block, "dp", [(i, i ^ 1) for i in range(dp_count)])

    lead = jnp.stack([clips.T, captions.T])
    lead_first = along(0, lead)
    arrived = [
        lax.ppermute(lead, "mp", [(i, i ^ k) for i in range(mp_count)]) for k in range(1, mp_count)
    ]
    lead_second = along(1, jnp.concatenate([lead, lead_first], axis=1))
    rest = jnp.concatenate(arrived, axis=1)
    rest, lead_second = lax.optimization_barrier((rest, lead_second))
    rest_first = along(0, rest)
    rest_second = along(1, rest)
    rest_third = along(1, rest_first)
    lead_other = across(jnp.concatenate([lead, lead_first, lead_second], axis=1))
    rest_held = [rest, rest_first, rest_second, rest_third]
    leads = [lead, lead_first, lead_second, lead_other]
    rests = rest_held + [across(piece) for piece in rest_held]
    places = [((0, 0), (0, 0)), ((1, 0), (1, 0)), ((2, 0), (2, 0)), ((2, 1), (3, 0))]
    places += [((3, p), (4 + p, 0)) for p in range(4)]

    offsets = [[0, even[0], even[1], even[0] ^ even[1]], [0, odd[0], odd[1], odd[0] ^ odd[1]]]
    offsets = [
        offsets[0] + [o ^ 1 for o in offsets[1]],
        offsets[1] + [o ^ 1 for o in offsets[0]],
    ]
    videos = []
    for even_offset, odd_offset in zip(*offsets):
        block = dp_index ^ jnp.where(dp_index & 1, odd_offset, even_offset)
        videos.append(lax.dynamic_slice_in_dim(video_id, block * row_count, row_count, 0))
    videos = jnp.concatenate(videos)

    vmem = pl.BlockSpec(memory_space=pltpu.VMEM)
    smem = pl.BlockSpec(memory_space=pltpu.SMEM)
    out = jax.ShapeDtypeStruct((own, width), jnp.float32)
    return pl.pallas_call(
        functools.partial(
            resident_kernel,
            piece_counts=(len(leads), len(rests)),
            places=places,
            mp_count=mp_count,
        ),
        out_shape=(out, out),
        in_specs=[smem, smem] + [vmem] * (len(leads) + len(rests) + 2),
        out_specs=(vmem, vmem),
        scratch_shapes=[
            pltpu.VMEM((total, width), jnp.bfloat16),
            pltpu.VMEM((width, total), jnp.bfloat16),
            pltpu.VMEM((2, row_count, width), jnp.bfloat16),
            pltpu.VMEM((8, total), jnp.float32),
        ],
        compiler_params=pltpu.CompilerParams(vmem_limit_bytes=40 * 1024 * 1024),
    )(
        jnp.reshape(mp_index, (1,)).astype(jnp.int32),
        jnp.reshape(logit_scale, (1,)),
        *leads,
        *rests,
        videos[None, :],
        videos[:, None],
    )


def body(clips, captions, video_id, logit_scale):
    dp_count, mp_count = lax.axis_size("dp"), lax.axis_size("mp")
    gathered_bytes = 2 * clips.size * clips.dtype.itemsize * dp_count * mp_count
    if len(gather_orders(dp_count)[0]) == 2 and gathered_bytes <= resident_limit:
        return resident_body(clips, captions, video_id, logit_scale)
    return streamed_body(clips, captions, video_id, logit_scale)


def solution(mesh):
    in_specs = (P("dp", "mp"), P("dp", "mp"), P(), P())
    out_specs = (P(("dp", "mp"), None), P(("dp", "mp"), None))
    return jax.shard_map(body, mesh=mesh, in_specs=in_specs, out_specs=out_specs, check_vma=False)
```

```python
import functools
import math

import jax
import jax.numpy as jnp
from jax import lax
from jax.experimental import pallas as pl
from jax.experimental.pallas import tpu as pltpu
from jax.sharding import PartitionSpec as P

epsilon = 1e-06
negative_fill = -1e30
log2_e = math.log2(math.e)
resident_limit = 8 * 1024 * 1024


def unit_rows(values):
    widened = values.astype(jnp.float32)
    length = jnp.sqrt(jnp.sum(widened * widened, axis=-1, keepdims=True) + epsilon)
    return widened / length, length


def gather_columns(block):
    count = lax.axis_size("mp")
    chunks = [block]
    for k in range(1, count):
        chunks.append(lax.ppermute(block, "mp", [(i, i ^ k) for i in range(count)]))
    return jnp.concatenate(chunks, axis=-1)


def gather_orders(dp_count):
    bits = [1 << k for k in range(1, dp_count.bit_length() - 1)]
    return bits, bits[1:] + bits[:1]


def gather_blocks(block):
    dp_count = lax.axis_size("dp")
    even, odd = gather_orders(dp_count)
    held = block[None]
    for bit_even, bit_odd in zip(even, odd):
        route = [(i, i ^ (bit_odd if i & 1 else bit_even)) for i in range(dp_count)]
        held = jnp.concatenate([held, lax.ppermute(held, "dp", route)], axis=0)
    other = lax.ppermute(held, "dp", [(i, i ^ 1) for i in range(dp_count)])
    return jnp.concatenate([held, other], axis=0)


def block_offsets(dp_count):
    even, odd = gather_orders(dp_count)
    own = []
    for order in (even, odd):
        held = [0]
        for bit in order:
            held = held + [h ^ bit for h in held]
        own.append(held)
    return [own[0] + [h ^ 1 for h in own[1]], own[1] + [h ^ 1 for h in own[0]]]


def streamed_kernel(
    mp_ref,
    scale_ref,
    clips_ref,
    caps_ref,
    own_clips_ref,
    own_caps_ref,
    row_videos_ref,
    column_videos_ref,
    d_clips_ref,
    d_caps_ref,
    row_lse_ref,
    col_max_ref,
    col_sum_ref,
    *,
    mp_count,
):
    total = clips_ref.shape[0]
    own = own_clips_ref.shape[0]
    width = clips_ref.shape[1]
    row_tile = min(256, total)
    col_tile = min(1024, total)
    mp_index = mp_ref[0]
    scale = scale_ref[0]
    scale2 = scale * log2_e
    contract_last = (((1,), (1,)), ((), ()))

    col_max_ref[...] = jnp.full(col_max_ref.shape, negative_fill, jnp.float32)
    col_sum_ref[...] = jnp.zeros(col_sum_ref.shape, jnp.float32)

    def one_tile(row_first, col_first, carry):
        row_max, row_sum = carry
        rows = pl.ds(row_first, row_tile)
        cols = pl.ds(col_first, col_tile)
        scores = scale2 * lax.dot_general(
            clips_ref[rows, :], caps_ref[cols, :], contract_last, preferred_element_type=jnp.float32
        )
        same = column_videos_ref[rows, :] == row_videos_ref[:, cols]
        distance = lax.broadcasted_iota(jnp.int32, scores.shape, 0) - lax.broadcasted_iota(
            jnp.int32, scores.shape, 1
        )
        off_diagonal = distance != col_first - row_first
        scores = jnp.where(same & off_diagonal, negative_fill, scores)
        new_row = jnp.maximum(row_max, jnp.max(scores, axis=1, keepdims=True))
        row_sum = row_sum * jnp.exp2(row_max - new_row) + jnp.sum(
            jnp.exp2(scores - new_row), axis=1, keepdims=True
        )
        old_col = col_max_ref[:, cols]
        new_col = jnp.maximum(old_col, jnp.max(scores, axis=0, keepdims=True))
        col_sum_ref[:, cols] = col_sum_ref[:, cols] * jnp.exp2(old_col - new_col) + jnp.sum(
            jnp.exp2(scores - new_col), axis=0, keepdims=True
        )
        col_max_ref[:, cols] = new_col
        return new_row, row_sum

    def one_row_block(block):
        row_first = block * row_tile
        if not isinstance(block, int):
            row_first = pl.multiple_of(row_first, row_tile)
        carry = (
            jnp.full((row_tile, 1), negative_fill, jnp.float32),
            jnp.zeros((row_tile, 1), jnp.float32),
        )
        if total == col_tile:
            row_max, row_sum = one_tile(row_first, 0, carry)
        else:
            row_max, row_sum = lax.fori_loop(
                0,
                total // col_tile,
                lambda c, so_far: one_tile(row_first, pl.multiple_of(c * col_tile, col_tile), so_far),
                carry,
            )
        lse = row_max + jnp.log2(row_sum)
        row_lse_ref[:, pl.ds(row_first, row_tile)] = jnp.transpose(
            jnp.broadcast_to(lse, (row_tile, 128))
        )[:8, :]

    if total // row_tile <= 8:
        for block in range(total // row_tile):
            one_row_block(block)
    else:
        pl.loop(0, total // row_tile)(one_row_block)

    col_lse = col_max_ref[...] + jnp.log2(col_sum_ref[...])
    row_lse = row_lse_ref[0:1, :]

    own_first = pl.multiple_of(mp_index * own, own)
    own_rows = pl.ds(own_first, own)
    clip_unit = clips_ref[own_rows, :]
    cap_unit = caps_ref[own_rows, :]
    same = column_videos_ref[own_rows, :] == row_videos_ref[...]
    distance = lax.broadcasted_iota(jnp.int32, (own, total), 1) - lax.broadcasted_iota(
        jnp.int32, (own, total), 0
    )
    blocked = same & (distance != own_first)
    same = same.astype(jnp.bfloat16)

    def strip(unit, others_ref, own_lse_all, other_lse):
        scores = scale2 * lax.dot_general(
            unit, others_ref[...], contract_last, preferred_element_type=jnp.float32
        )
        scores = jnp.where(blocked, negative_fill, scores)
        top = jnp.max(scores, axis=1, keepdims=True)
        own_lse = top + jnp.log2(jnp.sum(jnp.exp2(scores - top), axis=1, keepdims=True))
        weights = 0.5 * (jnp.exp2(scores - own_lse) + jnp.exp2(scores - other_lse))
        weights = weights.astype(jnp.bfloat16)
        both = jnp.concatenate([weights, same], axis=0)
        sums = jnp.dot(both, others_ref[...], preferred_element_type=jnp.float32)
        return sums[:own], sums[own:]

    clip_acc, caption_pool = strip(clip_unit, caps_ref, None, col_lse)
    cap_acc, pooled = strip(cap_unit, clips_ref, None, row_lse)
    clip_unit = clip_unit.astype(jnp.float32)
    cap_unit = cap_unit.astype(jnp.float32)
    pool_length = jnp.sqrt(jnp.sum(pooled * pooled, axis=1, keepdims=True) + epsilon)
    pool_unit = pooled / pool_length
    projected = caption_pool - pool_unit * jnp.sum(pool_unit * caption_pool, axis=1, keepdims=True)
    clip_grad = scale * clip_acc - 0.5 * scale * cap_unit - 0.5 * scale * projected / pool_length
    cap_grad = scale * cap_acc - 0.5 * scale * clip_unit - 0.5 * scale * pool_unit

    def finish(values_ref, grad, out_ref):
        unit, length = unit_rows(values_ref[...])
        result = (grad - unit * jnp.sum(unit * grad, axis=1, keepdims=True)) / length
        chunk = width // mp_count
        for index in range(mp_count):

            @pl.when(mp_index == index)
            def _():
                out_ref[...] = jnp.concatenate(
                    [result[:, (q ^ index) * chunk : ((q ^ index) + 1) * chunk] for q in range(mp_count)],
                    axis=1,
                )

    finish(own_clips_ref, clip_grad, d_clips_ref)
    finish(own_caps_ref, cap_grad, d_caps_ref)


def streamed_body(clips, captions, video_id, logit_scale):
    dp_count = lax.axis_size("dp")
    mp_count = lax.axis_size("mp")
    row_count = clips.shape[0]
    own = row_count // mp_count
    width = clips.shape[1] * mp_count
    total = row_count * dp_count
    dp_index = lax.axis_index("dp")
    mp_index = lax.axis_index("mp")

    full = gather_columns(jnp.stack([clips, captions]))
    unit = unit_rows(full)[0].astype(jnp.bfloat16)
    own_raw = lax.dynamic_slice_in_dim(full, mp_index * own, own, 1)
    every = gather_blocks(unit)
    all_clips = every[:, 0].reshape(total, width)
    all_caps = every[:, 1].reshape(total, width)

    offsets = block_offsets(dp_count)
    videos = []
    for even, odd in zip(*offsets):
        block = dp_index ^ jnp.where(dp_index & 1, odd, even)
        videos.append(lax.dynamic_slice_in_dim(video_id, block * row_count, row_count, 0))
    videos = jnp.concatenate(videos)

    vmem = pl.BlockSpec(memory_space=pltpu.VMEM)
    smem = pl.BlockSpec(memory_space=pltpu.SMEM)
    out = jax.ShapeDtypeStruct((own, width), jnp.float32)
    return pl.pallas_call(
        functools.partial(streamed_kernel, mp_count=mp_count),
        out_shape=(out, out),
        in_specs=[smem, smem] + [vmem] * 6,
        out_specs=(vmem, vmem),
        scratch_shapes=[
            pltpu.VMEM((8, total), jnp.float32),
            pltpu.VMEM((1, total), jnp.float32),
            pltpu.VMEM((1, total), jnp.float32),
        ],
        compiler_params=pltpu.CompilerParams(vmem_limit_bytes=48 * 1024 * 1024),
    )(
        jnp.reshape(mp_index, (1,)).astype(jnp.int32),
        jnp.reshape(logit_scale, (1,)),
        all_clips,
        all_caps,
        own_raw[0],
        own_raw[1],
        videos[None, :],
        videos[:, None],
    )


def joined_lse(left, right):
    top = jnp.maximum(left, right)
    return top + jnp.log2(jnp.exp2(left - top) + jnp.exp2(right - top))


def lane_vector(column):
    return jnp.transpose(jnp.broadcast_to(column, (column.shape[0], 128)))[0:1, :]


def add_terms(stat, scores, axis):
    top = jnp.max(scores, axis=axis, keepdims=True)
    if stat is not None:
        top = jnp.maximum(stat[0], top)
    terms = jnp.sum(jnp.exp2(scores - top), axis=axis, keepdims=True)
    if stat is not None:
        terms = terms + stat[1] * jnp.exp2(stat[0] - top)
    return top, terms


def stage_kernel(*refs, piece_counts, places, old_count, mp_count, final):
    mp_ref, scale_ref, row_videos_ref, column_videos_ref = refs[:4]
    refs = refs[4:]
    lead_refs, refs = refs[: piece_counts[0]], refs[piece_counts[0] :]
    rest_refs, refs = refs[: piece_counts[1]], refs[piece_counts[1] :]
    old_refs, refs = refs[: 2 * old_count], refs[2 * old_count :]
    old = [(old_refs[2 * k], old_refs[2 * k + 1]) for k in range(old_count)]
    if old_count:
        row_old_ref, col_old_ref, own_ref = refs[:3]
        refs = refs[3:]
    if final:
        d_clips_ref, d_caps_ref, clips_ref, caps_ref = refs
    elif old_count:
        clips_ref, caps_ref, row_ref, col_ref = refs
    else:
        clips_ref, caps_ref, row_ref, col_ref, own_ref = refs
    fresh, width = clips_ref.shape
    rows = fresh // len(places)
    chunk = width // mp_count
    start = sum(clips.shape[0] for clips, _ in old)
    total = start + fresh
    mp_index = mp_ref[0]
    scale = scale_ref[0]
    scale2 = scale * log2_e

    for position, (lead_place, rest_place) in enumerate(places):
        span = pl.ds(position * rows, rows)
        for kind in range(2):
            lead_ref, lead_at = lead_refs[lead_place[0]], lead_place[1]
            rest_ref, rest_at = rest_refs[rest_place[0]], rest_place[1]
            raw = jnp.concatenate(
                [
                    lead_ref[kind, lead_at * chunk : (lead_at + 1) * chunk, :],
                    rest_ref[kind, rest_at * (width - chunk) : (rest_at + 1) * (width - chunk), :],
                ],
                axis=0,
            )
            if position == 0 and not old_count:
                own_ref[kind] = jnp.transpose(raw)
            wide = raw.astype(jnp.float32)
            inverse = 1.0 / jnp.sqrt(jnp.sum(wide * wide, axis=0, keepdims=True) + epsilon)
            unit = (wide * inverse).astype(jnp.bfloat16)
            if kind == 0:
                clips_ref[span, :] = jnp.transpose(unit)
            else:
                caps_ref[:, span] = unit

    def tile(clip_tile, row_first, caps, col_first):
        size = (clip_tile.shape[0], caps.shape[1])
        scores = scale2 * jnp.dot(clip_tile, caps[...], preferred_element_type=jnp.float32)
        banned = (
            column_videos_ref[row_first : row_first + size[0], :]
            == row_videos_ref[:, col_first : col_first + size[1]]
        )
        if col_first <= row_first < col_first + size[1]:
            distance = lax.broadcasted_iota(jnp.int32, size, 1) - lax.broadcasted_iota(jnp.int32, size, 0)
            banned = banned & (distance != row_first - col_first)
        return jnp.where(banned, negative_fill, scores)

    row_tile = min(2 * rows, fresh)
    row_parts = []
    col_new = None
    at = 0
    for clips, _ in old:
        for first in range(0, clips.shape[0], row_tile):
            scores = tile(clips[first : first + row_tile, :], at + first, caps_ref, start)
            top, terms = add_terms(None, scores, 1)
            col_new = add_terms(col_new, scores, 0)
            row_parts.append(lane_vector(top + jnp.log2(terms)))
        at += clips.shape[0]
    col_olds = [None] * old_count
    row_news = []
    for first in range(0, fresh, row_tile):
        stat = None
        clip_tile = clips_ref[first : first + row_tile, :]
        at = 0
        for k, (clips, caps) in enumerate(old):
            scores = tile(clip_tile, start + first, caps, at)
            stat = add_terms(stat, scores, 1)
            col_olds[k] = add_terms(col_olds[k], scores, 0)
            at += clips.shape[0]
        scores = tile(clip_tile, start + first, caps_ref, start)
        top, terms = add_terms(stat, scores, 1)
        col_new = add_terms(col_new, scores, 0)
        row_news.append(lane_vector(top + jnp.log2(terms)))
    row_lse = row_news
    col_lse = [col_new[0] + jnp.log2(col_new[1])]
    if old_count:
        old_part = jnp.concatenate(row_parts, axis=1)
        row_lse = [joined_lse(row_old_ref[...], old_part)] + row_lse
        old_part = jnp.concatenate([top + jnp.log2(terms) for top, terms in col_olds], axis=1)
        col_lse = [joined_lse(col_old_ref[...], old_part)] + col_lse
    row_lse = jnp.concatenate(row_lse, axis=1)
    col_lse = jnp.concatenate(col_lse, axis=1)
    if not final:
        row_ref[...] = row_lse
        col_ref[...] = col_lse
        return

    own = d_clips_ref.shape[0]
    every = old + [(clips_ref, caps_ref)]
    own_first = pl.multiple_of(mp_index * own, own)
    own_rows = pl.ds(own_first, own)
    clip_float, clip_length = unit_rows(own_ref[0, own_rows, :])
    cap_float, cap_length = unit_rows(own_ref[1, own_rows, :])
    clip_unit = old[0][0][own_rows, :]
    cap_unit = cap_float.astype(jnp.bfloat16)
    same = column_videos_ref[own_rows, :] == row_videos_ref[...]
    distance = lax.broadcasted_iota(jnp.int32, (own, total), 1) - lax.broadcasted_iota(
        jnp.int32, (own, total), 0
    )
    blocked = same & (distance != own_first)
    same = same.astype(jnp.bfloat16)
    last = (((1,), (1,)), ((), ()))

    def strip(products, other_lse):
        scores = jnp.where(blocked, negative_fill, scale2 * jnp.concatenate(products, axis=1))
        top, terms = add_terms(None, scores, 1)
        weights = 0.5 * (jnp.exp2(scores - (top + jnp.log2(terms))) + jnp.exp2(scores - other_lse))
        return jnp.concatenate([weights.astype(jnp.bfloat16), same], axis=0)

    def summed(weights, multiply):
        at, result = 0, None
        for clips, caps in every:
            part = multiply(weights[:, at : at + clips.shape[0]], clips, caps)
            result = part if result is None else result + part
            at += clips.shape[0]
        return result[:own], result[own:]

    clip_products = [
        jnp.dot(clip_unit, caps[...], preferred_element_type=jnp.float32) for _, caps in every
    ]
    cap_products = [
        lax.dot_general(cap_unit, clips[...], last, preferred_element_type=jnp.float32)
        for clips, _ in every
    ]
    clip_acc, caption_pool = summed(
        strip(clip_products, col_lse),
        lambda w, clips, caps: lax.dot_general(w, caps[...], last, preferred_element_type=jnp.float32),
    )
    cap_acc, pooled = summed(
        strip(cap_products, row_lse),
        lambda w, clips, caps: jnp.dot(w, clips[...], preferred_element_type=jnp.float32),
    )
    pool_length = jnp.sqrt(jnp.sum(pooled * pooled, axis=1, keepdims=True) + epsilon)
    pool_unit = pooled / pool_length
    projected = caption_pool - pool_unit * jnp.sum(pool_unit * caption_pool, axis=1, keepdims=True)
    clip_grad = (
        scale * clip_acc
        - 0.5 * scale * cap_unit.astype(jnp.float32)
        - 0.5 * scale * projected / pool_length
    )
    cap_grad = scale * cap_acc - 0.5 * scale * clip_unit.astype(jnp.float32) - 0.5 * scale * pool_unit

    def finish(unit, length, grad, out_ref):
        result = (grad - unit * jnp.sum(unit * grad, axis=1, keepdims=True)) / length
        for index in range(mp_count):

            @pl.when(mp_index == index)
            def _():
                out_ref[...] = jnp.concatenate(
                    [result[:, (q ^ index) * chunk : ((q ^ index) + 1) * chunk] for q in range(mp_count)],
                    axis=1,
                )

    finish(clip_float, clip_length, clip_grad, d_clips_ref)
    finish(cap_float, cap_length, cap_grad, d_caps_ref)


def resident_body(clips, captions, video_id, logit_scale):
    dp_count = lax.axis_size("dp")
    mp_count = lax.axis_size("mp")
    row_count = clips.shape[0]
    own = row_count // mp_count
    width = clips.shape[1] * mp_count
    dp_index = lax.axis_index("dp")
    mp_index = lax.axis_index("mp")
    even, odd = gather_orders(dp_count)

    def along(step, block):
        route = [(i, i ^ (odd[step] if i & 1 else even[step])) for i in range(dp_count)]
        return lax.ppermute(block, "dp", route)

    def across(block):
        return lax.ppermute(block, "dp", [(i, i ^ 1) for i in range(dp_count)])

    reached = [(0, 0), (even[0], odd[0]), (even[1], odd[1]), (even[0] ^ even[1], odd[0] ^ odd[1])]
    crossed = [(b ^ 1, a ^ 1) for a, b in reached]
    ordered = [reached[0], crossed[0], reached[1], reached[2], crossed[1], crossed[2], reached[3], crossed[3]]
    videos = []
    for even_offset, odd_offset in ordered:
        block = dp_index ^ jnp.where(dp_index & 1, odd_offset, even_offset)
        videos.append(lax.dynamic_slice_in_dim(video_id, block * row_count, row_count, 0))
    videos = jnp.concatenate(videos)
    common = (
        jnp.reshape(mp_index, (1,)).astype(jnp.int32),
        jnp.reshape(logit_scale, (1,)),
        videos[None, :],
        videos[:, None],
    )
    vmem = pl.BlockSpec(memory_space=pltpu.VMEM)
    smem = pl.BlockSpec(memory_space=pltpu.SMEM)

    def stage(leads, rests, places, old, carried, final=False):
        fresh = len(places) * row_count
        total = fresh + sum(clips.shape[0] for clips, _ in old)
        units = [((fresh, width), jnp.bfloat16), ((width, fresh), jnp.bfloat16)]
        scratch = []
        if final:
            outs = [((own, width), jnp.float32)] * 2
            scratch = [pltpu.VMEM(*unit) for unit in units]
        else:
            outs = units + [((1, total), jnp.float32)] * 2
            if not old:
                outs = outs + [((2, row_count, width), jnp.bfloat16)]
        operands = [*common, *leads, *rests, *[unit for pair in old for unit in pair], *carried]
        score_count = (2 * total - fresh) * fresh
        return pl.pallas_call(
            functools.partial(
                stage_kernel,
                piece_counts=(len(leads), len(rests)),
                places=places,
                old_count=len(old),
                mp_count=mp_count,
                final=final,
            ),
            out_shape=[jax.ShapeDtypeStruct(*out) for out in outs],
            in_specs=[smem, smem] + [vmem] * (len(operands) - 2),
            out_specs=[vmem] * len(outs),
            scratch_shapes=scratch,
            cost_estimate=pl.CostEstimate(
                flops=2 * score_count * width, bytes_accessed=8 * fresh * width, transcendentals=2 * score_count
            ),
            compiler_params=pltpu.CompilerParams(vmem_limit_bytes=32 * 1024 * 1024),
        )(*operands)

    lead = jnp.stack([clips.T, captions.T])
    lead_first = along(0, lead)
    arrived = [
        lax.ppermute(lead, "mp", [(i, i ^ k) for i in range(mp_count)]) for k in range(1, mp_count)
    ]
    lead_second = along(1, jnp.concatenate([lead, lead_first], axis=1))
    rest = jnp.concatenate(arrived, axis=1)
    rest, lead_second = lax.optimization_barrier((rest, lead_second))
    rest_first = along(0, rest)
    lead_other = across(jnp.concatenate([lead, lead_first, lead_second], axis=1))
    rest_other = across(rest)
    clips_a, caps_a, row_a, col_a, own_raw = stage(
        [lead, lead_other], [rest, rest_other], [((0, 0), (0, 0)), ((1, 0), (1, 0))], [], []
    )
    rest, row_a = lax.optimization_barrier((rest, row_a))
    rest_second = along(1, rest)
    rest_third = along(1, rest_first)
    clips_b, caps_b, row_b, col_b = stage(
        [lead_first, lead_second, lead_other],
        [rest_first, rest_second, across(rest_first), across(rest_second)],
        [((0, 0), (0, 0)), ((1, 0), (1, 0)), ((2, 1), (2, 0)), ((2, 2), (3, 0))],
        [(clips_a, caps_a)],
        [row_a, col_a, own_raw],
    )
    return tuple(
        stage(
            [lead_second, lead_other],
            [rest_third, across(rest_third)],
            [((0, 1), (0, 0)), ((1, 3), (1, 0))],
            [(clips_a, caps_a), (clips_b, caps_b)],
            [row_b, col_b, own_raw],
            final=True,
        )
    )


def body(clips, captions, video_id, logit_scale):
    dp_count, mp_count = lax.axis_size("dp"), lax.axis_size("mp")
    gathered_bytes = 2 * clips.size * clips.dtype.itemsize * dp_count * mp_count
    if len(gather_orders(dp_count)[0]) == 2 and gathered_bytes <= resident_limit:
        return resident_body(clips, captions, video_id, logit_scale)
    return streamed_body(clips, captions, video_id, logit_scale)


def solution(mesh):
    in_specs = (P("dp", "mp"), P("dp", "mp"), P(), P())
    out_specs = (P(("dp", "mp"), None), P(("dp", "mp"), None))
    return jax.shard_map(body, mesh=mesh, in_specs=in_specs, out_specs=out_specs, check_vma=False)
```

```python
import functools
import math

import jax
import jax.numpy as jnp
from jax import lax
from jax.experimental import pallas as pl
from jax.experimental.pallas import tpu as pltpu
from jax.sharding import PartitionSpec as P

epsilon = 1e-06
negative_fill = -1e30
log2_e = math.log2(math.e)
resident_limit = 8 * 1024 * 1024


def unit_rows(values):
    widened = values.astype(jnp.float32)
    length = jnp.sqrt(jnp.sum(widened * widened, axis=-1, keepdims=True) + epsilon)
    return widened / length, length


def gather_columns(block):
    count = lax.axis_size("mp")
    chunks = [block]
    for k in range(1, count):
        chunks.append(lax.ppermute(block, "mp", [(i, i ^ k) for i in range(count)]))
    return jnp.concatenate(chunks, axis=-1)


def gather_orders(dp_count):
    bits = [1 << k for k in range(1, dp_count.bit_length() - 1)]
    return bits, bits[1:] + bits[:1]


def gather_blocks(block):
    dp_count = lax.axis_size("dp")
    even, odd = gather_orders(dp_count)
    held = block[None]
    for bit_even, bit_odd in zip(even, odd):
        route = [(i, i ^ (bit_odd if i & 1 else bit_even)) for i in range(dp_count)]
        held = jnp.concatenate([held, lax.ppermute(held, "dp", route)], axis=0)
    other = lax.ppermute(held, "dp", [(i, i ^ 1) for i in range(dp_count)])
    return jnp.concatenate([held, other], axis=0)


def block_offsets(dp_count):
    even, odd = gather_orders(dp_count)
    own = []
    for order in (even, odd):
        held = [0]
        for bit in order:
            held = held + [h ^ bit for h in held]
        own.append(held)
    return [own[0] + [h ^ 1 for h in own[1]], own[1] + [h ^ 1 for h in own[0]]]


def streamed_kernel(
    mp_ref,
    scale_ref,
    clips_ref,
    caps_ref,
    own_clips_ref,
    own_caps_ref,
    row_videos_ref,
    column_videos_ref,
    d_clips_ref,
    d_caps_ref,
    row_lse_ref,
    col_max_ref,
    col_sum_ref,
    *,
    mp_count,
):
    total = clips_ref.shape[0]
    own = own_clips_ref.shape[0]
    width = clips_ref.shape[1]
    row_tile = min(256, total)
    col_tile = min(1024, total)
    mp_index = mp_ref[0]
    scale = scale_ref[0]
    scale2 = scale * log2_e
    contract_last = (((1,), (1,)), ((), ()))

    col_max_ref[...] = jnp.full(col_max_ref.shape, negative_fill, jnp.float32)
    col_sum_ref[...] = jnp.zeros(col_sum_ref.shape, jnp.float32)

    def one_tile(row_first, col_first, carry):
        row_max, row_sum = carry
        rows = pl.ds(row_first, row_tile)
        cols = pl.ds(col_first, col_tile)
        scores = scale2 * lax.dot_general(
            clips_ref[rows, :], caps_ref[cols, :], contract_last, preferred_element_type=jnp.float32
        )
        same = column_videos_ref[rows, :] == row_videos_ref[:, cols]
        distance = lax.broadcasted_iota(jnp.int32, scores.shape, 0) - lax.broadcasted_iota(
            jnp.int32, scores.shape, 1
        )
        off_diagonal = distance != col_first - row_first
        scores = jnp.where(same & off_diagonal, negative_fill, scores)
        new_row = jnp.maximum(row_max, jnp.max(scores, axis=1, keepdims=True))
        row_sum = row_sum * jnp.exp2(row_max - new_row) + jnp.sum(
            jnp.exp2(scores - new_row), axis=1, keepdims=True
        )
        old_col = col_max_ref[:, cols]
        new_col = jnp.maximum(old_col, jnp.max(scores, axis=0, keepdims=True))
        col_sum_ref[:, cols] = col_sum_ref[:, cols] * jnp.exp2(old_col - new_col) + jnp.sum(
            jnp.exp2(scores - new_col), axis=0, keepdims=True
        )
        col_max_ref[:, cols] = new_col
        return new_row, row_sum

    def one_row_block(block):
        row_first = block * row_tile
        if not isinstance(block, int):
            row_first = pl.multiple_of(row_first, row_tile)
        carry = (
            jnp.full((row_tile, 1), negative_fill, jnp.float32),
            jnp.zeros((row_tile, 1), jnp.float32),
        )
        if total == col_tile:
            row_max, row_sum = one_tile(row_first, 0, carry)
        else:
            row_max, row_sum = lax.fori_loop(
                0,
                total // col_tile,
                lambda c, so_far: one_tile(row_first, pl.multiple_of(c * col_tile, col_tile), so_far),
                carry,
            )
        lse = row_max + jnp.log2(row_sum)
        row_lse_ref[:, pl.ds(row_first, row_tile)] = jnp.transpose(
            jnp.broadcast_to(lse, (row_tile, 128))
        )[:8, :]

    if total // row_tile <= 8:
        for block in range(total // row_tile):
            one_row_block(block)
    else:
        pl.loop(0, total // row_tile)(one_row_block)

    col_lse = col_max_ref[...] + jnp.log2(col_sum_ref[...])
    row_lse = row_lse_ref[0:1, :]

    own_first = pl.multiple_of(mp_index * own, own)
    own_rows = pl.ds(own_first, own)
    clip_unit = clips_ref[own_rows, :]
    cap_unit = caps_ref[own_rows, :]
    same = column_videos_ref[own_rows, :] == row_videos_ref[...]
    distance = lax.broadcasted_iota(jnp.int32, (own, total), 1) - lax.broadcasted_iota(
        jnp.int32, (own, total), 0
    )
    blocked = same & (distance != own_first)
    same = same.astype(jnp.bfloat16)

    def strip(unit, others_ref, own_lse_all, other_lse):
        scores = scale2 * lax.dot_general(
            unit, others_ref[...], contract_last, preferred_element_type=jnp.float32
        )
        scores = jnp.where(blocked, negative_fill, scores)
        top = jnp.max(scores, axis=1, keepdims=True)
        own_lse = top + jnp.log2(jnp.sum(jnp.exp2(scores - top), axis=1, keepdims=True))
        weights = 0.5 * (jnp.exp2(scores - own_lse) + jnp.exp2(scores - other_lse))
        weights = weights.astype(jnp.bfloat16)
        both = jnp.concatenate([weights, same], axis=0)
        sums = jnp.dot(both, others_ref[...], preferred_element_type=jnp.float32)
        return sums[:own], sums[own:]

    clip_acc, caption_pool = strip(clip_unit, caps_ref, None, col_lse)
    cap_acc, pooled = strip(cap_unit, clips_ref, None, row_lse)
    clip_unit = clip_unit.astype(jnp.float32)
    cap_unit = cap_unit.astype(jnp.float32)
    pool_length = jnp.sqrt(jnp.sum(pooled * pooled, axis=1, keepdims=True) + epsilon)
    pool_unit = pooled / pool_length
    projected = caption_pool - pool_unit * jnp.sum(pool_unit * caption_pool, axis=1, keepdims=True)
    clip_grad = scale * clip_acc - 0.5 * scale * cap_unit - 0.5 * scale * projected / pool_length
    cap_grad = scale * cap_acc - 0.5 * scale * clip_unit - 0.5 * scale * pool_unit

    def finish(values_ref, grad, out_ref):
        unit, length = unit_rows(values_ref[...])
        result = (grad - unit * jnp.sum(unit * grad, axis=1, keepdims=True)) / length
        chunk = width // mp_count
        for index in range(mp_count):

            @pl.when(mp_index == index)
            def _():
                out_ref[...] = jnp.concatenate(
                    [result[:, (q ^ index) * chunk : ((q ^ index) + 1) * chunk] for q in range(mp_count)],
                    axis=1,
                )

    finish(own_clips_ref, clip_grad, d_clips_ref)
    finish(own_caps_ref, cap_grad, d_caps_ref)


def streamed_body(clips, captions, video_id, logit_scale):
    dp_count = lax.axis_size("dp")
    mp_count = lax.axis_size("mp")
    row_count = clips.shape[0]
    own = row_count // mp_count
    width = clips.shape[1] * mp_count
    total = row_count * dp_count
    dp_index = lax.axis_index("dp")
    mp_index = lax.axis_index("mp")

    full = gather_columns(jnp.stack([clips, captions]))
    unit = unit_rows(full)[0].astype(jnp.bfloat16)
    own_raw = lax.dynamic_slice_in_dim(full, mp_index * own, own, 1)
    every = gather_blocks(unit)
    all_clips = every[:, 0].reshape(total, width)
    all_caps = every[:, 1].reshape(total, width)

    offsets = block_offsets(dp_count)
    videos = []
    for even, odd in zip(*offsets):
        block = dp_index ^ jnp.where(dp_index & 1, odd, even)
        videos.append(lax.dynamic_slice_in_dim(video_id, block * row_count, row_count, 0))
    videos = jnp.concatenate(videos)

    vmem = pl.BlockSpec(memory_space=pltpu.VMEM)
    smem = pl.BlockSpec(memory_space=pltpu.SMEM)
    out = jax.ShapeDtypeStruct((own, width), jnp.float32)
    return pl.pallas_call(
        functools.partial(streamed_kernel, mp_count=mp_count),
        out_shape=(out, out),
        in_specs=[smem, smem] + [vmem] * 6,
        out_specs=(vmem, vmem),
        scratch_shapes=[
            pltpu.VMEM((8, total), jnp.float32),
            pltpu.VMEM((1, total), jnp.float32),
            pltpu.VMEM((1, total), jnp.float32),
        ],
        compiler_params=pltpu.CompilerParams(vmem_limit_bytes=48 * 1024 * 1024),
    )(
        jnp.reshape(mp_index, (1,)).astype(jnp.int32),
        jnp.reshape(logit_scale, (1,)),
        all_clips,
        all_caps,
        own_raw[0],
        own_raw[1],
        videos[None, :],
        videos[:, None],
    )


def joined_lse(left, right):
    top = jnp.maximum(left, right)
    return top + jnp.log2(jnp.exp2(left - top) + jnp.exp2(right - top))


def lane_vector(column):
    return jnp.transpose(jnp.broadcast_to(column, (column.shape[0], 128)))[0:1, :]


def add_terms(stat, scores, axis):
    top = jnp.max(scores, axis=axis, keepdims=True)
    if stat is not None:
        top = jnp.maximum(stat[0], top)
    terms = jnp.sum(jnp.exp2(scores - top), axis=axis, keepdims=True)
    if stat is not None:
        terms = terms + stat[1] * jnp.exp2(stat[0] - top)
    return top, terms


def stage_kernel(*refs, piece_count, places, old_count, mp_count, final):
    mp_ref, scale_ref, row_videos_ref, column_videos_ref = refs[:4]
    refs = refs[4:]
    piece_refs, refs = refs[:piece_count], refs[piece_count:]
    old_refs, refs = refs[: 2 * old_count], refs[2 * old_count :]
    old = [(old_refs[2 * k], old_refs[2 * k + 1]) for k in range(old_count)]
    if old_count:
        row_old_ref, col_old_ref, own_ref = refs[:3]
        refs = refs[3:]
    if final:
        d_clips_ref, d_caps_ref, clips_ref, caps_ref = refs
    elif old_count:
        clips_ref, caps_ref, row_ref, col_ref = refs
    else:
        clips_ref, caps_ref, row_ref, col_ref, own_ref = refs
    fresh, width = clips_ref.shape
    rows = fresh // len(places)
    chunk = width // mp_count
    start = sum(clips.shape[0] for clips, _ in old)
    total = start + fresh
    mp_index = mp_ref[0]
    scale = scale_ref[0]
    scale2 = scale * log2_e

    for position, place in enumerate(places):
        span = pl.ds(position * rows, rows)
        for kind in range(2):
            raw = [
                piece_refs[piece][kind, first * chunk : (first + count) * chunk, :]
                for piece, first, count in place
            ]
            raw = jnp.concatenate(raw, axis=0)
            if position == 0 and not old_count:
                own_ref[kind] = jnp.transpose(raw)
            wide = raw.astype(jnp.float32)
            inverse = 1.0 / jnp.sqrt(jnp.sum(wide * wide, axis=0, keepdims=True) + epsilon)
            unit = (wide * inverse).astype(jnp.bfloat16)
            if kind == 0:
                clips_ref[span, :] = jnp.transpose(unit)
            else:
                caps_ref[:, span] = unit

    def tile(clip_tile, row_first, caps, col_first):
        size = (clip_tile.shape[0], caps.shape[1])
        scores = scale2 * jnp.dot(clip_tile, caps[...], preferred_element_type=jnp.float32)
        banned = (
            column_videos_ref[row_first : row_first + size[0], :]
            == row_videos_ref[:, col_first : col_first + size[1]]
        )
        if col_first <= row_first < col_first + size[1]:
            distance = lax.broadcasted_iota(jnp.int32, size, 1) - lax.broadcasted_iota(jnp.int32, size, 0)
            banned = banned & (distance != row_first - col_first)
        return jnp.where(banned, negative_fill, scores)

    row_tile = min(2 * rows, fresh)
    row_parts = []
    col_new = None
    at = 0
    for clips, _ in old:
        for first in range(0, clips.shape[0], row_tile):
            scores = tile(clips[first : first + row_tile, :], at + first, caps_ref, start)
            top, terms = add_terms(None, scores, 1)
            col_new = add_terms(col_new, scores, 0)
            row_parts.append(lane_vector(top + jnp.log2(terms)))
        at += clips.shape[0]
    col_olds = [None] * old_count
    row_news = []
    for first in range(0, fresh, row_tile):
        stat = None
        clip_tile = clips_ref[first : first + row_tile, :]
        at = 0
        for k, (clips, caps) in enumerate(old):
            scores = tile(clip_tile, start + first, caps, at)
            stat = add_terms(stat, scores, 1)
            col_olds[k] = add_terms(col_olds[k], scores, 0)
            at += clips.shape[0]
        scores = tile(clip_tile, start + first, caps_ref, start)
        top, terms = add_terms(stat, scores, 1)
        col_new = add_terms(col_new, scores, 0)
        row_news.append(lane_vector(top + jnp.log2(terms)))
    row_lse = row_news
    col_lse = [col_new[0] + jnp.log2(col_new[1])]
    if old_count:
        old_part = jnp.concatenate(row_parts, axis=1)
        row_lse = [joined_lse(row_old_ref[...], old_part)] + row_lse
        old_part = jnp.concatenate([top + jnp.log2(terms) for top, terms in col_olds], axis=1)
        col_lse = [joined_lse(col_old_ref[...], old_part)] + col_lse
    row_lse = jnp.concatenate(row_lse, axis=1)
    col_lse = jnp.concatenate(col_lse, axis=1)
    if not final:
        row_ref[...] = row_lse
        col_ref[...] = col_lse
        return

    own = d_clips_ref.shape[0]
    every = old + [(clips_ref, caps_ref)]
    own_first = pl.multiple_of(mp_index * own, own)
    own_rows = pl.ds(own_first, own)
    clip_float, clip_length = unit_rows(own_ref[0, own_rows, :])
    cap_float, cap_length = unit_rows(own_ref[1, own_rows, :])
    clip_unit = old[0][0][own_rows, :]
    cap_unit = cap_float.astype(jnp.bfloat16)
    same = column_videos_ref[own_rows, :] == row_videos_ref[...]
    distance = lax.broadcasted_iota(jnp.int32, (own, total), 1) - lax.broadcasted_iota(
        jnp.int32, (own, total), 0
    )
    blocked = same & (distance != own_first)
    same = same.astype(jnp.bfloat16)
    last = (((1,), (1,)), ((), ()))

    def strip(products, other_lse):
        scores = jnp.where(blocked, negative_fill, scale2 * jnp.concatenate(products, axis=1))
        top, terms = add_terms(None, scores, 1)
        weights = 0.5 * (jnp.exp2(scores - (top + jnp.log2(terms))) + jnp.exp2(scores - other_lse))
        return jnp.concatenate([weights.astype(jnp.bfloat16), same], axis=0)

    def summed(weights, multiply):
        at, result = 0, None
        for clips, caps in every:
            part = multiply(weights[:, at : at + clips.shape[0]], clips, caps)
            result = part if result is None else result + part
            at += clips.shape[0]
        return result[:own], result[own:]

    clip_products = [
        jnp.dot(clip_unit, caps[...], preferred_element_type=jnp.float32) for _, caps in every
    ]
    cap_products = [
        lax.dot_general(cap_unit, clips[...], last, preferred_element_type=jnp.float32)
        for clips, _ in every
    ]
    clip_acc, caption_pool = summed(
        strip(clip_products, col_lse),
        lambda w, clips, caps: lax.dot_general(w, caps[...], last, preferred_element_type=jnp.float32),
    )
    cap_acc, pooled = summed(
        strip(cap_products, row_lse),
        lambda w, clips, caps: jnp.dot(w, clips[...], preferred_element_type=jnp.float32),
    )
    pool_length = jnp.sqrt(jnp.sum(pooled * pooled, axis=1, keepdims=True) + epsilon)
    pool_unit = pooled / pool_length
    projected = caption_pool - pool_unit * jnp.sum(pool_unit * caption_pool, axis=1, keepdims=True)
    clip_grad = (
        scale * clip_acc
        - 0.5 * scale * cap_unit.astype(jnp.float32)
        - 0.5 * scale * projected / pool_length
    )
    cap_grad = scale * cap_acc - 0.5 * scale * clip_unit.astype(jnp.float32) - 0.5 * scale * pool_unit

    def finish(unit, length, grad, out_ref):
        result = (grad - unit * jnp.sum(unit * grad, axis=1, keepdims=True)) / length
        for index in range(mp_count):

            @pl.when(mp_index == index)
            def _():
                out_ref[...] = jnp.concatenate(
                    [result[:, (q ^ index) * chunk : ((q ^ index) + 1) * chunk] for q in range(mp_count)],
                    axis=1,
                )

    finish(clip_float, clip_length, clip_grad, d_clips_ref)
    finish(cap_float, cap_length, cap_grad, d_caps_ref)


def resident_body(clips, captions, video_id, logit_scale):
    dp_count = lax.axis_size("dp")
    mp_count = lax.axis_size("mp")
    row_count = clips.shape[0]
    own = row_count // mp_count
    width = clips.shape[1] * mp_count
    dp_index = lax.axis_index("dp")
    mp_index = lax.axis_index("mp")
    even, odd = gather_orders(dp_count)

    def along(step, block):
        route = [(i, i ^ (odd[step] if i & 1 else even[step])) for i in range(dp_count)]
        return lax.ppermute(block, "dp", route)

    def across(block):
        return lax.ppermute(block, "dp", [(i, i ^ 1) for i in range(dp_count)])

    reached = [(0, 0), (even[0], odd[0]), (even[1], odd[1]), (even[0] ^ even[1], odd[0] ^ odd[1])]
    crossed = [(b ^ 1, a ^ 1) for a, b in reached]
    ordered = [reached[0], crossed[0], reached[1], reached[2], crossed[1], crossed[2], reached[3], crossed[3]]
    videos = []
    for even_offset, odd_offset in ordered:
        block = dp_index ^ jnp.where(dp_index & 1, odd_offset, even_offset)
        videos.append(lax.dynamic_slice_in_dim(video_id, block * row_count, row_count, 0))
    videos = jnp.concatenate(videos)
    common = (
        jnp.reshape(mp_index, (1,)).astype(jnp.int32),
        jnp.reshape(logit_scale, (1,)),
        videos[None, :],
        videos[:, None],
    )
    vmem = pl.BlockSpec(memory_space=pltpu.VMEM)
    smem = pl.BlockSpec(memory_space=pltpu.SMEM)

    def stage(pieces, places, old, carried, final=False):
        fresh = len(places) * row_count
        total = fresh + sum(clips.shape[0] for clips, _ in old)
        units = [((fresh, width), jnp.bfloat16), ((width, fresh), jnp.bfloat16)]
        scratch = []
        if final:
            outs = [((own, width), jnp.float32)] * 2
            scratch = [pltpu.VMEM(*unit) for unit in units]
        else:
            outs = units + [((1, total), jnp.float32)] * 2
            if not old:
                outs = outs + [((2, row_count, width), jnp.bfloat16)]
        operands = [*common, *pieces, *[unit for pair in old for unit in pair], *carried]
        score_count = (2 * total - fresh) * fresh
        return pl.pallas_call(
            functools.partial(
                stage_kernel,
                piece_count=len(pieces),
                places=places,
                old_count=len(old),
                mp_count=mp_count,
                final=final,
            ),
            out_shape=[jax.ShapeDtypeStruct(*out) for out in outs],
            in_specs=[smem, smem] + [vmem] * (len(operands) - 2),
            out_specs=[vmem] * len(outs),
            scratch_shapes=scratch,
            cost_estimate=pl.CostEstimate(
                flops=1, bytes_accessed=1, transcendentals=0
            ),
            compiler_params=pltpu.CompilerParams(vmem_limit_bytes=32 * 1024 * 1024),
        )(*operands)

    def after(value, other):
        return lax.optimization_barrier((value, other))[0]

    others = mp_count - 1
    lead = jnp.stack([clips.T, captions.T])
    arrived = [
        lax.ppermute(lead, "mp", [(i, i ^ k) for i in range(mp_count)]) for k in range(1, mp_count)
    ]
    lead_first = along(0, after(lead, arrived[0]))
    lead_second = along(1, after(lead, arrived[0]))
    lead_pair = jnp.concatenate([lead, lead_first], axis=1)
    lead_pair_other = across(lead_pair)
    arrived[-1] = after(arrived[-1], (lead_first, lead_second, lead_pair_other))
    rest = jnp.concatenate(arrived, axis=1)
    rest_first = along(0, rest)
    clips_a, caps_a, row_a, col_a, own_raw = stage([lead, rest], [[(0, 0, 1), (1, 0, others)]], [], [])
    rest_second = along(1, after(rest, row_a))
    third = along(1, jnp.concatenate([lead_first, rest_first], axis=1))
    rest_other = across(after(rest, rest_first))
    lead_second_other = across(after(lead_second, rest_first))
    clips_b, caps_b, row_b, col_b = stage(
        [
            lead_pair_other,
            rest_other,
            lead_first,
            rest_first,
            lead_second,
            rest_second,
            across(rest_first),
            lead_second_other,
            across(rest_second),
        ],
        [
            [(0, 0, 1), (1, 0, others)],
            [(2, 0, 1), (3, 0, others)],
            [(4, 0, 1), (5, 0, others)],
            [(0, 1, 1), (6, 0, others)],
            [(7, 0, 1), (8, 0, others)],
        ],
        [(clips_a, caps_a)],
        [row_a, col_a, own_raw],
    )
    third_other = across(after(third, row_b))
    clips_c, caps_c, row_c, col_c = stage(
        [third],
        [[(0, 0, mp_count)]],
        [(clips_a, caps_a), (clips_b, caps_b)],
        [row_b, col_b, own_raw],
    )
    return tuple(
        stage(
            [third_other],
            [[(0, 0, mp_count)]],
            [(clips_a, caps_a), (clips_b, caps_b), (clips_c, caps_c)],
            [row_c, col_c, own_raw],
            final=True,
        )
    )


def body(clips, captions, video_id, logit_scale):
    dp_count, mp_count = lax.axis_size("dp"), lax.axis_size("mp")
    gathered_bytes = 2 * clips.size * clips.dtype.itemsize * dp_count * mp_count
    if len(gather_orders(dp_count)[0]) == 2 and gathered_bytes <= resident_limit:
        return resident_body(clips, captions, video_id, logit_scale)
    return streamed_body(clips, captions, video_id, logit_scale)


def solution(mesh):
    in_specs = (P("dp", "mp"), P("dp", "mp"), P(), P())
    out_specs = (P(("dp", "mp"), None), P(("dp", "mp"), None))
    return jax.shard_map(body, mesh=mesh, in_specs=in_specs, out_specs=out_specs, check_vma=False)
```

```python
import functools
import math

import jax
import jax.numpy as jnp
from jax import lax
from jax.experimental import pallas as pl
from jax.experimental.pallas import tpu as pltpu
from jax.sharding import PartitionSpec as P

epsilon = 1e-06
negative_fill = -1e30
log2_e = math.log2(math.e)
resident_limit = 8 * 1024 * 1024


def unit_rows(values):
    widened = values.astype(jnp.float32)
    length = jnp.sqrt(jnp.sum(widened * widened, axis=-1, keepdims=True) + epsilon)
    return widened / length, length


def gather_columns(block):
    count = lax.axis_size("mp")
    chunks = [block]
    for k in range(1, count):
        chunks.append(lax.ppermute(block, "mp", [(i, i ^ k) for i in range(count)]))
    return jnp.concatenate(chunks, axis=-1)


def gather_orders(dp_count):
    bits = [1 << k for k in range(1, dp_count.bit_length() - 1)]
    return bits, bits[1:] + bits[:1]


def gather_blocks(block):
    dp_count = lax.axis_size("dp")
    even, odd = gather_orders(dp_count)
    held = block[None]
    for bit_even, bit_odd in zip(even, odd):
        route = [(i, i ^ (bit_odd if i & 1 else bit_even)) for i in range(dp_count)]
        held = jnp.concatenate([held, lax.ppermute(held, "dp", route)], axis=0)
    other = lax.ppermute(held, "dp", [(i, i ^ 1) for i in range(dp_count)])
    return jnp.concatenate([held, other], axis=0)


def block_offsets(dp_count):
    even, odd = gather_orders(dp_count)
    own = []
    for order in (even, odd):
        held = [0]
        for bit in order:
            held = held + [h ^ bit for h in held]
        own.append(held)
    return [own[0] + [h ^ 1 for h in own[1]], own[1] + [h ^ 1 for h in own[0]]]


def streamed_kernel(
    mp_ref,
    scale_ref,
    clips_ref,
    caps_ref,
    own_clips_ref,
    own_caps_ref,
    row_videos_ref,
    column_videos_ref,
    d_clips_ref,
    d_caps_ref,
    row_lse_ref,
    col_max_ref,
    col_sum_ref,
    *,
    mp_count,
):
    total = clips_ref.shape[0]
    own = own_clips_ref.shape[0]
    width = clips_ref.shape[1]
    row_tile = min(256, total)
    col_tile = min(1024, total)
    mp_index = mp_ref[0]
    scale = scale_ref[0]
    scale2 = scale * log2_e
    contract_last = (((1,), (1,)), ((), ()))

    col_max_ref[...] = jnp.full(col_max_ref.shape, negative_fill, jnp.float32)
    col_sum_ref[...] = jnp.zeros(col_sum_ref.shape, jnp.float32)

    def one_tile(row_first, col_first, carry):
        row_max, row_sum = carry
        rows = pl.ds(row_first, row_tile)
        cols = pl.ds(col_first, col_tile)
        scores = scale2 * lax.dot_general(
            clips_ref[rows, :], caps_ref[cols, :], contract_last, preferred_element_type=jnp.float32
        )
        same = column_videos_ref[rows, :] == row_videos_ref[:, cols]
        distance = lax.broadcasted_iota(jnp.int32, scores.shape, 0) - lax.broadcasted_iota(
            jnp.int32, scores.shape, 1
        )
        off_diagonal = distance != col_first - row_first
        scores = jnp.where(same & off_diagonal, negative_fill, scores)
        new_row = jnp.maximum(row_max, jnp.max(scores, axis=1, keepdims=True))
        row_sum = row_sum * jnp.exp2(row_max - new_row) + jnp.sum(
            jnp.exp2(scores - new_row), axis=1, keepdims=True
        )
        old_col = col_max_ref[:, cols]
        new_col = jnp.maximum(old_col, jnp.max(scores, axis=0, keepdims=True))
        col_sum_ref[:, cols] = col_sum_ref[:, cols] * jnp.exp2(old_col - new_col) + jnp.sum(
            jnp.exp2(scores - new_col), axis=0, keepdims=True
        )
        col_max_ref[:, cols] = new_col
        return new_row, row_sum

    def one_row_block(block):
        row_first = block * row_tile
        if not isinstance(block, int):
            row_first = pl.multiple_of(row_first, row_tile)
        carry = (
            jnp.full((row_tile, 1), negative_fill, jnp.float32),
            jnp.zeros((row_tile, 1), jnp.float32),
        )
        if total == col_tile:
            row_max, row_sum = one_tile(row_first, 0, carry)
        else:
            row_max, row_sum = lax.fori_loop(
                0,
                total // col_tile,
                lambda c, so_far: one_tile(row_first, pl.multiple_of(c * col_tile, col_tile), so_far),
                carry,
            )
        lse = row_max + jnp.log2(row_sum)
        row_lse_ref[:, pl.ds(row_first, row_tile)] = jnp.transpose(
            jnp.broadcast_to(lse, (row_tile, 128))
        )[:8, :]

    if total // row_tile <= 8:
        for block in range(total // row_tile):
            one_row_block(block)
    else:
        pl.loop(0, total // row_tile)(one_row_block)

    col_lse = col_max_ref[...] + jnp.log2(col_sum_ref[...])
    row_lse = row_lse_ref[0:1, :]

    own_first = pl.multiple_of(mp_index * own, own)
    own_rows = pl.ds(own_first, own)
    clip_unit = clips_ref[own_rows, :]
    cap_unit = caps_ref[own_rows, :]
    same = column_videos_ref[own_rows, :] == row_videos_ref[...]
    distance = lax.broadcasted_iota(jnp.int32, (own, total), 1) - lax.broadcasted_iota(
        jnp.int32, (own, total), 0
    )
    blocked = same & (distance != own_first)
    same = same.astype(jnp.bfloat16)

    def strip(unit, others_ref, own_lse_all, other_lse):
        scores = scale2 * lax.dot_general(
            unit, others_ref[...], contract_last, preferred_element_type=jnp.float32
        )
        scores = jnp.where(blocked, negative_fill, scores)
        top = jnp.max(scores, axis=1, keepdims=True)
        own_lse = top + jnp.log2(jnp.sum(jnp.exp2(scores - top), axis=1, keepdims=True))
        weights = 0.5 * (jnp.exp2(scores - own_lse) + jnp.exp2(scores - other_lse))
        weights = weights.astype(jnp.bfloat16)
        both = jnp.concatenate([weights, same], axis=0)
        sums = jnp.dot(both, others_ref[...], preferred_element_type=jnp.float32)
        return sums[:own], sums[own:]

    clip_acc, caption_pool = strip(clip_unit, caps_ref, None, col_lse)
    cap_acc, pooled = strip(cap_unit, clips_ref, None, row_lse)
    clip_unit = clip_unit.astype(jnp.float32)
    cap_unit = cap_unit.astype(jnp.float32)
    pool_length = jnp.sqrt(jnp.sum(pooled * pooled, axis=1, keepdims=True) + epsilon)
    pool_unit = pooled / pool_length
    projected = caption_pool - pool_unit * jnp.sum(pool_unit * caption_pool, axis=1, keepdims=True)
    clip_grad = scale * clip_acc - 0.5 * scale * cap_unit - 0.5 * scale * projected / pool_length
    cap_grad = scale * cap_acc - 0.5 * scale * clip_unit - 0.5 * scale * pool_unit

    def finish(values_ref, grad, out_ref):
        unit, length = unit_rows(values_ref[...])
        result = (grad - unit * jnp.sum(unit * grad, axis=1, keepdims=True)) / length
        chunk = width // mp_count
        for index in range(mp_count):

            @pl.when(mp_index == index)
            def _():
                out_ref[...] = jnp.concatenate(
                    [result[:, (q ^ index) * chunk : ((q ^ index) + 1) * chunk] for q in range(mp_count)],
                    axis=1,
                )

    finish(own_clips_ref, clip_grad, d_clips_ref)
    finish(own_caps_ref, cap_grad, d_caps_ref)


def streamed_body(clips, captions, video_id, logit_scale):
    dp_count = lax.axis_size("dp")
    mp_count = lax.axis_size("mp")
    row_count = clips.shape[0]
    own = row_count // mp_count
    width = clips.shape[1] * mp_count
    total = row_count * dp_count
    dp_index = lax.axis_index("dp")
    mp_index = lax.axis_index("mp")

    full = gather_columns(jnp.stack([clips, captions]))
    unit = unit_rows(full)[0].astype(jnp.bfloat16)
    own_raw = lax.dynamic_slice_in_dim(full, mp_index * own, own, 1)
    every = gather_blocks(unit)
    all_clips = every[:, 0].reshape(total, width)
    all_caps = every[:, 1].reshape(total, width)

    offsets = block_offsets(dp_count)
    videos = []
    for even, odd in zip(*offsets):
        block = dp_index ^ jnp.where(dp_index & 1, odd, even)
        videos.append(lax.dynamic_slice_in_dim(video_id, block * row_count, row_count, 0))
    videos = jnp.concatenate(videos)

    vmem = pl.BlockSpec(memory_space=pltpu.VMEM)
    smem = pl.BlockSpec(memory_space=pltpu.SMEM)
    out = jax.ShapeDtypeStruct((own, width), jnp.float32)
    return pl.pallas_call(
        functools.partial(streamed_kernel, mp_count=mp_count),
        out_shape=(out, out),
        in_specs=[smem, smem] + [vmem] * 6,
        out_specs=(vmem, vmem),
        scratch_shapes=[
            pltpu.VMEM((8, total), jnp.float32),
            pltpu.VMEM((1, total), jnp.float32),
            pltpu.VMEM((1, total), jnp.float32),
        ],
        compiler_params=pltpu.CompilerParams(vmem_limit_bytes=48 * 1024 * 1024),
    )(
        jnp.reshape(mp_index, (1,)).astype(jnp.int32),
        jnp.reshape(logit_scale, (1,)),
        all_clips,
        all_caps,
        own_raw[0],
        own_raw[1],
        videos[None, :],
        videos[:, None],
    )


def joined_lse(left, right):
    top = jnp.maximum(left, right)
    return top + jnp.log2(jnp.exp2(left - top) + jnp.exp2(right - top))


def lane_vector(column):
    return jnp.transpose(jnp.broadcast_to(column, (column.shape[0], 128)))[0:1, :]


def add_terms(stat, scores, axis):
    top = jnp.max(scores, axis=axis, keepdims=True)
    if stat is not None:
        top = jnp.maximum(stat[0], top)
    terms = jnp.sum(jnp.exp2(scores - top), axis=axis, keepdims=True)
    if stat is not None:
        terms = terms + stat[1] * jnp.exp2(stat[0] - top)
    return top, terms


def stage_kernel(*refs, piece_count, places, old_count, mp_count, final):
    mp_ref, scale_ref, row_videos_ref, column_videos_ref = refs[:4]
    refs = refs[4:]
    piece_refs, refs = refs[:piece_count], refs[piece_count:]
    old_refs, refs = refs[: 2 * old_count], refs[2 * old_count :]
    old = [(old_refs[2 * k], old_refs[2 * k + 1]) for k in range(old_count)]
    if old_count:
        row_old_ref, col_old_ref, own_ref = refs[:3]
        refs = refs[3:]
    if final:
        d_clips_ref, d_caps_ref, clips_ref, caps_ref = refs
    elif old_count:
        clips_ref, caps_ref, row_ref, col_ref = refs
    else:
        clips_ref, caps_ref, row_ref, col_ref, own_ref = refs
    fresh, width = clips_ref.shape
    rows = fresh // len(places)
    chunk = width // mp_count
    start = sum(clips.shape[0] for clips, _ in old)
    total = start + fresh
    mp_index = mp_ref[0]
    scale = scale_ref[0]
    scale2 = scale * log2_e

    for position, place in enumerate(places):
        span = pl.ds(position * rows, rows)
        for kind in range(2):
            raw = [
                piece_refs[piece][kind, first * chunk : (first + count) * chunk, :]
                for piece, first, count in place
            ]
            raw = jnp.concatenate(raw, axis=0)
            if position == 0 and not old_count:
                own_ref[kind] = jnp.transpose(raw)
            wide = raw.astype(jnp.float32)
            inverse = 1.0 / jnp.sqrt(jnp.sum(wide * wide, axis=0, keepdims=True) + epsilon)
            unit = (wide * inverse).astype(jnp.bfloat16)
            if kind == 0:
                clips_ref[span, :] = jnp.transpose(unit)
            else:
                caps_ref[:, span] = unit

    def tile(clip_tile, row_first, caps, col_first):
        size = (clip_tile.shape[0], caps.shape[1])
        scores = scale2 * jnp.dot(clip_tile, caps[...], preferred_element_type=jnp.float32)
        banned = (
            column_videos_ref[row_first : row_first + size[0], :]
            == row_videos_ref[:, col_first : col_first + size[1]]
        )
        if col_first <= row_first < col_first + size[1]:
            distance = lax.broadcasted_iota(jnp.int32, size, 1) - lax.broadcasted_iota(jnp.int32, size, 0)
            banned = banned & (distance != row_first - col_first)
        return jnp.where(banned, negative_fill, scores)

    row_tile = min(2 * rows, fresh)
    row_parts = []
    col_new = None
    at = 0
    for clips, _ in old:
        for first in range(0, clips.shape[0], row_tile):
            scores = tile(clips[first : first + row_tile, :], at + first, caps_ref, start)
            top, terms = add_terms(None, scores, 1)
            col_new = add_terms(col_new, scores, 0)
            row_parts.append(lane_vector(top + jnp.log2(terms)))
        at += clips.shape[0]
    col_olds = [None] * old_count
    row_news = []
    for first in range(0, fresh, row_tile):
        stat = None
        clip_tile = clips_ref[first : first + row_tile, :]
        at = 0
        for k, (clips, caps) in enumerate(old):
            scores = tile(clip_tile, start + first, caps, at)
            stat = add_terms(stat, scores, 1)
            col_olds[k] = add_terms(col_olds[k], scores, 0)
            at += clips.shape[0]
        scores = tile(clip_tile, start + first, caps_ref, start)
        top, terms = add_terms(stat, scores, 1)
        col_new = add_terms(col_new, scores, 0)
        row_news.append(lane_vector(top + jnp.log2(terms)))
    row_lse = row_news
    col_lse = [col_new[0] + jnp.log2(col_new[1])]
    if old_count:
        old_part = jnp.concatenate(row_parts, axis=1)
        row_lse = [joined_lse(row_old_ref[...], old_part)] + row_lse
        old_part = jnp.concatenate([top + jnp.log2(terms) for top, terms in col_olds], axis=1)
        col_lse = [joined_lse(col_old_ref[...], old_part)] + col_lse
    row_lse = jnp.concatenate(row_lse, axis=1)
    col_lse = jnp.concatenate(col_lse, axis=1)
    if not final:
        row_ref[...] = row_lse
        col_ref[...] = col_lse
        return

    own = d_clips_ref.shape[0]
    every = old + [(clips_ref, caps_ref)]
    own_first = pl.multiple_of(mp_index * own, own)
    own_rows = pl.ds(own_first, own)
    clip_float, clip_length = unit_rows(own_ref[0, own_rows, :])
    cap_float, cap_length = unit_rows(own_ref[1, own_rows, :])
    clip_unit = old[0][0][own_rows, :]
    cap_unit = cap_float.astype(jnp.bfloat16)
    same = column_videos_ref[own_rows, :] == row_videos_ref[...]
    distance = lax.broadcasted_iota(jnp.int32, (own, total), 1) - lax.broadcasted_iota(
        jnp.int32, (own, total), 0
    )
    blocked = same & (distance != own_first)
    same = same.astype(jnp.bfloat16)
    last = (((1,), (1,)), ((), ()))

    def strip(products, other_lse):
        scores = jnp.where(blocked, negative_fill, scale2 * jnp.concatenate(products, axis=1))
        top, terms = add_terms(None, scores, 1)
        weights = 0.5 * (jnp.exp2(scores - (top + jnp.log2(terms))) + jnp.exp2(scores - other_lse))
        return jnp.concatenate([weights.astype(jnp.bfloat16), same], axis=0)

    def summed(weights, multiply):
        at, result = 0, None
        for clips, caps in every:
            part = multiply(weights[:, at : at + clips.shape[0]], clips, caps)
            result = part if result is None else result + part
            at += clips.shape[0]
        return result[:own], result[own:]

    clip_products = [
        jnp.dot(clip_unit, caps[...], preferred_element_type=jnp.float32) for _, caps in every
    ]
    cap_products = [
        lax.dot_general(cap_unit, clips[...], last, preferred_element_type=jnp.float32)
        for clips, _ in every
    ]
    clip_acc, caption_pool = summed(
        strip(clip_products, col_lse),
        lambda w, clips, caps: lax.dot_general(w, caps[...], last, preferred_element_type=jnp.float32),
    )
    cap_acc, pooled = summed(
        strip(cap_products, row_lse),
        lambda w, clips, caps: jnp.dot(w, clips[...], preferred_element_type=jnp.float32),
    )
    pool_length = jnp.sqrt(jnp.sum(pooled * pooled, axis=1, keepdims=True) + epsilon)
    pool_unit = pooled / pool_length
    projected = caption_pool - pool_unit * jnp.sum(pool_unit * caption_pool, axis=1, keepdims=True)
    clip_grad = (
        scale * clip_acc
        - 0.5 * scale * cap_unit.astype(jnp.float32)
        - 0.5 * scale * projected / pool_length
    )
    cap_grad = scale * cap_acc - 0.5 * scale * clip_unit.astype(jnp.float32) - 0.5 * scale * pool_unit

    def finish(unit, length, grad, out_ref):
        result = (grad - unit * jnp.sum(unit * grad, axis=1, keepdims=True)) / length
        for index in range(mp_count):

            @pl.when(mp_index == index)
            def _():
                out_ref[...] = jnp.concatenate(
                    [result[:, (q ^ index) * chunk : ((q ^ index) + 1) * chunk] for q in range(mp_count)],
                    axis=1,
                )

    finish(clip_float, clip_length, clip_grad, d_clips_ref)
    finish(cap_float, cap_length, cap_grad, d_caps_ref)


def resident_body(clips, captions, video_id, logit_scale):
    dp_count = lax.axis_size("dp")
    mp_count = lax.axis_size("mp")
    row_count = clips.shape[0]
    own = row_count // mp_count
    width = clips.shape[1] * mp_count
    dp_index = lax.axis_index("dp")
    mp_index = lax.axis_index("mp")
    even, odd = gather_orders(dp_count)

    def along(step, block):
        route = [(i, i ^ (odd[step] if i & 1 else even[step])) for i in range(dp_count)]
        return lax.ppermute(block, "dp", route)

    def across(block):
        return lax.ppermute(block, "dp", [(i, i ^ 1) for i in range(dp_count)])

    reached = [(0, 0), (even[0], odd[0]), (even[1], odd[1]), (even[0] ^ even[1], odd[0] ^ odd[1])]
    crossed = [(b ^ 1, a ^ 1) for a, b in reached]
    ordered = [reached[0], crossed[0], reached[1], reached[2], crossed[1], crossed[2], reached[3], crossed[3]]
    videos = []
    for even_offset, odd_offset in ordered:
        block = dp_index ^ jnp.where(dp_index & 1, odd_offset, even_offset)
        videos.append(lax.dynamic_slice_in_dim(video_id, block * row_count, row_count, 0))
    videos = jnp.concatenate(videos)
    common = (
        jnp.reshape(mp_index, (1,)).astype(jnp.int32),
        jnp.reshape(logit_scale, (1,)),
        videos[None, :],
        videos[:, None],
    )
    vmem = pl.BlockSpec(memory_space=pltpu.VMEM)
    smem = pl.BlockSpec(memory_space=pltpu.SMEM)

    def stage(pieces, places, old, carried, final=False):
        fresh = len(places) * row_count
        total = fresh + sum(clips.shape[0] for clips, _ in old)
        units = [((fresh, width), jnp.bfloat16), ((width, fresh), jnp.bfloat16)]
        scratch = []
        if final:
            outs = [((own, width), jnp.float32)] * 2
            scratch = [pltpu.VMEM(*unit) for unit in units]
        else:
            outs = units + [((1, total), jnp.float32)] * 2
            if not old:
                outs = outs + [((2, row_count, width), jnp.bfloat16)]
        operands = [*common, *pieces, *[unit for pair in old for unit in pair], *carried]
        score_count = (2 * total - fresh) * fresh
        return pl.pallas_call(
            functools.partial(
                stage_kernel,
                piece_count=len(pieces),
                places=places,
                old_count=len(old),
                mp_count=mp_count,
                final=final,
            ),
            out_shape=[jax.ShapeDtypeStruct(*out) for out in outs],
            in_specs=[smem, smem] + [vmem] * (len(operands) - 2),
            out_specs=[vmem] * len(outs),
            scratch_shapes=scratch,
            cost_estimate=pl.CostEstimate(
                flops=1, bytes_accessed=1, transcendentals=0
            ),
            compiler_params=pltpu.CompilerParams(vmem_limit_bytes=32 * 1024 * 1024),
        )(*operands)

    def after(value, other):
        return lax.optimization_barrier((value, other))[0]

    early = mp_count // 2
    late = mp_count - early
    chunk = jnp.stack([clips.T, captions.T])
    arrived = [
        lax.ppermute(chunk, "mp", [(i, i ^ k) for i in range(mp_count)]) for k in range(1, mp_count)
    ]
    lead = jnp.concatenate([chunk] + arrived[: early - 1], axis=1)
    lead_first = along(0, lead)
    lead_second = along(1, lead)
    lead_pair_other = across(after(jnp.concatenate([lead, lead_first], axis=1), lead_second))
    arrived[-1] = after(arrived[-1], (lead_first, lead_second, lead_pair_other))
    rest = jnp.concatenate(arrived[early - 1 :], axis=1)
    rest_first = along(0, rest)
    clips_a, caps_a, row_a, col_a, own_raw = stage(
        [lead, rest], [[(0, 0, early), (1, 0, late)]], [], []
    )
    rest_second = along(1, after(rest, row_a))
    third = along(1, jnp.concatenate([lead_first, rest_first], axis=1))
    rest_other = across(after(rest, rest_first))
    lead_second_other = across(after(lead_second, rest_first))
    clips_b, caps_b, row_b, col_b = stage(
        [
            lead_pair_other,
            rest_other,
            lead_first,
            rest_first,
            lead_second,
            rest_second,
            across(rest_first),
            lead_second_other,
            across(rest_second),
        ],
        [
            [(0, 0, early), (1, 0, late)],
            [(2, 0, early), (3, 0, late)],
            [(4, 0, early), (5, 0, late)],
            [(0, early, early), (6, 0, late)],
            [(7, 0, early), (8, 0, late)],
        ],
        [(clips_a, caps_a)],
        [row_a, col_a, own_raw],
    )
    third_other = across(after(third, row_b))
    clips_c, caps_c, row_c, col_c = stage(
        [third],
        [[(0, 0, mp_count)]],
        [(clips_a, caps_a), (clips_b, caps_b)],
        [row_b, col_b, own_raw],
    )
    return tuple(
        stage(
            [third_other],
            [[(0, 0, mp_count)]],
            [(clips_a, caps_a), (clips_b, caps_b), (clips_c, caps_c)],
            [row_c, col_c, own_raw],
            final=True,
        )
    )


def body(clips, captions, video_id, logit_scale):
    dp_count, mp_count = lax.axis_size("dp"), lax.axis_size("mp")
    gathered_bytes = 2 * clips.size * clips.dtype.itemsize * dp_count * mp_count
    if len(gather_orders(dp_count)[0]) == 2 and gathered_bytes <= resident_limit:
        return resident_body(clips, captions, video_id, logit_scale)
    return streamed_body(clips, captions, video_id, logit_scale)


def solution(mesh):
    in_specs = (P("dp", "mp"), P("dp", "mp"), P(), P())
    out_specs = (P(("dp", "mp"), None), P(("dp", "mp"), None))
    return jax.shard_map(body, mesh=mesh, in_specs=in_specs, out_specs=out_specs, check_vma=False)
```

```python
import functools
import math

import jax
import jax.numpy as jnp
from jax import lax
from jax.experimental import pallas as pl
from jax.experimental.pallas import tpu as pltpu
from jax.sharding import PartitionSpec as P

epsilon = 1e-06
negative_fill = -1e30
log2_e = math.log2(math.e)
resident_limit = 8 * 1024 * 1024


def unit_rows(values):
    widened = values.astype(jnp.float32)
    length = jnp.sqrt(jnp.sum(widened * widened, axis=-1, keepdims=True) + epsilon)
    return widened / length, length


def gather_columns(block):
    count = lax.axis_size("mp")
    chunks = [block]
    for k in range(1, count):
        chunks.append(lax.ppermute(block, "mp", [(i, i ^ k) for i in range(count)]))
    return jnp.concatenate(chunks, axis=-1)


def gather_orders(dp_count):
    bits = [1 << k for k in range(1, dp_count.bit_length() - 1)]
    return bits, bits[1:] + bits[:1]


def gather_blocks(block):
    dp_count = lax.axis_size("dp")
    even, odd = gather_orders(dp_count)
    held = block[None]
    for bit_even, bit_odd in zip(even, odd):
        route = [(i, i ^ (bit_odd if i & 1 else bit_even)) for i in range(dp_count)]
        held = jnp.concatenate([held, lax.ppermute(held, "dp", route)], axis=0)
    other = lax.ppermute(held, "dp", [(i, i ^ 1) for i in range(dp_count)])
    return jnp.concatenate([held, other], axis=0)


def block_offsets(dp_count):
    even, odd = gather_orders(dp_count)
    own = []
    for order in (even, odd):
        held = [0]
        for bit in order:
            held = held + [h ^ bit for h in held]
        own.append(held)
    return [own[0] + [h ^ 1 for h in own[1]], own[1] + [h ^ 1 for h in own[0]]]


def streamed_kernel(
    mp_ref,
    scale_ref,
    clips_ref,
    caps_ref,
    own_clips_ref,
    own_caps_ref,
    row_videos_ref,
    column_videos_ref,
    d_clips_ref,
    d_caps_ref,
    row_lse_ref,
    col_max_ref,
    col_sum_ref,
    *,
    mp_count,
):
    total = clips_ref.shape[0]
    own = own_clips_ref.shape[0]
    width = clips_ref.shape[1]
    row_tile = min(256, total)
    col_tile = min(1024, total)
    mp_index = mp_ref[0]
    scale = scale_ref[0]
    scale2 = scale * log2_e
    contract_last = (((1,), (1,)), ((), ()))

    col_max_ref[...] = jnp.full(col_max_ref.shape, negative_fill, jnp.float32)
    col_sum_ref[...] = jnp.zeros(col_sum_ref.shape, jnp.float32)

    def one_tile(row_first, col_first, carry):
        row_max, row_sum = carry
        rows = pl.ds(row_first, row_tile)
        cols = pl.ds(col_first, col_tile)
        scores = scale2 * lax.dot_general(
            clips_ref[rows, :], caps_ref[cols, :], contract_last, preferred_element_type=jnp.float32
        )
        same = column_videos_ref[rows, :] == row_videos_ref[:, cols]
        distance = lax.broadcasted_iota(jnp.int32, scores.shape, 0) - lax.broadcasted_iota(
            jnp.int32, scores.shape, 1
        )
        off_diagonal = distance != col_first - row_first
        scores = jnp.where(same & off_diagonal, negative_fill, scores)
        new_row = jnp.maximum(row_max, jnp.max(scores, axis=1, keepdims=True))
        row_sum = row_sum * jnp.exp2(row_max - new_row) + jnp.sum(
            jnp.exp2(scores - new_row), axis=1, keepdims=True
        )
        old_col = col_max_ref[:, cols]
        new_col = jnp.maximum(old_col, jnp.max(scores, axis=0, keepdims=True))
        col_sum_ref[:, cols] = col_sum_ref[:, cols] * jnp.exp2(old_col - new_col) + jnp.sum(
            jnp.exp2(scores - new_col), axis=0, keepdims=True
        )
        col_max_ref[:, cols] = new_col
        return new_row, row_sum

    def one_row_block(block):
        row_first = block * row_tile
        if not isinstance(block, int):
            row_first = pl.multiple_of(row_first, row_tile)
        carry = (
            jnp.full((row_tile, 1), negative_fill, jnp.float32),
            jnp.zeros((row_tile, 1), jnp.float32),
        )
        if total == col_tile:
            row_max, row_sum = one_tile(row_first, 0, carry)
        else:
            row_max, row_sum = lax.fori_loop(
                0,
                total // col_tile,
                lambda c, so_far: one_tile(row_first, pl.multiple_of(c * col_tile, col_tile), so_far),
                carry,
            )
        lse = row_max + jnp.log2(row_sum)
        row_lse_ref[:, pl.ds(row_first, row_tile)] = jnp.transpose(
            jnp.broadcast_to(lse, (row_tile, 128))
        )[:8, :]

    if total // row_tile <= 8:
        for block in range(total // row_tile):
            one_row_block(block)
    else:
        pl.loop(0, total // row_tile)(one_row_block)

    col_lse = col_max_ref[...] + jnp.log2(col_sum_ref[...])
    row_lse = row_lse_ref[0:1, :]

    own_first = pl.multiple_of(mp_index * own, own)
    own_rows = pl.ds(own_first, own)
    clip_unit = clips_ref[own_rows, :]
    cap_unit = caps_ref[own_rows, :]
    same = column_videos_ref[own_rows, :] == row_videos_ref[...]
    distance = lax.broadcasted_iota(jnp.int32, (own, total), 1) - lax.broadcasted_iota(
        jnp.int32, (own, total), 0
    )
    blocked = same & (distance != own_first)
    same = same.astype(jnp.bfloat16)

    def strip(unit, others_ref, own_lse_all, other_lse):
        scores = scale2 * lax.dot_general(
            unit, others_ref[...], contract_last, preferred_element_type=jnp.float32
        )
        scores = jnp.where(blocked, negative_fill, scores)
        top = jnp.max(scores, axis=1, keepdims=True)
        own_lse = top + jnp.log2(jnp.sum(jnp.exp2(scores - top), axis=1, keepdims=True))
        weights = 0.5 * (jnp.exp2(scores - own_lse) + jnp.exp2(scores - other_lse))
        weights = weights.astype(jnp.bfloat16)
        both = jnp.concatenate([weights, same], axis=0)
        sums = jnp.dot(both, others_ref[...], preferred_element_type=jnp.float32)
        return sums[:own], sums[own:]

    clip_acc, caption_pool = strip(clip_unit, caps_ref, None, col_lse)
    cap_acc, pooled = strip(cap_unit, clips_ref, None, row_lse)
    clip_unit = clip_unit.astype(jnp.float32)
    cap_unit = cap_unit.astype(jnp.float32)
    pool_length = jnp.sqrt(jnp.sum(pooled * pooled, axis=1, keepdims=True) + epsilon)
    pool_unit = pooled / pool_length
    projected = caption_pool - pool_unit * jnp.sum(pool_unit * caption_pool, axis=1, keepdims=True)
    clip_grad = scale * clip_acc - 0.5 * scale * cap_unit - 0.5 * scale * projected / pool_length
    cap_grad = scale * cap_acc - 0.5 * scale * clip_unit - 0.5 * scale * pool_unit

    def finish(values_ref, grad, out_ref):
        unit, length = unit_rows(values_ref[...])
        result = (grad - unit * jnp.sum(unit * grad, axis=1, keepdims=True)) / length
        chunk = width // mp_count
        for index in range(mp_count):

            @pl.when(mp_index == index)
            def _():
                out_ref[...] = jnp.concatenate(
                    [result[:, (q ^ index) * chunk : ((q ^ index) + 1) * chunk] for q in range(mp_count)],
                    axis=1,
                )

    finish(own_clips_ref, clip_grad, d_clips_ref)
    finish(own_caps_ref, cap_grad, d_caps_ref)


def streamed_body(clips, captions, video_id, logit_scale):
    dp_count = lax.axis_size("dp")
    mp_count = lax.axis_size("mp")
    row_count = clips.shape[0]
    own = row_count // mp_count
    width = clips.shape[1] * mp_count
    total = row_count * dp_count
    dp_index = lax.axis_index("dp")
    mp_index = lax.axis_index("mp")

    full = gather_columns(jnp.stack([clips, captions]))
    unit = unit_rows(full)[0].astype(jnp.bfloat16)
    own_raw = lax.dynamic_slice_in_dim(full, mp_index * own, own, 1)
    every = gather_blocks(unit)
    all_clips = every[:, 0].reshape(total, width)
    all_caps = every[:, 1].reshape(total, width)

    offsets = block_offsets(dp_count)
    videos = []
    for even, odd in zip(*offsets):
        block = dp_index ^ jnp.where(dp_index & 1, odd, even)
        videos.append(lax.dynamic_slice_in_dim(video_id, block * row_count, row_count, 0))
    videos = jnp.concatenate(videos)

    vmem = pl.BlockSpec(memory_space=pltpu.VMEM)
    smem = pl.BlockSpec(memory_space=pltpu.SMEM)
    out = jax.ShapeDtypeStruct((own, width), jnp.float32)
    return pl.pallas_call(
        functools.partial(streamed_kernel, mp_count=mp_count),
        out_shape=(out, out),
        in_specs=[smem, smem] + [vmem] * 6,
        out_specs=(vmem, vmem),
        scratch_shapes=[
            pltpu.VMEM((8, total), jnp.float32),
            pltpu.VMEM((1, total), jnp.float32),
            pltpu.VMEM((1, total), jnp.float32),
        ],
        compiler_params=pltpu.CompilerParams(vmem_limit_bytes=48 * 1024 * 1024),
    )(
        jnp.reshape(mp_index, (1,)).astype(jnp.int32),
        jnp.reshape(logit_scale, (1,)),
        all_clips,
        all_caps,
        own_raw[0],
        own_raw[1],
        videos[None, :],
        videos[:, None],
    )


def joined_lse(left, right):
    top = jnp.maximum(left, right)
    return top + jnp.log2(jnp.exp2(left - top) + jnp.exp2(right - top))


def lane_vector(column):
    return jnp.transpose(jnp.broadcast_to(column, (column.shape[0], 128)))[0:1, :]


def add_terms(stat, scores, axis):
    top = jnp.max(scores, axis=axis, keepdims=True)
    if stat is not None:
        top = jnp.maximum(stat[0], top)
    terms = jnp.sum(jnp.exp2(scores - top), axis=axis, keepdims=True)
    if stat is not None:
        terms = terms + stat[1] * jnp.exp2(stat[0] - top)
    return top, terms


def lse_of(stat):
    return stat[0] + jnp.log2(stat[1])


def stage_kernel(*refs, piece_count, places, old_count, mp_count, final):
    refs = list(refs)

    def take(count):
        taken = refs[:count]
        del refs[:count]
        return taken

    mp_ref, scale_ref, row_videos_ref, column_videos_ref = take(4)
    piece_refs = take(piece_count)
    old = [take(2) for _ in range(old_count)]
    if old_count:
        row_old_ref, col_old_ref, own_ref, own_caps_ref = take(4)
    if final:
        strip_refs = [take(2) for _ in range(old_count)]
        d_clips_ref, d_caps_ref = take(2)
    clips_ref, caps_ref = take(2)
    if not final:
        row_ref, col_ref = take(2)
    clip_strip_ref, cap_strip_ref = take(2)
    if not old_count:
        own_ref, own_caps_ref = take(2)
    if refs:
        (caps_rows_ref,) = take(1)
    fresh, width = clips_ref.shape
    rows = fresh // len(places)
    chunk = width // mp_count
    start = sum(clips.shape[0] for clips, _ in old)
    wide_old = old_count > 1 or start > fresh
    mp_index = mp_ref[0]
    scale = scale_ref[0]
    scale2 = scale * log2_e
    last = (((1,), (1,)), ((), ()))

    for position, place in enumerate(places):
        span = pl.ds(position * rows, rows)
        for kind in range(2):
            raw = [
                piece_refs[piece][kind, first * chunk : (first + count) * chunk, :]
                for piece, first, count in place
            ]
            raw = jnp.concatenate(raw, axis=0)
            wide = raw.astype(jnp.float32)
            inverse = 1.0 / jnp.sqrt(jnp.sum(wide * wide, axis=0, keepdims=True) + epsilon)
            unit = (wide * inverse).astype(jnp.bfloat16)
            if kind == 0:
                clips_ref[span, :] = jnp.transpose(unit)
            else:
                caps_ref[:, span] = unit
                if wide_old:
                    caps_rows_ref[span, :] = jnp.transpose(unit)
            if not old_count:
                own_ref[kind] = jnp.transpose(raw)
                if kind == 1:
                    own_caps_ref[...] = jnp.transpose(unit)

    def masked(products, row_first, col_first):
        size = products.shape
        banned = (
            column_videos_ref[row_first : row_first + size[0], :]
            == row_videos_ref[:, col_first : col_first + size[1]]
        )
        if col_first <= row_first < col_first + size[1]:
            distance = lax.broadcasted_iota(jnp.int32, size, 1) - lax.broadcasted_iota(jnp.int32, size, 0)
            banned = banned & (distance != row_first - col_first)
        return jnp.where(banned, negative_fill, scale2 * products)

    def plain(left, right):
        return jnp.dot(left, right, preferred_element_type=jnp.float32)

    def crossed(left, right):
        return lax.dot_general(left, right, last, preferred_element_type=jnp.float32)

    clip_old, cap_old, clip_new, cap_new = [], [], [], []
    clip_stat, cap_stat, cap_lanes = None, None, None
    if wide_old:
        at = 0
        for index, (clips, caps) in enumerate(old):
            scores = masked(crossed(caps_rows_ref[...], clips[...]), start, at)
            clip_old.append(lse_of(add_terms(None, scores, 0)))
            cap_stat = add_terms(cap_stat, scores, 1)
            if index == 0:
                clip_strip_ref[...] = jnp.transpose(scores)
            scores = masked(plain(clips_ref[...], caps[...]), start, at)
            cap_old.append(lse_of(add_terms(None, scores, 0)))
            clip_stat = add_terms(clip_stat, scores, 1)
            if index == 0:
                cap_strip_ref[...] = jnp.transpose(scores)
            at += clips.shape[0]
        cap_new.append(lane_vector(lse_of(cap_stat)))
    elif old:
        scores = masked(plain(old[0][0][...], caps_ref[...]), 0, start)
        clip_strip_ref[...] = scores
        clip_old.append(lane_vector(lse_of(add_terms(None, scores, 1))))
        cap_lanes = add_terms(None, scores, 0)
        scores = masked(crossed(own_caps_ref[...], clips_ref[...]), 0, start)
        cap_strip_ref[...] = scores
        cap_old.append(lane_vector(lse_of(add_terms(None, scores, 1))))
        clip_new.append(lse_of(add_terms(None, scores, 0)))
    parts = []
    for first in range(0, fresh, rows):
        scores = masked(plain(clips_ref[first : first + rows, :], caps_ref[...]), start + first, start)
        stat = clip_stat and tuple(part[first : first + rows] for part in clip_stat)
        parts.append(lane_vector(lse_of(add_terms(stat, scores, 1))))
        cap_lanes = add_terms(cap_lanes, scores, 0)
        if not old:
            clip_strip_ref[...] = scores
            cap_strip_ref[...] = jnp.transpose(scores)
    clip_new.append(jnp.concatenate(parts, axis=1))
    cap_new.append(lse_of(cap_lanes))

    def joined(old_ref, old_parts, new_parts):
        new = functools.reduce(joined_lse, new_parts)
        if not old:
            return new
        return jnp.concatenate([joined_lse(old_ref[...], jnp.concatenate(old_parts, axis=1)), new], axis=1)

    row_lse = joined(row_old_ref if old else None, clip_old, clip_new)
    col_lse = joined(col_old_ref if old else None, cap_old, cap_new)
    if not final:
        row_ref[...] = row_lse
        col_ref[...] = col_lse
        return

    own = d_clips_ref.shape[0]
    every = old + [(clips_ref, caps_ref)]
    own_first = pl.multiple_of(mp_index * own, own)
    own_rows = pl.ds(own_first, own)
    clip_float, clip_length = unit_rows(own_ref[0, own_rows, :])
    cap_float, cap_length = unit_rows(own_ref[1, own_rows, :])
    clip_unit = old[0][0][own_rows, :]
    cap_unit = cap_float.astype(jnp.bfloat16)
    same = (column_videos_ref[own_rows, :] == row_videos_ref[...]).astype(jnp.bfloat16)
    strip_refs = strip_refs + [(clip_strip_ref, cap_strip_ref)]

    def strip(kind, other_lse):
        scores = jnp.concatenate([pair[kind][own_rows, :] for pair in strip_refs], axis=1)
        own_lse = lse_of(add_terms(None, scores, 1))
        weights = 0.5 * (jnp.exp2(scores - own_lse) + jnp.exp2(scores - other_lse))
        return jnp.concatenate([weights.astype(jnp.bfloat16), same], axis=0)

    def summed(weights, multiply):
        at, result = 0, None
        for clips, caps in every:
            part = multiply(weights[:, at : at + clips.shape[0]], clips, caps)
            result = part if result is None else result + part
            at += clips.shape[0]
        return result[:own], result[own:]

    clip_acc, caption_pool = summed(strip(0, col_lse), lambda w, clips, caps: crossed(w, caps[...]))
    cap_acc, pooled = summed(strip(1, row_lse), lambda w, clips, caps: plain(w, clips[...]))
    pool_length = jnp.sqrt(jnp.sum(pooled * pooled, axis=1, keepdims=True) + epsilon)
    pool_unit = pooled / pool_length
    projected = caption_pool - pool_unit * jnp.sum(pool_unit * caption_pool, axis=1, keepdims=True)
    clip_grad = (
        scale * clip_acc
        - 0.5 * scale * cap_unit.astype(jnp.float32)
        - 0.5 * scale * projected / pool_length
    )
    cap_grad = scale * cap_acc - 0.5 * scale * clip_unit.astype(jnp.float32) - 0.5 * scale * pool_unit

    def finish(unit, length, grad, out_ref):
        result = (grad - unit * jnp.sum(unit * grad, axis=1, keepdims=True)) / length
        for index in range(mp_count):

            @pl.when(mp_index == index)
            def _():
                out_ref[...] = jnp.concatenate(
                    [result[:, (q ^ index) * chunk : ((q ^ index) + 1) * chunk] for q in range(mp_count)],
                    axis=1,
                )

    finish(clip_float, clip_length, clip_grad, d_clips_ref)
    finish(cap_float, cap_length, cap_grad, d_caps_ref)


def resident_body(clips, captions, video_id, logit_scale):
    dp_count = lax.axis_size("dp")
    mp_count = lax.axis_size("mp")
    row_count = clips.shape[0]
    own = row_count // mp_count
    width = clips.shape[1] * mp_count
    dp_index = lax.axis_index("dp")
    mp_index = lax.axis_index("mp")
    even, odd = gather_orders(dp_count)

    def along(step, block):
        route = [(i, i ^ (odd[step] if i & 1 else even[step])) for i in range(dp_count)]
        return lax.ppermute(block, "dp", route)

    def across(block):
        return lax.ppermute(block, "dp", [(i, i ^ 1) for i in range(dp_count)])

    reached = [(0, 0), (even[0], odd[0]), (even[1], odd[1]), (even[0] ^ even[1], odd[0] ^ odd[1])]
    crossed = [(b ^ 1, a ^ 1) for a, b in reached]
    ordered = [reached[0], crossed[0], reached[1], reached[2], crossed[1], crossed[2], reached[3], crossed[3]]
    videos = []
    for even_offset, odd_offset in ordered:
        block = dp_index ^ jnp.where(dp_index & 1, odd_offset, even_offset)
        videos.append(lax.dynamic_slice_in_dim(video_id, block * row_count, row_count, 0))
    videos = jnp.concatenate(videos)
    common = (
        jnp.reshape(mp_index, (1,)).astype(jnp.int32),
        jnp.reshape(logit_scale, (1,)),
        videos[None, :],
        videos[:, None],
    )
    vmem = pl.BlockSpec(memory_space=pltpu.VMEM)
    smem = pl.BlockSpec(memory_space=pltpu.SMEM)

    def stage(pieces, places, old, carried, final=False, cost=1):
        fresh = len(places) * row_count
        total = fresh + sum(clips.shape[0] for clips, _ in old)
        units = [((fresh, width), jnp.bfloat16), ((width, fresh), jnp.bfloat16)]
        strips = [((row_count, fresh), jnp.float32)] * 2
        scratch = [((fresh, width), jnp.bfloat16)] if len(old) > 1 or total > 2 * fresh else []
        if final:
            outs = [((own, width), jnp.float32)] * 2
            scratch = units + strips + scratch
        else:
            outs = units + [((1, total), jnp.float32)] * 2 + strips
            if not old:
                outs = outs + [((2, row_count, width), jnp.bfloat16), ((row_count, width), jnp.bfloat16)]
        scratch = [pltpu.VMEM(*entry) for entry in scratch]
        operands = [*common, *pieces, *[unit for pair in old for unit in pair], *carried]
        return pl.pallas_call(
            functools.partial(
                stage_kernel,
                piece_count=len(pieces),
                places=places,
                old_count=len(old),
                mp_count=mp_count,
                final=final,
            ),
            out_shape=[jax.ShapeDtypeStruct(*out) for out in outs],
            in_specs=[smem, smem] + [vmem] * (len(operands) - 2),
            out_specs=[vmem] * len(outs),
            scratch_shapes=scratch,
            cost_estimate=pl.CostEstimate(
                flops=cost, bytes_accessed=1, transcendentals=0
            ),
            compiler_params=pltpu.CompilerParams(vmem_limit_bytes=32 * 1024 * 1024),
        )(*operands)

    def after(value, other):
        return lax.optimization_barrier((value, other))[0]

    early = mp_count // 2
    late = mp_count - early

    chunk = jnp.stack([clips.T, captions.T])
    arrived = [
        lax.ppermute(chunk, "mp", [(i, i ^ k) for i in range(mp_count)]) for k in range(1, mp_count)
    ]
    lead = jnp.concatenate([chunk] + arrived[: early - 1], axis=1)
    lead_first = along(0, lead)
    lead_second = along(1, lead)
    lead_other = across(after(lead, lead_second))
    arrived[-1] = after(arrived[-1], lead_other)
    rest = jnp.concatenate(arrived[early - 1 :], axis=1)
    rest_first = along(0, rest)
    rest_other = across(rest)
    whole = [(0, 0, early), (1, 0, late)]
    clips_a, caps_a, row_a, col_a, *strips_a, own_raw, own_caps = stage([lead, rest], [whole], [], [], cost=10**8)
    rest_second = along(1, after(rest, row_a))
    third = along(1, jnp.concatenate([lead_first, rest_first], axis=1))

    pairs = [
        (lead_other, rest_other),
        (lead_first, rest_first),
        (lead_second, rest_second),
        (across(after(lead_first, lead_second)), across(after(rest_first, rest_second))),
        (across(lead_second), across(rest_second)),
    ]
    clips_b, caps_b, row_b, col_b, *strips_b = stage(
        [piece for pair in pairs for piece in pair],
        [[(2 * k + piece, first, count) for piece, first, count in whole] for k in range(len(pairs))],
        [(clips_a, caps_a)],
        [row_a, col_a, own_raw, own_caps],
    )
    third_other = across(after(third, row_b))
    clips_c, caps_c, row_c, col_c, *strips_c = stage(
        [third],
        [[(0, 0, mp_count)]],
        [(clips_a, caps_a), (clips_b, caps_b)],
        [row_b, col_b, own_raw, own_caps],
    )
    return tuple(
        stage(
            [third_other],
            [[(0, 0, mp_count)]],
            [(clips_a, caps_a), (clips_b, caps_b), (clips_c, caps_c)],
            [row_c, col_c, own_raw, own_caps, *strips_a, *strips_b, *strips_c],
            final=True,
        )
    )


def body(clips, captions, video_id, logit_scale):
    dp_count, mp_count = lax.axis_size("dp"), lax.axis_size("mp")
    gathered_bytes = 2 * clips.size * clips.dtype.itemsize * dp_count * mp_count
    if len(gather_orders(dp_count)[0]) == 2 and gathered_bytes <= resident_limit:
        return resident_body(clips, captions, video_id, logit_scale)
    return streamed_body(clips, captions, video_id, logit_scale)


def solution(mesh):
    in_specs = (P("dp", "mp"), P("dp", "mp"), P(), P())
    out_specs = (P(("dp", "mp"), None), P(("dp", "mp"), None))
    return jax.shard_map(body, mesh=mesh, in_specs=in_specs, out_specs=out_specs, check_vma=False)
```

```python
import functools
import math

import jax
import jax.numpy as jnp
from jax import lax
from jax.experimental import pallas as pl
from jax.experimental.pallas import tpu as pltpu
from jax.sharding import PartitionSpec as P

epsilon = 1e-06
negative_fill = -1e30
log2_e = math.log2(math.e)
resident_limit = 8 * 1024 * 1024


def unit_rows(values):
    widened = values.astype(jnp.float32)
    length = jnp.sqrt(jnp.sum(widened * widened, axis=-1, keepdims=True) + epsilon)
    return widened / length, length


def gather_columns(block):
    count = lax.axis_size("mp")
    chunks = [block]
    for k in range(1, count):
        chunks.append(lax.ppermute(block, "mp", [(i, i ^ k) for i in range(count)]))
    return jnp.concatenate(chunks, axis=-1)


def gather_orders(dp_count):
    bits = [1 << k for k in range(1, dp_count.bit_length() - 1)]
    return bits, bits[1:] + bits[:1]


def gather_blocks(block):
    dp_count = lax.axis_size("dp")
    even, odd = gather_orders(dp_count)
    held = block[None]
    for bit_even, bit_odd in zip(even, odd):
        route = [(i, i ^ (bit_odd if i & 1 else bit_even)) for i in range(dp_count)]
        held = jnp.concatenate([held, lax.ppermute(held, "dp", route)], axis=0)
    other = lax.ppermute(held, "dp", [(i, i ^ 1) for i in range(dp_count)])
    return jnp.concatenate([held, other], axis=0)


def block_offsets(dp_count):
    even, odd = gather_orders(dp_count)
    own = []
    for order in (even, odd):
        held = [0]
        for bit in order:
            held = held + [h ^ bit for h in held]
        own.append(held)
    return [own[0] + [h ^ 1 for h in own[1]], own[1] + [h ^ 1 for h in own[0]]]


def streamed_kernel(
    mp_ref,
    scale_ref,
    clips_ref,
    caps_ref,
    own_clips_ref,
    own_caps_ref,
    row_videos_ref,
    column_videos_ref,
    d_clips_ref,
    d_caps_ref,
    row_lse_ref,
    col_max_ref,
    col_sum_ref,
    *,
    mp_count,
):
    total = clips_ref.shape[0]
    own = own_clips_ref.shape[0]
    width = clips_ref.shape[1]
    row_tile = min(256, total)
    col_tile = min(1024, total)
    mp_index = mp_ref[0]
    scale = scale_ref[0]
    scale2 = scale * log2_e
    contract_last = (((1,), (1,)), ((), ()))

    col_max_ref[...] = jnp.full(col_max_ref.shape, negative_fill, jnp.float32)
    col_sum_ref[...] = jnp.zeros(col_sum_ref.shape, jnp.float32)

    def one_tile(row_first, col_first, carry):
        row_max, row_sum = carry
        rows = pl.ds(row_first, row_tile)
        cols = pl.ds(col_first, col_tile)
        scores = scale2 * lax.dot_general(
            clips_ref[rows, :], caps_ref[cols, :], contract_last, preferred_element_type=jnp.float32
        )
        same = column_videos_ref[rows, :] == row_videos_ref[:, cols]
        distance = lax.broadcasted_iota(jnp.int32, scores.shape, 0) - lax.broadcasted_iota(
            jnp.int32, scores.shape, 1
        )
        off_diagonal = distance != col_first - row_first
        scores = jnp.where(same & off_diagonal, negative_fill, scores)
        new_row = jnp.maximum(row_max, jnp.max(scores, axis=1, keepdims=True))
        row_sum = row_sum * jnp.exp2(row_max - new_row) + jnp.sum(
            jnp.exp2(scores - new_row), axis=1, keepdims=True
        )
        old_col = col_max_ref[:, cols]
        new_col = jnp.maximum(old_col, jnp.max(scores, axis=0, keepdims=True))
        col_sum_ref[:, cols] = col_sum_ref[:, cols] * jnp.exp2(old_col - new_col) + jnp.sum(
            jnp.exp2(scores - new_col), axis=0, keepdims=True
        )
        col_max_ref[:, cols] = new_col
        return new_row, row_sum

    def one_row_block(block):
        row_first = block * row_tile
        if not isinstance(block, int):
            row_first = pl.multiple_of(row_first, row_tile)
        carry = (
            jnp.full((row_tile, 1), negative_fill, jnp.float32),
            jnp.zeros((row_tile, 1), jnp.float32),
        )
        if total == col_tile:
            row_max, row_sum = one_tile(row_first, 0, carry)
        else:
            row_max, row_sum = lax.fori_loop(
                0,
                total // col_tile,
                lambda c, so_far: one_tile(row_first, pl.multiple_of(c * col_tile, col_tile), so_far),
                carry,
            )
        lse = row_max + jnp.log2(row_sum)
        row_lse_ref[:, pl.ds(row_first, row_tile)] = jnp.transpose(
            jnp.broadcast_to(lse, (row_tile, 128))
        )[:8, :]

    if total // row_tile <= 8:
        for block in range(total // row_tile):
            one_row_block(block)
    else:
        pl.loop(0, total // row_tile)(one_row_block)

    col_lse = col_max_ref[...] + jnp.log2(col_sum_ref[...])
    row_lse = row_lse_ref[0:1, :]

    own_first = pl.multiple_of(mp_index * own, own)
    own_rows = pl.ds(own_first, own)
    clip_unit = clips_ref[own_rows, :]
    cap_unit = caps_ref[own_rows, :]
    same = column_videos_ref[own_rows, :] == row_videos_ref[...]
    distance = lax.broadcasted_iota(jnp.int32, (own, total), 1) - lax.broadcasted_iota(
        jnp.int32, (own, total), 0
    )
    blocked = same & (distance != own_first)
    same = same.astype(jnp.bfloat16)

    def strip(unit, others_ref, own_lse_all, other_lse):
        scores = scale2 * lax.dot_general(
            unit, others_ref[...], contract_last, preferred_element_type=jnp.float32
        )
        scores = jnp.where(blocked, negative_fill, scores)
        top = jnp.max(scores, axis=1, keepdims=True)
        own_lse = top + jnp.log2(jnp.sum(jnp.exp2(scores - top), axis=1, keepdims=True))
        weights = 0.5 * (jnp.exp2(scores - own_lse) + jnp.exp2(scores - other_lse))
        weights = weights.astype(jnp.bfloat16)
        both = jnp.concatenate([weights, same], axis=0)
        sums = jnp.dot(both, others_ref[...], preferred_element_type=jnp.float32)
        return sums[:own], sums[own:]

    clip_acc, caption_pool = strip(clip_unit, caps_ref, None, col_lse)
    cap_acc, pooled = strip(cap_unit, clips_ref, None, row_lse)
    clip_unit = clip_unit.astype(jnp.float32)
    cap_unit = cap_unit.astype(jnp.float32)
    pool_length = jnp.sqrt(jnp.sum(pooled * pooled, axis=1, keepdims=True) + epsilon)
    pool_unit = pooled / pool_length
    projected = caption_pool - pool_unit * jnp.sum(pool_unit * caption_pool, axis=1, keepdims=True)
    clip_grad = scale * clip_acc - 0.5 * scale * cap_unit - 0.5 * scale * projected / pool_length
    cap_grad = scale * cap_acc - 0.5 * scale * clip_unit - 0.5 * scale * pool_unit

    def finish(values_ref, grad, out_ref):
        unit, length = unit_rows(values_ref[...])
        result = (grad - unit * jnp.sum(unit * grad, axis=1, keepdims=True)) / length
        chunk = width // mp_count
        for index in range(mp_count):

            @pl.when(mp_index == index)
            def _():
                out_ref[...] = jnp.concatenate(
                    [result[:, (q ^ index) * chunk : ((q ^ index) + 1) * chunk] for q in range(mp_count)],
                    axis=1,
                )

    finish(own_clips_ref, clip_grad, d_clips_ref)
    finish(own_caps_ref, cap_grad, d_caps_ref)


def streamed_body(clips, captions, video_id, logit_scale):
    dp_count = lax.axis_size("dp")
    mp_count = lax.axis_size("mp")
    row_count = clips.shape[0]
    own = row_count // mp_count
    width = clips.shape[1] * mp_count
    total = row_count * dp_count
    dp_index = lax.axis_index("dp")
    mp_index = lax.axis_index("mp")

    full = gather_columns(jnp.stack([clips, captions]))
    unit = unit_rows(full)[0].astype(jnp.bfloat16)
    own_raw = lax.dynamic_slice_in_dim(full, mp_index * own, own, 1)
    every = gather_blocks(unit)
    all_clips = every[:, 0].reshape(total, width)
    all_caps = every[:, 1].reshape(total, width)

    offsets = block_offsets(dp_count)
    videos = []
    for even, odd in zip(*offsets):
        block = dp_index ^ jnp.where(dp_index & 1, odd, even)
        videos.append(lax.dynamic_slice_in_dim(video_id, block * row_count, row_count, 0))
    videos = jnp.concatenate(videos)

    vmem = pl.BlockSpec(memory_space=pltpu.VMEM)
    smem = pl.BlockSpec(memory_space=pltpu.SMEM)
    out = jax.ShapeDtypeStruct((own, width), jnp.float32)
    return pl.pallas_call(
        functools.partial(streamed_kernel, mp_count=mp_count),
        out_shape=(out, out),
        in_specs=[smem, smem] + [vmem] * 6,
        out_specs=(vmem, vmem),
        scratch_shapes=[
            pltpu.VMEM((8, total), jnp.float32),
            pltpu.VMEM((1, total), jnp.float32),
            pltpu.VMEM((1, total), jnp.float32),
        ],
        compiler_params=pltpu.CompilerParams(vmem_limit_bytes=48 * 1024 * 1024),
    )(
        jnp.reshape(mp_index, (1,)).astype(jnp.int32),
        jnp.reshape(logit_scale, (1,)),
        all_clips,
        all_caps,
        own_raw[0],
        own_raw[1],
        videos[None, :],
        videos[:, None],
    )


def joined_lse(left, right):
    top = jnp.maximum(left, right)
    return top + jnp.log2(jnp.exp2(left - top) + jnp.exp2(right - top))


def lane_vector(column):
    return jnp.transpose(jnp.broadcast_to(column, (column.shape[0], 128)))[0:1, :]


def add_terms(stat, scores, axis):
    top = jnp.max(scores, axis=axis, keepdims=True)
    if stat is not None:
        top = jnp.maximum(stat[0], top)
    terms = jnp.sum(jnp.exp2(scores - top), axis=axis, keepdims=True)
    if stat is not None:
        terms = terms + stat[1] * jnp.exp2(stat[0] - top)
    return top, terms


def lse_of(stat):
    return stat[0] + jnp.log2(stat[1])


def stage_kernel(*refs, piece_count, places, old_count, mp_count, final):
    refs = list(refs)

    def take(count):
        taken = refs[:count]
        del refs[:count]
        return taken

    mp_ref, scale_ref, row_videos_ref, column_videos_ref = take(4)
    piece_refs = take(piece_count)
    old = [take(2) for _ in range(old_count)]
    if old_count:
        row_old_ref, col_old_ref, own_ref, own_caps_ref = take(4)
    if final:
        strip_refs = [take(2) for _ in range(old_count)]
        d_clips_ref, d_caps_ref = take(2)
    clips_ref, caps_ref = take(2)
    if not final:
        row_ref, col_ref = take(2)
    clip_strip_ref, cap_strip_ref = take(2)
    if not old_count:
        own_ref, own_caps_ref = take(2)
    if refs:
        (caps_rows_ref,) = take(1)
    fresh, width = clips_ref.shape
    rows = fresh // len(places)
    chunk = width // mp_count
    start = sum(clips.shape[0] for clips, _ in old)
    wide_old = old_count > 1 or start > fresh
    mp_index = mp_ref[0]
    scale = scale_ref[0]
    scale2 = scale * log2_e
    last = (((1,), (1,)), ((), ()))

    for position, place in enumerate(places):
        span = pl.ds(position * rows, rows)
        for kind in range(2):
            raw = [
                piece_refs[piece][kind, first * chunk : (first + count) * chunk, :]
                for piece, first, count in place
            ]
            raw = jnp.concatenate(raw, axis=0)
            wide = raw.astype(jnp.float32)
            inverse = 1.0 / jnp.sqrt(jnp.sum(wide * wide, axis=0, keepdims=True) + epsilon)
            unit = (wide * inverse).astype(jnp.bfloat16)
            if kind == 0:
                clips_ref[span, :] = jnp.transpose(unit)
            else:
                caps_ref[:, span] = unit
                if wide_old:
                    caps_rows_ref[span, :] = jnp.transpose(unit)
            if not old_count:
                own_ref[kind] = jnp.transpose(raw)
                if kind == 1:
                    own_caps_ref[...] = jnp.transpose(unit)

    def masked(products, row_first, col_first):
        size = products.shape
        banned = (
            column_videos_ref[row_first : row_first + size[0], :]
            == row_videos_ref[:, col_first : col_first + size[1]]
        )
        if col_first <= row_first < col_first + size[1]:
            distance = lax.broadcasted_iota(jnp.int32, size, 1) - lax.broadcasted_iota(jnp.int32, size, 0)
            banned = banned & (distance != row_first - col_first)
        return jnp.where(banned, negative_fill, scale2 * products)

    def plain(left, right):
        return jnp.dot(left, right, preferred_element_type=jnp.float32)

    def crossed(left, right):
        return lax.dot_general(left, right, last, preferred_element_type=jnp.float32)

    clip_old, cap_old, clip_new, cap_new = [], [], [], []
    clip_stat, cap_stat, cap_lanes = None, None, None
    if wide_old:
        at = 0
        for index, (clips, caps) in enumerate(old):
            scores = masked(crossed(caps_rows_ref[...], clips[...]), start, at)
            clip_old.append(lse_of(add_terms(None, scores, 0)))
            cap_stat = add_terms(cap_stat, scores, 1)
            if index == 0:
                clip_strip_ref[...] = jnp.transpose(scores)
            scores = masked(plain(clips_ref[...], caps[...]), start, at)
            cap_old.append(lse_of(add_terms(None, scores, 0)))
            clip_stat = add_terms(clip_stat, scores, 1)
            if index == 0:
                cap_strip_ref[...] = jnp.transpose(scores)
            at += clips.shape[0]
        cap_new.append(lane_vector(lse_of(cap_stat)))
    elif old:
        scores = masked(plain(old[0][0][...], caps_ref[...]), 0, start)
        clip_strip_ref[...] = scores
        clip_old.append(lane_vector(lse_of(add_terms(None, scores, 1))))
        cap_lanes = add_terms(None, scores, 0)
        scores = masked(crossed(own_caps_ref[...], clips_ref[...]), 0, start)
        cap_strip_ref[...] = scores
        cap_old.append(lane_vector(lse_of(add_terms(None, scores, 1))))
        clip_new.append(lse_of(add_terms(None, scores, 0)))
    scores = masked(plain(clips_ref[...], caps_ref[...]), start, start)
    clip_new.append(lane_vector(lse_of(add_terms(clip_stat, scores, 1))))
    cap_new.append(lse_of(add_terms(cap_lanes, scores, 0)))
    if not old:
        clip_strip_ref[...] = scores
        cap_strip_ref[...] = jnp.transpose(scores)

    def joined(old_ref, old_parts, new_parts):
        new = functools.reduce(joined_lse, new_parts)
        if not old:
            return new
        return jnp.concatenate([joined_lse(old_ref[...], jnp.concatenate(old_parts, axis=1)), new], axis=1)

    row_lse = joined(row_old_ref if old else None, clip_old, clip_new)
    col_lse = joined(col_old_ref if old else None, cap_old, cap_new)
    if not final:
        row_ref[...] = row_lse
        col_ref[...] = col_lse
        return

    own = d_clips_ref.shape[0]
    every = old + [(clips_ref, caps_ref)]
    own_first = pl.multiple_of(mp_index * own, own)
    own_rows = pl.ds(own_first, own)
    clip_float, clip_length = unit_rows(own_ref[0, own_rows, :])
    cap_float, cap_length = unit_rows(own_ref[1, own_rows, :])
    clip_unit = old[0][0][own_rows, :]
    cap_unit = cap_float.astype(jnp.bfloat16)
    same = (column_videos_ref[own_rows, :] == row_videos_ref[...]).astype(jnp.bfloat16)
    strip_refs = strip_refs + [(clip_strip_ref, cap_strip_ref)]

    def strip(kind, other_lse):
        scores = jnp.concatenate([pair[kind][own_rows, :] for pair in strip_refs], axis=1)
        own_lse = lse_of(add_terms(None, scores, 1))
        weights = 0.5 * (jnp.exp2(scores - own_lse) + jnp.exp2(scores - other_lse))
        return jnp.concatenate([weights.astype(jnp.bfloat16), same], axis=0)

    def summed(weights, multiply):
        at, result = 0, None
        for clips, caps in every:
            part = multiply(weights[:, at : at + clips.shape[0]], clips, caps)
            result = part if result is None else result + part
            at += clips.shape[0]
        return result[:own], result[own:]

    clip_acc, caption_pool = summed(strip(0, col_lse), lambda w, clips, caps: crossed(w, caps[...]))
    cap_acc, pooled = summed(strip(1, row_lse), lambda w, clips, caps: plain(w, clips[...]))
    pool_length = jnp.sqrt(jnp.sum(pooled * pooled, axis=1, keepdims=True) + epsilon)
    pool_unit = pooled / pool_length
    projected = caption_pool - pool_unit * jnp.sum(pool_unit * caption_pool, axis=1, keepdims=True)
    clip_grad = (
        scale * clip_acc
        - 0.5 * scale * cap_unit.astype(jnp.float32)
        - 0.5 * scale * projected / pool_length
    )
    cap_grad = scale * cap_acc - 0.5 * scale * clip_unit.astype(jnp.float32) - 0.5 * scale * pool_unit

    def finish(unit, length, grad, out_ref):
        result = (grad - unit * jnp.sum(unit * grad, axis=1, keepdims=True)) / length
        for index in range(mp_count):

            @pl.when(mp_index == index)
            def _():
                out_ref[...] = jnp.concatenate(
                    [result[:, (q ^ index) * chunk : ((q ^ index) + 1) * chunk] for q in range(mp_count)],
                    axis=1,
                )

    finish(clip_float, clip_length, clip_grad, d_clips_ref)
    finish(cap_float, cap_length, cap_grad, d_caps_ref)


def resident_body(clips, captions, video_id, logit_scale):
    dp_count = lax.axis_size("dp")
    mp_count = lax.axis_size("mp")
    row_count = clips.shape[0]
    own = row_count // mp_count
    width = clips.shape[1] * mp_count
    dp_index = lax.axis_index("dp")
    mp_index = lax.axis_index("mp")
    even, odd = gather_orders(dp_count)

    def along(step, block):
        route = [(i, i ^ (odd[step] if i & 1 else even[step])) for i in range(dp_count)]
        return lax.ppermute(block, "dp", route)

    def across(block):
        return lax.ppermute(block, "dp", [(i, i ^ 1) for i in range(dp_count)])

    reached = [(0, 0), (even[0], odd[0]), (even[1], odd[1]), (even[0] ^ even[1], odd[0] ^ odd[1])]
    crossed = [(b ^ 1, a ^ 1) for a, b in reached]
    ordered = [reached[0], crossed[0], reached[1], reached[2], crossed[1], crossed[2], reached[3], crossed[3]]
    videos = []
    for even_offset, odd_offset in ordered:
        block = dp_index ^ jnp.where(dp_index & 1, odd_offset, even_offset)
        videos.append(lax.dynamic_slice_in_dim(video_id, block * row_count, row_count, 0))
    videos = jnp.concatenate(videos)
    common = (
        jnp.reshape(mp_index, (1,)).astype(jnp.int32),
        jnp.reshape(logit_scale, (1,)),
        videos[None, :],
        videos[:, None],
    )
    vmem = pl.BlockSpec(memory_space=pltpu.VMEM)
    smem = pl.BlockSpec(memory_space=pltpu.SMEM)

    def stage(pieces, places, old, carried, final=False, cost=1):
        fresh = len(places) * row_count
        total = fresh + sum(clips.shape[0] for clips, _ in old)
        units = [((fresh, width), jnp.bfloat16), ((width, fresh), jnp.bfloat16)]
        strips = [((row_count, fresh), jnp.float32)] * 2
        scratch = [((fresh, width), jnp.bfloat16)] if len(old) > 1 or total > 2 * fresh else []
        if final:
            outs = [((own, width), jnp.float32)] * 2
            scratch = units + strips + scratch
        else:
            outs = units + [((1, total), jnp.float32)] * 2 + strips
            if not old:
                outs = outs + [((2, row_count, width), jnp.bfloat16), ((row_count, width), jnp.bfloat16)]
        scratch = [pltpu.VMEM(*entry) for entry in scratch]
        operands = [*common, *pieces, *[unit for pair in old for unit in pair], *carried]
        return pl.pallas_call(
            functools.partial(
                stage_kernel,
                piece_count=len(pieces),
                places=places,
                old_count=len(old),
                mp_count=mp_count,
                final=final,
            ),
            out_shape=[jax.ShapeDtypeStruct(*out) for out in outs],
            in_specs=[smem, smem] + [vmem] * (len(operands) - 2),
            out_specs=[vmem] * len(outs),
            scratch_shapes=scratch,
            cost_estimate=pl.CostEstimate(
                flops=cost, bytes_accessed=1, transcendentals=0
            ),
            compiler_params=pltpu.CompilerParams(vmem_limit_bytes=32 * 1024 * 1024),
        )(*operands)

    def after(value, other):
        return lax.optimization_barrier((value, other))[0]

    early = mp_count // 2
    late = mp_count - early

    chunk = jnp.stack([clips.T, captions.T])
    arrived = [
        lax.ppermute(chunk, "mp", [(i, i ^ k) for i in range(mp_count)]) for k in range(1, mp_count)
    ]
    lead = jnp.concatenate([chunk] + arrived[: early - 1], axis=1)
    lead_first = along(0, lead)
    lead_second = along(1, lead)
    lead_other = across(lead)
    arrived[-1] = after(arrived[-1], (lead_first, lead_second, lead_other))
    rest = jnp.concatenate(arrived[early - 1 :], axis=1)
    rest_first = along(0, rest)
    rest_other = across(rest)
    whole = [(0, 0, early), (1, 0, late)]
    clips_a, caps_a, row_a, col_a, *strips_a, own_raw, own_caps = stage([lead, rest], [whole], [], [], cost=10**8)
    rest_second = along(1, after(rest, row_a))
    third = along(1, jnp.concatenate([lead_first, rest_first], axis=1))

    pairs = [
        (lead_other, rest_other),
        (lead_first, rest_first),
        (lead_second, rest_second),
        (across(after(lead_first, lead_second)), across(rest_first)),
        (across(after(lead_second, rest_second)), across(rest_second)),
    ]
    clips_b, caps_b, row_b, col_b, *strips_b = stage(
        [piece for pair in pairs for piece in pair],
        [[(2 * k + piece, first, count) for piece, first, count in whole] for k in range(len(pairs))],
        [(clips_a, caps_a)],
        [row_a, col_a, own_raw, own_caps],
    )
    third_other = across(after(third, row_b))
    clips_c, caps_c, row_c, col_c, *strips_c = stage(
        [third],
        [[(0, 0, mp_count)]],
        [(clips_a, caps_a), (clips_b, caps_b)],
        [row_b, col_b, own_raw, own_caps],
    )
    return tuple(
        stage(
            [third_other],
            [[(0, 0, mp_count)]],
            [(clips_a, caps_a), (clips_b, caps_b), (clips_c, caps_c)],
            [row_c, col_c, own_raw, own_caps, *strips_a, *strips_b, *strips_c],
            final=True,
        )
    )


def body(clips, captions, video_id, logit_scale):
    dp_count, mp_count = lax.axis_size("dp"), lax.axis_size("mp")
    gathered_bytes = 2 * clips.size * clips.dtype.itemsize * dp_count * mp_count
    if len(gather_orders(dp_count)[0]) == 2 and gathered_bytes <= resident_limit:
        return resident_body(clips, captions, video_id, logit_scale)
    return streamed_body(clips, captions, video_id, logit_scale)


def solution(mesh):
    in_specs = (P("dp", "mp"), P("dp", "mp"), P(), P())
    out_specs = (P(("dp", "mp"), None), P(("dp", "mp"), None))
    return jax.shard_map(body, mesh=mesh, in_specs=in_specs, out_specs=out_specs, check_vma=False)
```

```python
import functools
import math

import jax
import jax.numpy as jnp
from jax import lax
from jax.experimental import pallas as pl
from jax.experimental.pallas import tpu as pltpu
from jax.sharding import PartitionSpec as P

epsilon = 1e-06
negative_fill = -1e30
log2_e = math.log2(math.e)
resident_limit = 8 * 1024 * 1024


def unit_rows(values):
    widened = values.astype(jnp.float32)
    length = jnp.sqrt(jnp.sum(widened * widened, axis=-1, keepdims=True) + epsilon)
    return widened / length, length


def gather_columns(block):
    count = lax.axis_size("mp")
    chunks = [block]
    for k in range(1, count):
        chunks.append(lax.ppermute(block, "mp", [(i, i ^ k) for i in range(count)]))
    return jnp.concatenate(chunks, axis=-1)


def gather_orders(dp_count):
    bits = [1 << k for k in range(1, dp_count.bit_length() - 1)]
    return bits, bits[1:] + bits[:1]


def gather_blocks(block):
    dp_count = lax.axis_size("dp")
    even, odd = gather_orders(dp_count)
    held = block[None]
    for bit_even, bit_odd in zip(even, odd):
        route = [(i, i ^ (bit_odd if i & 1 else bit_even)) for i in range(dp_count)]
        held = jnp.concatenate([held, lax.ppermute(held, "dp", route)], axis=0)
    other = lax.ppermute(held, "dp", [(i, i ^ 1) for i in range(dp_count)])
    return jnp.concatenate([held, other], axis=0)


def block_offsets(dp_count):
    even, odd = gather_orders(dp_count)
    own = []
    for order in (even, odd):
        held = [0]
        for bit in order:
            held = held + [h ^ bit for h in held]
        own.append(held)
    return [own[0] + [h ^ 1 for h in own[1]], own[1] + [h ^ 1 for h in own[0]]]


def streamed_kernel(
    mp_ref,
    scale_ref,
    clips_ref,
    caps_ref,
    own_clips_ref,
    own_caps_ref,
    row_videos_ref,
    column_videos_ref,
    d_clips_ref,
    d_caps_ref,
    row_lse_ref,
    col_max_ref,
    col_sum_ref,
    *,
    mp_count,
):
    total = clips_ref.shape[0]
    own = own_clips_ref.shape[0]
    width = clips_ref.shape[1]
    row_tile = min(256, total)
    col_tile = min(1024, total)
    mp_index = mp_ref[0]
    scale = scale_ref[0]
    scale2 = scale * log2_e
    contract_last = (((1,), (1,)), ((), ()))

    col_max_ref[...] = jnp.full(col_max_ref.shape, negative_fill, jnp.float32)
    col_sum_ref[...] = jnp.zeros(col_sum_ref.shape, jnp.float32)

    def one_tile(row_first, col_first, carry):
        row_max, row_sum = carry
        rows = pl.ds(row_first, row_tile)
        cols = pl.ds(col_first, col_tile)
        scores = scale2 * lax.dot_general(
            clips_ref[rows, :], caps_ref[cols, :], contract_last, preferred_element_type=jnp.float32
        )
        same = column_videos_ref[rows, :] == row_videos_ref[:, cols]
        distance = lax.broadcasted_iota(jnp.int32, scores.shape, 0) - lax.broadcasted_iota(
            jnp.int32, scores.shape, 1
        )
        off_diagonal = distance != col_first - row_first
        scores = jnp.where(same & off_diagonal, negative_fill, scores)
        new_row = jnp.maximum(row_max, jnp.max(scores, axis=1, keepdims=True))
        row_sum = row_sum * jnp.exp2(row_max - new_row) + jnp.sum(
            jnp.exp2(scores - new_row), axis=1, keepdims=True
        )
        old_col = col_max_ref[:, cols]
        new_col = jnp.maximum(old_col, jnp.max(scores, axis=0, keepdims=True))
        col_sum_ref[:, cols] = col_sum_ref[:, cols] * jnp.exp2(old_col - new_col) + jnp.sum(
            jnp.exp2(scores - new_col), axis=0, keepdims=True
        )
        col_max_ref[:, cols] = new_col
        return new_row, row_sum

    def one_row_block(block):
        row_first = block * row_tile
        if not isinstance(block, int):
            row_first = pl.multiple_of(row_first, row_tile)
        carry = (
            jnp.full((row_tile, 1), negative_fill, jnp.float32),
            jnp.zeros((row_tile, 1), jnp.float32),
        )
        if total == col_tile:
            row_max, row_sum = one_tile(row_first, 0, carry)
        else:
            row_max, row_sum = lax.fori_loop(
                0,
                total // col_tile,
                lambda c, so_far: one_tile(row_first, pl.multiple_of(c * col_tile, col_tile), so_far),
                carry,
            )
        lse = row_max + jnp.log2(row_sum)
        row_lse_ref[:, pl.ds(row_first, row_tile)] = jnp.transpose(
            jnp.broadcast_to(lse, (row_tile, 128))
        )[:8, :]

    if total // row_tile <= 8:
        for block in range(total // row_tile):
            one_row_block(block)
    else:
        pl.loop(0, total // row_tile)(one_row_block)

    col_lse = col_max_ref[...] + jnp.log2(col_sum_ref[...])
    row_lse = row_lse_ref[0:1, :]

    own_first = pl.multiple_of(mp_index * own, own)
    own_rows = pl.ds(own_first, own)
    clip_unit = clips_ref[own_rows, :]
    cap_unit = caps_ref[own_rows, :]
    same = column_videos_ref[own_rows, :] == row_videos_ref[...]
    distance = lax.broadcasted_iota(jnp.int32, (own, total), 1) - lax.broadcasted_iota(
        jnp.int32, (own, total), 0
    )
    blocked = same & (distance != own_first)
    same = same.astype(jnp.bfloat16)

    def strip(unit, others_ref, own_lse_all, other_lse):
        scores = scale2 * lax.dot_general(
            unit, others_ref[...], contract_last, preferred_element_type=jnp.float32
        )
        scores = jnp.where(blocked, negative_fill, scores)
        top = jnp.max(scores, axis=1, keepdims=True)
        own_lse = top + jnp.log2(jnp.sum(jnp.exp2(scores - top), axis=1, keepdims=True))
        weights = 0.5 * (jnp.exp2(scores - own_lse) + jnp.exp2(scores - other_lse))
        weights = weights.astype(jnp.bfloat16)
        both = jnp.concatenate([weights, same], axis=0)
        sums = jnp.dot(both, others_ref[...], preferred_element_type=jnp.float32)
        return sums[:own], sums[own:]

    clip_acc, caption_pool = strip(clip_unit, caps_ref, None, col_lse)
    cap_acc, pooled = strip(cap_unit, clips_ref, None, row_lse)
    clip_unit = clip_unit.astype(jnp.float32)
    cap_unit = cap_unit.astype(jnp.float32)
    pool_length = jnp.sqrt(jnp.sum(pooled * pooled, axis=1, keepdims=True) + epsilon)
    pool_unit = pooled / pool_length
    projected = caption_pool - pool_unit * jnp.sum(pool_unit * caption_pool, axis=1, keepdims=True)
    clip_grad = scale * clip_acc - 0.5 * scale * cap_unit - 0.5 * scale * projected / pool_length
    cap_grad = scale * cap_acc - 0.5 * scale * clip_unit - 0.5 * scale * pool_unit

    def finish(values_ref, grad, out_ref):
        unit, length = unit_rows(values_ref[...])
        result = (grad - unit * jnp.sum(unit * grad, axis=1, keepdims=True)) / length
        chunk = width // mp_count
        for index in range(mp_count):

            @pl.when(mp_index == index)
            def _():
                out_ref[...] = jnp.concatenate(
                    [result[:, (q ^ index) * chunk : ((q ^ index) + 1) * chunk] for q in range(mp_count)],
                    axis=1,
                )

    finish(own_clips_ref, clip_grad, d_clips_ref)
    finish(own_caps_ref, cap_grad, d_caps_ref)


def streamed_body(clips, captions, video_id, logit_scale):
    dp_count = lax.axis_size("dp")
    mp_count = lax.axis_size("mp")
    row_count = clips.shape[0]
    own = row_count // mp_count
    width = clips.shape[1] * mp_count
    total = row_count * dp_count
    dp_index = lax.axis_index("dp")
    mp_index = lax.axis_index("mp")

    full = gather_columns(jnp.stack([clips, captions]))
    unit = unit_rows(full)[0].astype(jnp.bfloat16)
    own_raw = lax.dynamic_slice_in_dim(full, mp_index * own, own, 1)
    every = gather_blocks(unit)
    all_clips = every[:, 0].reshape(total, width)
    all_caps = every[:, 1].reshape(total, width)

    offsets = block_offsets(dp_count)
    videos = []
    for even, odd in zip(*offsets):
        block = dp_index ^ jnp.where(dp_index & 1, odd, even)
        videos.append(lax.dynamic_slice_in_dim(video_id, block * row_count, row_count, 0))
    videos = jnp.concatenate(videos)

    vmem = pl.BlockSpec(memory_space=pltpu.VMEM)
    smem = pl.BlockSpec(memory_space=pltpu.SMEM)
    out = jax.ShapeDtypeStruct((own, width), jnp.float32)
    return pl.pallas_call(
        functools.partial(streamed_kernel, mp_count=mp_count),
        out_shape=(out, out),
        in_specs=[smem, smem] + [vmem] * 6,
        out_specs=(vmem, vmem),
        scratch_shapes=[
            pltpu.VMEM((8, total), jnp.float32),
            pltpu.VMEM((1, total), jnp.float32),
            pltpu.VMEM((1, total), jnp.float32),
        ],
        compiler_params=pltpu.CompilerParams(vmem_limit_bytes=48 * 1024 * 1024),
    )(
        jnp.reshape(mp_index, (1,)).astype(jnp.int32),
        jnp.reshape(logit_scale, (1,)),
        all_clips,
        all_caps,
        own_raw[0],
        own_raw[1],
        videos[None, :],
        videos[:, None],
    )


def joined_lse(left, right):
    top = jnp.maximum(left, right)
    return top + jnp.log2(jnp.exp2(left - top) + jnp.exp2(right - top))


def lane_vector(column):
    return jnp.transpose(jnp.broadcast_to(column, (column.shape[0], 128)))[0:1, :]


def add_terms(stat, scores, axis):
    top = jnp.max(scores, axis=axis, keepdims=True)
    if stat is not None:
        top = jnp.maximum(stat[0], top)
    terms = jnp.sum(jnp.exp2(scores - top), axis=axis, keepdims=True)
    if stat is not None:
        terms = terms + stat[1] * jnp.exp2(stat[0] - top)
    return top, terms


def lse_of(stat):
    return stat[0] + jnp.log2(stat[1])


def stage_kernel(*refs, piece_count, places, old_count, mp_count, final):
    refs = list(refs)

    def take(count):
        taken = refs[:count]
        del refs[:count]
        return taken

    mp_ref, scale_ref, row_videos_ref, column_videos_ref = take(4)
    piece_refs = take(piece_count)
    old = [take(2) for _ in range(old_count)]
    if old_count:
        row_old_ref, col_old_ref, own_ref, own_caps_ref = take(4)
    if final:
        strip_refs = [take(2) for _ in range(old_count)]
        d_clips_ref, d_caps_ref = take(2)
    clips_ref, caps_ref = take(2)
    if not final:
        row_ref, col_ref = take(2)
    clip_strip_ref, cap_strip_ref = take(2)
    if not old_count:
        own_ref, own_caps_ref = take(2)
    if refs:
        (caps_rows_ref,) = take(1)
    fresh, width = clips_ref.shape
    rows = fresh // len(places)
    chunk = width // mp_count
    start = sum(clips.shape[0] for clips, _ in old)
    wide_old = old_count > 1 or start > fresh
    mp_index = mp_ref[0]
    scale = scale_ref[0]
    scale2 = scale * log2_e
    last = (((1,), (1,)), ((), ()))

    for position, place in enumerate(places):
        span = pl.ds(position * rows, rows)
        for kind in range(2):
            raw = [
                piece_refs[piece][kind, first * chunk : (first + count) * chunk, :]
                for piece, first, count in place
            ]
            raw = jnp.concatenate(raw, axis=0)
            wide = raw.astype(jnp.float32)
            inverse = 1.0 / jnp.sqrt(jnp.sum(wide * wide, axis=0, keepdims=True) + epsilon)
            unit = (wide * inverse).astype(jnp.bfloat16)
            if kind == 0:
                clips_ref[span, :] = jnp.transpose(unit)
            else:
                caps_ref[:, span] = unit
                if wide_old:
                    caps_rows_ref[span, :] = jnp.transpose(unit)
            if not old_count:
                own_ref[kind] = jnp.transpose(raw)
                if kind == 1:
                    own_caps_ref[...] = jnp.transpose(unit)

    def masked(products, row_first, col_first):
        size = products.shape
        banned = (
            column_videos_ref[row_first : row_first + size[0], :]
            == row_videos_ref[:, col_first : col_first + size[1]]
        )
        if col_first <= row_first < col_first + size[1]:
            distance = lax.broadcasted_iota(jnp.int32, size, 1) - lax.broadcasted_iota(jnp.int32, size, 0)
            banned = banned & (distance != row_first - col_first)
        return jnp.where(banned, negative_fill, scale2 * products)

    def plain(left, right):
        return jnp.dot(left, right, preferred_element_type=jnp.float32)

    def crossed(left, right):
        return lax.dot_general(left, right, last, preferred_element_type=jnp.float32)

    clip_old, cap_old, clip_new, cap_new = [], [], [], []
    clip_stat, cap_stat, cap_lanes = None, None, None
    if wide_old:
        at = 0
        for index, (clips, caps) in enumerate(old):
            scores = masked(crossed(caps_rows_ref[...], clips[...]), start, at)
            clip_old.append(lse_of(add_terms(None, scores, 0)))
            cap_stat = add_terms(cap_stat, scores, 1)
            if index == 0:
                clip_strip_ref[...] = jnp.transpose(scores)
            scores = masked(plain(clips_ref[...], caps[...]), start, at)
            cap_old.append(lse_of(add_terms(None, scores, 0)))
            clip_stat = add_terms(clip_stat, scores, 1)
            if index == 0:
                cap_strip_ref[...] = jnp.transpose(scores)
            at += clips.shape[0]
        cap_new.append(lane_vector(lse_of(cap_stat)))
    elif old:
        scores = masked(plain(old[0][0][...], caps_ref[...]), 0, start)
        clip_strip_ref[...] = scores
        clip_old.append(lane_vector(lse_of(add_terms(None, scores, 1))))
        cap_lanes = add_terms(None, scores, 0)
        scores = masked(crossed(own_caps_ref[...], clips_ref[...]), 0, start)
        cap_strip_ref[...] = scores
        cap_old.append(lane_vector(lse_of(add_terms(None, scores, 1))))
        clip_new.append(lse_of(add_terms(None, scores, 0)))
    scores = masked(plain(clips_ref[...], caps_ref[...]), start, start)
    clip_new.append(lane_vector(lse_of(add_terms(clip_stat, scores, 1))))
    cap_new.append(lse_of(add_terms(cap_lanes, scores, 0)))
    if not old:
        clip_strip_ref[...] = scores
        cap_strip_ref[...] = jnp.transpose(scores)

    def joined(old_ref, old_parts, new_parts):
        new = functools.reduce(joined_lse, new_parts)
        if not old:
            return new
        return jnp.concatenate([joined_lse(old_ref[...], jnp.concatenate(old_parts, axis=1)), new], axis=1)

    row_lse = joined(row_old_ref if old else None, clip_old, clip_new)
    col_lse = joined(col_old_ref if old else None, cap_old, cap_new)
    if not final:
        row_ref[...] = row_lse
        col_ref[...] = col_lse
        return

    own = d_clips_ref.shape[0]
    every = old + [(clips_ref, caps_ref)]
    own_first = pl.multiple_of(mp_index * own, own)
    own_rows = pl.ds(own_first, own)
    clip_float, clip_length = unit_rows(own_ref[0, own_rows, :])
    cap_float, cap_length = unit_rows(own_ref[1, own_rows, :])
    clip_unit = old[0][0][own_rows, :]
    cap_unit = cap_float.astype(jnp.bfloat16)
    same = (column_videos_ref[own_rows, :] == row_videos_ref[...]).astype(jnp.bfloat16)
    strip_refs = strip_refs + [(clip_strip_ref, cap_strip_ref)]

    def strip(kind, other_lse):
        scores = jnp.concatenate([pair[kind][own_rows, :] for pair in strip_refs], axis=1)
        own_lse = lse_of(add_terms(None, scores, 1))
        weights = 0.5 * (jnp.exp2(scores - own_lse) + jnp.exp2(scores - other_lse))
        return jnp.concatenate([weights.astype(jnp.bfloat16), same], axis=0)

    def summed(weights, multiply):
        at, result = 0, None
        for clips, caps in every:
            part = multiply(weights[:, at : at + clips.shape[0]], clips, caps)
            result = part if result is None else result + part
            at += clips.shape[0]
        return result[:own], result[own:]

    clip_acc, caption_pool = summed(strip(0, col_lse), lambda w, clips, caps: crossed(w, caps[...]))
    cap_acc, pooled = summed(strip(1, row_lse), lambda w, clips, caps: plain(w, clips[...]))
    pool_length = jnp.sqrt(jnp.sum(pooled * pooled, axis=1, keepdims=True) + epsilon)
    pool_unit = pooled / pool_length
    projected = caption_pool - pool_unit * jnp.sum(pool_unit * caption_pool, axis=1, keepdims=True)
    clip_grad = (
        scale * clip_acc
        - 0.5 * scale * cap_unit.astype(jnp.float32)
        - (0.5 * scale / pool_length) * projected
    )
    cap_grad = scale * cap_acc - 0.5 * scale * clip_unit.astype(jnp.float32) - 0.5 * scale * pool_unit

    def finish(unit, length, grad):
        return (grad - unit * jnp.sum(unit * grad, axis=1, keepdims=True)) * (1.0 / length)

    results = [finish(clip_float, clip_length, clip_grad), finish(cap_float, cap_length, cap_grad)]
    for index in range(mp_count):

        @pl.when(mp_index == index)
        def _():
            for result, out_ref in zip(results, (d_clips_ref, d_caps_ref)):
                out_ref[...] = jnp.concatenate(
                    [result[:, (q ^ index) * chunk : ((q ^ index) + 1) * chunk] for q in range(mp_count)],
                    axis=1,
                )


def resident_body(clips, captions, video_id, logit_scale):
    dp_count = lax.axis_size("dp")
    mp_count = lax.axis_size("mp")
    row_count = clips.shape[0]
    own = row_count // mp_count
    width = clips.shape[1] * mp_count
    dp_index = lax.axis_index("dp")
    mp_index = lax.axis_index("mp")
    even, odd = gather_orders(dp_count)

    def along(step, block):
        route = [(i, i ^ (odd[step] if i & 1 else even[step])) for i in range(dp_count)]
        return lax.ppermute(block, "dp", route)

    def across(block):
        return lax.ppermute(block, "dp", [(i, i ^ 1) for i in range(dp_count)])

    reached = [(0, 0), (even[0], odd[0]), (even[1], odd[1]), (even[0] ^ even[1], odd[0] ^ odd[1])]
    crossed = [(b ^ 1, a ^ 1) for a, b in reached]
    ordered = [reached[0], crossed[0], reached[1], reached[2], crossed[1], crossed[2], reached[3], crossed[3]]
    videos = []
    for even_offset, odd_offset in ordered:
        block = dp_index ^ jnp.where(dp_index & 1, odd_offset, even_offset)
        videos.append(lax.dynamic_slice_in_dim(video_id, block * row_count, row_count, 0))
    videos = jnp.concatenate(videos)
    common = (
        jnp.reshape(mp_index, (1,)).astype(jnp.int32),
        jnp.reshape(logit_scale, (1,)),
        videos[None, :],
        videos[:, None],
    )
    vmem = pl.BlockSpec(memory_space=pltpu.VMEM)
    smem = pl.BlockSpec(memory_space=pltpu.SMEM)

    def stage(pieces, places, old, carried, final=False, cost=1):
        fresh = len(places) * row_count
        total = fresh + sum(clips.shape[0] for clips, _ in old)
        units = [((fresh, width), jnp.bfloat16), ((width, fresh), jnp.bfloat16)]
        strips = [((row_count, fresh), jnp.float32)] * 2
        scratch = [((fresh, width), jnp.bfloat16)] if len(old) > 1 or total > 2 * fresh else []
        if final:
            outs = [((own, width), jnp.float32)] * 2
            scratch = units + strips + scratch
        else:
            outs = units + [((1, total), jnp.float32)] * 2 + strips
            if not old:
                outs = outs + [((2, row_count, width), jnp.bfloat16), ((row_count, width), jnp.bfloat16)]
        scratch = [pltpu.VMEM(*entry) for entry in scratch]
        operands = [*common, *pieces, *[unit for pair in old for unit in pair], *carried]
        return pl.pallas_call(
            functools.partial(
                stage_kernel,
                piece_count=len(pieces),
                places=places,
                old_count=len(old),
                mp_count=mp_count,
                final=final,
            ),
            out_shape=[jax.ShapeDtypeStruct(*out) for out in outs],
            in_specs=[smem, smem] + [vmem] * (len(operands) - 2),
            out_specs=[vmem] * len(outs),
            scratch_shapes=scratch,
            cost_estimate=pl.CostEstimate(
                flops=cost, bytes_accessed=1, transcendentals=0
            ),
            compiler_params=pltpu.CompilerParams(vmem_limit_bytes=32 * 1024 * 1024),
        )(*operands)

    def after(value, other):
        return lax.optimization_barrier((value, other))[0]

    early = mp_count // 2
    late = mp_count - early

    chunk = jnp.stack([clips.T, captions.T])
    arrived = [
        lax.ppermute(chunk, "mp", [(i, i ^ k) for i in range(mp_count)]) for k in range(1, mp_count)
    ]
    lead = jnp.concatenate([chunk] + arrived[: early - 1], axis=1)
    lead_first = along(0, lead)
    lead_second = along(1, lead)
    lead_other = across(lead)
    arrived[-1] = after(arrived[-1], (lead_first, lead_second, lead_other, common[3]))
    rest = jnp.concatenate(arrived[early - 1 :], axis=1)
    rest_first = along(0, rest)
    rest_other = across(rest)
    whole = [(0, 0, early), (1, 0, late)]
    clips_a, caps_a, row_a, col_a, *strips_a, own_raw, own_caps = stage([lead, rest], [whole], [], [], cost=10**8)
    rest_second = along(1, after(rest, row_a))
    third = along(1, jnp.concatenate([lead_first, rest_first], axis=1))

    pairs = [
        (lead_other, rest_other),
        (lead_first, rest_first),
        (lead_second, rest_second),
        (across(after(lead_first, lead_second)), across(rest_first)),
        (across(after(lead_second, rest_second)), across(rest_second)),
    ]
    clips_b, caps_b, row_b, col_b, *strips_b = stage(
        [piece for pair in pairs for piece in pair],
        [[(2 * k + piece, first, count) for piece, first, count in whole] for k in range(len(pairs))],
        [(clips_a, caps_a)],
        [row_a, col_a, own_raw, own_caps],
    )
    third_other = across(after(third, row_b))
    clips_c, caps_c, row_c, col_c, *strips_c = stage(
        [third],
        [[(0, 0, mp_count)]],
        [(clips_a, caps_a), (clips_b, caps_b)],
        [row_b, col_b, own_raw, own_caps],
    )
    return tuple(
        stage(
            [third_other],
            [[(0, 0, mp_count)]],
            [(clips_a, caps_a), (clips_b, caps_b), (clips_c, caps_c)],
            [row_c, col_c, own_raw, own_caps, *strips_a, *strips_b, *strips_c],
            final=True,
        )
    )


def body(clips, captions, video_id, logit_scale):
    dp_count, mp_count = lax.axis_size("dp"), lax.axis_size("mp")
    gathered_bytes = 2 * clips.size * clips.dtype.itemsize * dp_count * mp_count
    if len(gather_orders(dp_count)[0]) == 2 and gathered_bytes <= resident_limit:
        return resident_body(clips, captions, video_id, logit_scale)
    return streamed_body(clips, captions, video_id, logit_scale)


def solution(mesh):
    in_specs = (P("dp", "mp"), P("dp", "mp"), P(), P())
    out_specs = (P(("dp", "mp"), None), P(("dp", "mp"), None))
    return jax.shard_map(body, mesh=mesh, in_specs=in_specs, out_specs=out_specs, check_vma=False)
```

```python
import functools
import math

import jax
import jax.numpy as jnp
from jax import lax
from jax.experimental import pallas as pl
from jax.experimental.pallas import tpu as pltpu
from jax.sharding import PartitionSpec as P

epsilon = 1e-06
negative_fill = -1e30
log2_e = math.log2(math.e)
resident_limit = 8 * 1024 * 1024


def unit_rows(values):
    widened = values.astype(jnp.float32)
    length = jnp.sqrt(jnp.sum(widened * widened, axis=-1, keepdims=True) + epsilon)
    return widened / length, length


def gather_columns(block):
    count = lax.axis_size("mp")
    chunks = [block]
    for k in range(1, count):
        chunks.append(lax.ppermute(block, "mp", [(i, i ^ k) for i in range(count)]))
    return jnp.concatenate(chunks, axis=-1)


def gather_orders(dp_count):
    bits = [1 << k for k in range(1, dp_count.bit_length() - 1)]
    return bits, bits[1:] + bits[:1]


def gather_blocks(block):
    dp_count = lax.axis_size("dp")
    even, odd = gather_orders(dp_count)
    held = block[None]
    for bit_even, bit_odd in zip(even, odd):
        route = [(i, i ^ (bit_odd if i & 1 else bit_even)) for i in range(dp_count)]
        held = jnp.concatenate([held, lax.ppermute(held, "dp", route)], axis=0)
    other = lax.ppermute(held, "dp", [(i, i ^ 1) for i in range(dp_count)])
    return jnp.concatenate([held, other], axis=0)


def block_offsets(dp_count):
    even, odd = gather_orders(dp_count)
    own = []
    for order in (even, odd):
        held = [0]
        for bit in order:
            held = held + [h ^ bit for h in held]
        own.append(held)
    return [own[0] + [h ^ 1 for h in own[1]], own[1] + [h ^ 1 for h in own[0]]]


def streamed_kernel(
    mp_ref,
    scale_ref,
    clips_ref,
    caps_ref,
    own_clips_ref,
    own_caps_ref,
    row_videos_ref,
    column_videos_ref,
    d_clips_ref,
    d_caps_ref,
    row_lse_ref,
    col_max_ref,
    col_sum_ref,
    *,
    mp_count,
):
    total = clips_ref.shape[0]
    own = own_clips_ref.shape[0]
    width = clips_ref.shape[1]
    row_tile = min(256, total)
    col_tile = min(1024, total)
    mp_index = mp_ref[0]
    scale = scale_ref[0]
    scale2 = scale * log2_e
    contract_last = (((1,), (1,)), ((), ()))

    col_max_ref[...] = jnp.full(col_max_ref.shape, negative_fill, jnp.float32)
    col_sum_ref[...] = jnp.zeros(col_sum_ref.shape, jnp.float32)

    def one_tile(row_first, col_first, carry):
        row_max, row_sum = carry
        rows = pl.ds(row_first, row_tile)
        cols = pl.ds(col_first, col_tile)
        scores = scale2 * lax.dot_general(
            clips_ref[rows, :], caps_ref[cols, :], contract_last, preferred_element_type=jnp.float32
        )
        same = column_videos_ref[rows, :] == row_videos_ref[:, cols]
        distance = lax.broadcasted_iota(jnp.int32, scores.shape, 0) - lax.broadcasted_iota(
            jnp.int32, scores.shape, 1
        )
        off_diagonal = distance != col_first - row_first
        scores = jnp.where(same & off_diagonal, negative_fill, scores)
        new_row = jnp.maximum(row_max, jnp.max(scores, axis=1, keepdims=True))
        row_sum = row_sum * jnp.exp2(row_max - new_row) + jnp.sum(
            jnp.exp2(scores - new_row), axis=1, keepdims=True
        )
        old_col = col_max_ref[:, cols]
        new_col = jnp.maximum(old_col, jnp.max(scores, axis=0, keepdims=True))
        col_sum_ref[:, cols] = col_sum_ref[:, cols] * jnp.exp2(old_col - new_col) + jnp.sum(
            jnp.exp2(scores - new_col), axis=0, keepdims=True
        )
        col_max_ref[:, cols] = new_col
        return new_row, row_sum

    def one_row_block(block):
        row_first = block * row_tile
        if not isinstance(block, int):
            row_first = pl.multiple_of(row_first, row_tile)
        carry = (
            jnp.full((row_tile, 1), negative_fill, jnp.float32),
            jnp.zeros((row_tile, 1), jnp.float32),
        )
        if total == col_tile:
            row_max, row_sum = one_tile(row_first, 0, carry)
        else:
            row_max, row_sum = lax.fori_loop(
                0,
                total // col_tile,
                lambda c, so_far: one_tile(row_first, pl.multiple_of(c * col_tile, col_tile), so_far),
                carry,
            )
        lse = row_max + jnp.log2(row_sum)
        row_lse_ref[:, pl.ds(row_first, row_tile)] = jnp.transpose(
            jnp.broadcast_to(lse, (row_tile, 128))
        )[:8, :]

    if total // row_tile <= 8:
        for block in range(total // row_tile):
            one_row_block(block)
    else:
        pl.loop(0, total // row_tile)(one_row_block)

    col_lse = col_max_ref[...] + jnp.log2(col_sum_ref[...])
    row_lse = row_lse_ref[0:1, :]

    own_first = pl.multiple_of(mp_index * own, own)
    own_rows = pl.ds(own_first, own)
    clip_unit = clips_ref[own_rows, :]
    cap_unit = caps_ref[own_rows, :]
    same = column_videos_ref[own_rows, :] == row_videos_ref[...]
    distance = lax.broadcasted_iota(jnp.int32, (own, total), 1) - lax.broadcasted_iota(
        jnp.int32, (own, total), 0
    )
    blocked = same & (distance != own_first)
    same = same.astype(jnp.bfloat16)

    def strip(unit, others_ref, own_lse_all, other_lse):
        scores = scale2 * lax.dot_general(
            unit, others_ref[...], contract_last, preferred_element_type=jnp.float32
        )
        scores = jnp.where(blocked, negative_fill, scores)
        top = jnp.max(scores, axis=1, keepdims=True)
        own_lse = top + jnp.log2(jnp.sum(jnp.exp2(scores - top), axis=1, keepdims=True))
        weights = 0.5 * (jnp.exp2(scores - own_lse) + jnp.exp2(scores - other_lse))
        weights = weights.astype(jnp.bfloat16)
        both = jnp.concatenate([weights, same], axis=0)
        sums = jnp.dot(both, others_ref[...], preferred_element_type=jnp.float32)
        return sums[:own], sums[own:]

    clip_acc, caption_pool = strip(clip_unit, caps_ref, None, col_lse)
    cap_acc, pooled = strip(cap_unit, clips_ref, None, row_lse)
    clip_unit = clip_unit.astype(jnp.float32)
    cap_unit = cap_unit.astype(jnp.float32)
    pool_length = jnp.sqrt(jnp.sum(pooled * pooled, axis=1, keepdims=True) + epsilon)
    pool_unit = pooled / pool_length
    projected = caption_pool - pool_unit * jnp.sum(pool_unit * caption_pool, axis=1, keepdims=True)
    clip_grad = scale * clip_acc - 0.5 * scale * cap_unit - 0.5 * scale * projected / pool_length
    cap_grad = scale * cap_acc - 0.5 * scale * clip_unit - 0.5 * scale * pool_unit

    def finish(values_ref, grad, out_ref):
        unit, length = unit_rows(values_ref[...])
        result = (grad - unit * jnp.sum(unit * grad, axis=1, keepdims=True)) / length
        chunk = width // mp_count
        for index in range(mp_count):

            @pl.when(mp_index == index)
            def _():
                out_ref[...] = jnp.concatenate(
                    [result[:, (q ^ index) * chunk : ((q ^ index) + 1) * chunk] for q in range(mp_count)],
                    axis=1,
                )

    finish(own_clips_ref, clip_grad, d_clips_ref)
    finish(own_caps_ref, cap_grad, d_caps_ref)


def streamed_body(clips, captions, video_id, logit_scale):
    dp_count = lax.axis_size("dp")
    mp_count = lax.axis_size("mp")
    row_count = clips.shape[0]
    own = row_count // mp_count
    width = clips.shape[1] * mp_count
    total = row_count * dp_count
    dp_index = lax.axis_index("dp")
    mp_index = lax.axis_index("mp")

    full = gather_columns(jnp.stack([clips, captions]))
    unit = unit_rows(full)[0].astype(jnp.bfloat16)
    own_raw = lax.dynamic_slice_in_dim(full, mp_index * own, own, 1)
    every = gather_blocks(unit)
    all_clips = every[:, 0].reshape(total, width)
    all_caps = every[:, 1].reshape(total, width)

    offsets = block_offsets(dp_count)
    videos = []
    for even, odd in zip(*offsets):
        block = dp_index ^ jnp.where(dp_index & 1, odd, even)
        videos.append(lax.dynamic_slice_in_dim(video_id, block * row_count, row_count, 0))
    videos = jnp.concatenate(videos)

    vmem = pl.BlockSpec(memory_space=pltpu.VMEM)
    smem = pl.BlockSpec(memory_space=pltpu.SMEM)
    out = jax.ShapeDtypeStruct((own, width), jnp.float32)
    return pl.pallas_call(
        functools.partial(streamed_kernel, mp_count=mp_count),
        out_shape=(out, out),
        in_specs=[smem, smem] + [vmem] * 6,
        out_specs=(vmem, vmem),
        scratch_shapes=[
            pltpu.VMEM((8, total), jnp.float32),
            pltpu.VMEM((1, total), jnp.float32),
            pltpu.VMEM((1, total), jnp.float32),
        ],
        compiler_params=pltpu.CompilerParams(vmem_limit_bytes=48 * 1024 * 1024),
    )(
        jnp.reshape(mp_index, (1,)).astype(jnp.int32),
        jnp.reshape(logit_scale, (1,)),
        all_clips,
        all_caps,
        own_raw[0],
        own_raw[1],
        videos[None, :],
        videos[:, None],
    )


def joined_lse(left, right):
    top = jnp.maximum(left, right)
    return top + jnp.log2(jnp.exp2(left - top) + jnp.exp2(right - top))


def lane_vector(column):
    return jnp.transpose(jnp.broadcast_to(column, (column.shape[0], 128)))[0:1, :]


def add_terms(stat, scores, axis):
    top = jnp.max(scores, axis=axis, keepdims=True)
    if stat is not None:
        top = jnp.maximum(stat[0], top)
    terms = jnp.sum(jnp.exp2(scores - top), axis=axis, keepdims=True)
    if stat is not None:
        terms = terms + stat[1] * jnp.exp2(stat[0] - top)
    return top, terms


def lse_of(stat):
    return stat[0] + jnp.log2(stat[1])


def stage_kernel(*refs, piece_count, places, old_count, mp_count, final):
    refs = list(refs)

    def take(count):
        taken = refs[:count]
        del refs[:count]
        return taken

    mp_ref, scale_ref, row_videos_ref, column_videos_ref = take(4)
    piece_refs = take(piece_count)
    old = [take(2) for _ in range(old_count)]
    if old_count:
        row_old_ref, col_old_ref, own_ref, own_caps_ref = take(4)
    if final:
        strip_refs = [take(2) for _ in range(old_count)]
        d_clips_ref, d_caps_ref = take(2)
    clips_ref, caps_ref = take(2)
    if not final:
        row_ref, col_ref = take(2)
    clip_strip_ref, cap_strip_ref = take(2)
    if not old_count:
        own_ref, own_caps_ref = take(2)
    if refs:
        (caps_rows_ref,) = take(1)
    fresh, width = clips_ref.shape
    rows = fresh // len(places)
    chunk = width // mp_count
    start = sum(clips.shape[0] for clips, _ in old)
    wide_old = old_count > 1 or start > fresh
    mp_index = mp_ref[0]
    scale = scale_ref[0]
    scale2 = scale * log2_e
    last = (((1,), (1,)), ((), ()))

    for position, place in enumerate(places):
        span = pl.ds(position * rows, rows)
        for kind in range(2):
            raw = [
                piece_refs[piece][kind, first * chunk : (first + count) * chunk, :]
                for piece, first, count in place
            ]
            raw = jnp.concatenate(raw, axis=0)
            wide = raw.astype(jnp.float32)
            inverse = 1.0 / jnp.sqrt(jnp.sum(wide * wide, axis=0, keepdims=True) + epsilon)
            unit = (wide * inverse).astype(jnp.bfloat16)
            if kind == 0:
                clips_ref[span, :] = jnp.transpose(unit)
            else:
                caps_ref[:, span] = unit
                if wide_old:
                    caps_rows_ref[span, :] = jnp.transpose(unit)
            if not old_count:
                own_ref[kind] = jnp.transpose(raw)
                if kind == 1:
                    own_caps_ref[...] = jnp.transpose(unit)

    def masked(products, row_first, col_first):
        size = products.shape
        banned = (
            column_videos_ref[row_first : row_first + size[0], :]
            == row_videos_ref[:, col_first : col_first + size[1]]
        )
        if col_first <= row_first < col_first + size[1]:
            distance = lax.broadcasted_iota(jnp.int32, size, 1) - lax.broadcasted_iota(jnp.int32, size, 0)
            banned = banned & (distance != row_first - col_first)
        return jnp.where(banned, negative_fill, scale2 * products)

    def plain(left, right):
        return jnp.dot(left, right, preferred_element_type=jnp.float32)

    def crossed(left, right):
        return lax.dot_general(left, right, last, preferred_element_type=jnp.float32)

    clip_old, cap_old, clip_new, cap_new = [], [], [], []
    clip_stat, cap_stat, cap_lanes = None, None, None
    if wide_old:
        at = 0
        for index, (clips, caps) in enumerate(old):
            scores = masked(crossed(caps_rows_ref[...], clips[...]), start, at)
            clip_old.append(lse_of(add_terms(None, scores, 0)))
            cap_stat = add_terms(cap_stat, scores, 1)
            if index == 0:
                clip_strip_ref[...] = jnp.transpose(scores)
            scores = masked(plain(clips_ref[...], caps[...]), start, at)
            cap_old.append(lse_of(add_terms(None, scores, 0)))
            clip_stat = add_terms(clip_stat, scores, 1)
            if index == 0:
                cap_strip_ref[...] = jnp.transpose(scores)
            at += clips.shape[0]
        cap_new.append(lane_vector(lse_of(cap_stat)))
    elif old:
        scores = masked(plain(old[0][0][...], caps_ref[...]), 0, start)
        clip_strip_ref[...] = scores
        clip_old.append(lane_vector(lse_of(add_terms(None, scores, 1))))
        cap_lanes = add_terms(None, scores, 0)
        scores = masked(crossed(own_caps_ref[...], clips_ref[...]), 0, start)
        cap_strip_ref[...] = scores
        cap_old.append(lane_vector(lse_of(add_terms(None, scores, 1))))
        clip_new.append(lse_of(add_terms(None, scores, 0)))
    scores = masked(plain(clips_ref[...], caps_ref[...]), start, start)
    clip_new.append(lane_vector(lse_of(add_terms(clip_stat, scores, 1))))
    cap_new.append(lse_of(add_terms(cap_lanes, scores, 0)))
    if not old:
        clip_strip_ref[...] = scores
        cap_strip_ref[...] = jnp.transpose(scores)

    def joined(old_ref, old_parts, new_parts):
        new = functools.reduce(joined_lse, new_parts)
        if not old:
            return new
        return jnp.concatenate([joined_lse(old_ref[...], jnp.concatenate(old_parts, axis=1)), new], axis=1)

    row_lse = joined(row_old_ref if old else None, clip_old, clip_new)
    col_lse = joined(col_old_ref if old else None, cap_old, cap_new)
    if not final:
        row_ref[...] = row_lse
        col_ref[...] = col_lse
        return

    own = d_clips_ref.shape[0]
    every = old + [(clips_ref, caps_ref)]
    own_first = pl.multiple_of(mp_index * own, own)
    own_rows = pl.ds(own_first, own)
    clip_float, clip_length = unit_rows(own_ref[0, own_rows, :])
    cap_float, cap_length = unit_rows(own_ref[1, own_rows, :])
    clip_unit = old[0][0][own_rows, :]
    cap_unit = cap_float.astype(jnp.bfloat16)
    same = (column_videos_ref[own_rows, :] == row_videos_ref[...]).astype(jnp.bfloat16)
    strip_refs = strip_refs + [(clip_strip_ref, cap_strip_ref)]

    def strip(kind, other_lse):
        scores = jnp.concatenate([pair[kind][own_rows, :] for pair in strip_refs], axis=1)
        own_lse = lse_of(add_terms(None, scores, 1))
        weights = 0.5 * (jnp.exp2(scores - own_lse) + jnp.exp2(scores - other_lse))
        return jnp.concatenate([weights.astype(jnp.bfloat16), same], axis=0)

    def summed(weights, multiply):
        at, result = 0, None
        for clips, caps in every:
            part = multiply(weights[:, at : at + clips.shape[0]], clips, caps)
            result = part if result is None else result + part
            at += clips.shape[0]
        return result[:own], result[own:]

    clip_acc, caption_pool = summed(strip(0, col_lse), lambda w, clips, caps: crossed(w, caps[...]))
    cap_acc, pooled = summed(strip(1, row_lse), lambda w, clips, caps: plain(w, clips[...]))
    pool_length = jnp.sqrt(jnp.sum(pooled * pooled, axis=1, keepdims=True) + epsilon)
    pool_unit = pooled / pool_length
    projected = caption_pool - pool_unit * jnp.sum(pool_unit * caption_pool, axis=1, keepdims=True)
    clip_grad = (
        scale * clip_acc
        - 0.5 * scale * cap_unit.astype(jnp.float32)
        - (0.5 * scale / pool_length) * projected
    )
    cap_grad = scale * cap_acc - 0.5 * scale * clip_unit.astype(jnp.float32) - 0.5 * scale * pool_unit

    def finish(unit, length, grad):
        return (grad - unit * jnp.sum(unit * grad, axis=1, keepdims=True)) * (1.0 / length)

    results = [finish(clip_float, clip_length, clip_grad), finish(cap_float, cap_length, cap_grad)]
    for index in range(mp_count):

        @pl.when(mp_index == index)
        def _():
            for result, out_ref in zip(results, (d_clips_ref, d_caps_ref)):
                out_ref[...] = jnp.concatenate(
                    [result[:, (q ^ index) * chunk : ((q ^ index) + 1) * chunk] for q in range(mp_count)],
                    axis=1,
                )


def resident_body(clips, captions, video_id, logit_scale):
    dp_count = lax.axis_size("dp")
    mp_count = lax.axis_size("mp")
    row_count = clips.shape[0]
    own = row_count // mp_count
    width = clips.shape[1] * mp_count
    dp_index = lax.axis_index("dp")
    mp_index = lax.axis_index("mp")
    even, odd = gather_orders(dp_count)

    def along(step, block):
        route = [(i, i ^ (odd[step] if i & 1 else even[step])) for i in range(dp_count)]
        return lax.ppermute(block, "dp", route)

    def across(block):
        return lax.ppermute(block, "dp", [(i, i ^ 1) for i in range(dp_count)])

    reached = [(0, 0), (even[0], odd[0]), (even[1], odd[1]), (even[0] ^ even[1], odd[0] ^ odd[1])]
    crossed = [(b ^ 1, a ^ 1) for a, b in reached]
    ordered = [reached[0], crossed[0], reached[1], reached[2], crossed[1], crossed[2], reached[3], crossed[3]]
    videos = []
    for even_offset, odd_offset in ordered:
        block = dp_index ^ jnp.where(dp_index & 1, odd_offset, even_offset)
        videos.append(lax.dynamic_slice_in_dim(video_id, block * row_count, row_count, 0))
    videos = jnp.concatenate(videos)
    common = (
        jnp.reshape(mp_index, (1,)).astype(jnp.int32),
        jnp.reshape(logit_scale, (1,)),
        videos[None, :],
        videos[:, None],
    )
    vmem = pl.BlockSpec(memory_space=pltpu.VMEM)
    smem = pl.BlockSpec(memory_space=pltpu.SMEM)

    def stage(pieces, places, old, carried, final=False, cost=1):
        fresh = len(places) * row_count
        total = fresh + sum(clips.shape[0] for clips, _ in old)
        units = [((fresh, width), jnp.bfloat16), ((width, fresh), jnp.bfloat16)]
        strips = [((row_count, fresh), jnp.float32)] * 2
        scratch = [((fresh, width), jnp.bfloat16)] if len(old) > 1 or total > 2 * fresh else []
        if final:
            outs = [((own, width), jnp.float32)] * 2
            scratch = units + strips + scratch
        else:
            outs = units + [((1, total), jnp.float32)] * 2 + strips
            if not old:
                outs = outs + [((2, row_count, width), jnp.bfloat16), ((row_count, width), jnp.bfloat16)]
        scratch = [pltpu.VMEM(*entry) for entry in scratch]
        operands = [*common, *pieces, *[unit for pair in old for unit in pair], *carried]
        return pl.pallas_call(
            functools.partial(
                stage_kernel,
                piece_count=len(pieces),
                places=places,
                old_count=len(old),
                mp_count=mp_count,
                final=final,
            ),
            out_shape=[jax.ShapeDtypeStruct(*out) for out in outs],
            in_specs=[smem, smem] + [vmem] * (len(operands) - 2),
            out_specs=[vmem] * len(outs),
            scratch_shapes=scratch,
            cost_estimate=pl.CostEstimate(
                flops=cost, bytes_accessed=1, transcendentals=0
            ),
            compiler_params=pltpu.CompilerParams(vmem_limit_bytes=32 * 1024 * 1024),
        )(*operands)

    def after(value, other):
        return lax.optimization_barrier((value, other))[0]

    early = mp_count // 2
    late = mp_count - early

    chunk = jnp.stack([clips.T, captions.T])
    arrived = [
        lax.ppermute(chunk, "mp", [(i, i ^ k) for i in range(mp_count)]) for k in range(1, mp_count)
    ]
    lead = jnp.concatenate([chunk] + arrived[: early - 1], axis=1)
    lead_first = along(0, lead)
    lead_second = along(1, lead)
    lead_other = across(lead)
    arrived[-1] = after(arrived[-1], (lead_first, lead_second, lead_other, common[3]))
    rest = jnp.concatenate(arrived[early - 1 :], axis=1)
    rest_first = along(0, rest)
    rest_other = across(rest)
    whole = [(0, 0, early), (1, 0, late)]
    clips_a, caps_a, row_a, col_a, *strips_a, own_raw, own_caps = stage([lead, rest], [whole], [], [], cost=10**8)
    rest_second = along(1, after(rest, row_a))
    third = along(1, jnp.concatenate([lead_first, rest_first], axis=1))

    pairs = [
        (lead_other, rest_other),
        (lead_first, rest_first),
        (lead_second, rest_second),
        (across(lead_first), across(rest_first)),
        (across(after(lead_second, rest_second)), across(rest_second)),
    ]
    clips_b, caps_b, row_b, col_b, *strips_b = stage(
        [piece for pair in pairs for piece in pair],
        [[(2 * k + piece, first, count) for piece, first, count in whole] for k in range(len(pairs))],
        [(clips_a, caps_a)],
        [row_a, col_a, own_raw, own_caps],
    )
    third_other = across(after(third, row_b))
    clips_c, caps_c, row_c, col_c, *strips_c = stage(
        [third],
        [[(0, 0, mp_count)]],
        [(clips_a, caps_a), (clips_b, caps_b)],
        [row_b, col_b, own_raw, own_caps],
    )
    return tuple(
        stage(
            [third_other],
            [[(0, 0, mp_count)]],
            [(clips_a, caps_a), (clips_b, caps_b), (clips_c, caps_c)],
            [row_c, col_c, own_raw, own_caps, *strips_a, *strips_b, *strips_c],
            final=True,
        )
    )


def body(clips, captions, video_id, logit_scale):
    dp_count, mp_count = lax.axis_size("dp"), lax.axis_size("mp")
    gathered_bytes = 2 * clips.size * clips.dtype.itemsize * dp_count * mp_count
    if len(gather_orders(dp_count)[0]) == 2 and gathered_bytes <= resident_limit:
        return resident_body(clips, captions, video_id, logit_scale)
    return streamed_body(clips, captions, video_id, logit_scale)


def solution(mesh):
    in_specs = (P("dp", "mp"), P("dp", "mp"), P(), P())
    out_specs = (P(("dp", "mp"), None), P(("dp", "mp"), None))
    return jax.shard_map(body, mesh=mesh, in_specs=in_specs, out_specs=out_specs, check_vma=False)
```
